32 devices in a mesh: dp: 16 (over z, y, x), mp: 2 (over core).
Axes of the slice: x: 2, y: 2, z: 4, core: 2. Of those that a mesh axis runs over, the one named last changes fastest.
Arguments:
- tokens_in: bfloat16 [4096, 1024], P('dp'), may hold values from -6 to 6
- out_cotangent: bfloat16 [4096, 1024], P('dp'), may hold values from -6 to 6
- utt_lengths: int32 [16, 2], P('dp'), may hold values from 0 to 256, as said below
- feed_in: float32 [2, 1024, 4096], P(None, 'dp', 'mp'), may hold values from -0.1875 to 0.1875
- feed_in_mean: float32 [2, 1024, 4096], P(None, 'dp', 'mp')
- feed_in_square: float32 [2, 1024, 4096], P(None, 'dp', 'mp')
- feed_out: float32 [2, 4096, 1024], P(None, 'mp', 'dp'), may hold values from -0.09375 to 0.09375
- feed_out_mean: float32 [2, 4096, 1024], P(None, 'mp', 'dp')
- feed_out_square: float32 [2, 4096, 1024], P(None, 'mp', 'dp')
- mixer_in: float32 [5, 1024, 1024], P(None, 'dp', 'mp'), may hold values from -0.1875 to 0.1875
- mixer_in_mean: float32 [5, 1024, 1024], P(None, 'dp', 'mp')
- mixer_in_square: float32 [5, 1024, 1024], P(None, 'dp', 'mp')
- mixer_out: float32 [2, 1024, 1024], P(None, 'mp', 'dp')
- mixer_out_mean: float32 [2, 1024, 1024], P(None, 'mp', 'dp')
- mixer_out_square: float32 [2, 1024, 1024], P(None, 'mp', 'dp')
- norm_vectors: float32 [10, 1024], replicated
- norm_vectors_mean: float32 [10, 1024], replicated
- norm_vectors_square: float32 [10, 1024], replicated
- channel_vectors: float32 [7, 1024], P(None, 'mp')
- channel_vectors_mean: float32 [7, 1024], P(None, 'mp')
- channel_vectors_square: float32 [7, 1024], P(None, 'mp')
Outputs:
- tokens_out: float32 [4096, 1024], P('dp')
- tokens_grad: float32 [4096, 1024], P('dp')
- feed_in_next: float32 [2, 1024, 4096], P(None, 'dp', 'mp')
- feed_in_mean_next: float32 [2, 1024, 4096], P(None, 'dp', 'mp')
- feed_in_square_next: float32 [2, 1024, 4096], P(None, 'dp', 'mp')
- feed_out_next: float32 [2, 4096, 1024], P(None, 'mp', 'dp')
- feed_out_mean_next: float32 [2, 4096, 1024], P(None, 'mp', 'dp')
- feed_out_square_next: float32 [2, 4096, 1024], P(None, 'mp', 'dp')
- mixer_in_next: float32 [5, 1024, 1024], P(None, 'dp', 'mp')
- mixer_in_mean_next: float32 [5, 1024, 1024], P(None, 'dp', 'mp')
- mixer_in_square_next: float32 [4, 1024, 1024], P(None, 'dp', 'mp')
- conv_gate_square_next: float32 [1024, 1024], P('dp', 'mp')
- mixer_out_next: float32 [2, 1024, 1024], P(None, 'mp', 'dp')
- mixer_out_mean_next: float32 [2, 1024, 1024], P(None, 'mp', 'dp')
- mixer_out_square_next: float32 [2, 1024, 1024], P(None, 'mp', 'dp')
- norm_vectors_next: float32 [10, 1024], replicated
- norm_vectors_mean_next: float32 [10, 1024], replicated
- norm_vectors_square_next: float32 [10, 1024], replicated
- channel_vectors_next: float32 [7, 1024], P(None, 'mp')
- channel_vectors_mean_next: float32 [7, 1024], P(None, 'mp')
- channel_vectors_square_next: float32 [7, 1024], P(None, 'mp')
The draws below stay inside these ranges and needn't reach their ends.
Inputs may be any that keep to these rules, and one draw needn't show every extreme that they name: `utt_lengths`: row b holds the lengths of the first and second utterance packed at the start of block b; their sum is at most 256, and the rest of the block is padding. Some block holds a single utterance of 256 frames.
All inputs are finite; a program needn't handle non-finite values.
Results may differ from the reference program's by a relative error of at most 0.025.
Values may be sent and summed in bfloat16 or wider, within the bound.
A program may use at most 192 MiB of HBM per device.

```python
import math
from functools import partial
import jax
import jax.numpy as jnp
from jax import lax

D = 1024
FF = 4096
HEADS = 8
HEAD_DIM = 128
KERNEL = 5
STEP_COUNT = 3
TOK_DEV = 256
TOKENS = 4096
N_DP = 16


def draw_utt_lengths(key, part):
    key_group = jax.random.fold_in(key, 11)
    key_first = jax.random.fold_in(key, 12)
    key_second = jax.random.fold_in(key, 13)
    key_full = jax.random.fold_in(key, 14)
    groups = jax.random.randint(key_group, (N_DP,), 0, 4)
    ceiling = TOK_DEV * (groups + 1) // 4
    first_len = jax.random.randint(key_first, (N_DP,), ceiling // 2, ceiling + 1)
    second = jax.random.randint(key_second, (N_DP,), 0, ceiling - first_len + 1)
    chosen = jax.random.randint(key_full, (), 0, N_DP)
    full_block = jnp.arange(N_DP) == chosen
    first_len = jnp.where(full_block, TOK_DEV, first_len)
    second = jnp.where(full_block, 0, second)
    return jnp.stack([first_len, second], axis=1).astype(jnp.int32)


def clipped_normal(key, salt_value, array_shape):
    return jnp.clip(jax.random.normal(jax.random.fold_in(key, salt_value), array_shape, jnp.float32), -4.0, 4.0)


def spread_draw(key, salt_value, array_shape):
    return clipped_normal(key, salt_value, array_shape)


def gain_draw(key, salt_value, array_shape):
    return jnp.exp(jax.random.uniform(jax.random.fold_in(key, salt_value), array_shape, jnp.float32, -0.4, 0.4))


def draw_mixer_out(key, part):
    attention_fan = max(2 * D // TOK_DEV, 1)
    scales = jnp.array([attention_fan ** (-0.5), D ** (-0.5)], jnp.float32)[:, None, None]
    return (scales * spread_draw(key, 21, (2, D, D))).astype(jnp.float32)


def draw_norm_vectors(key, part):
    gain_rows = gain_draw(key, 31, (5, D))
    shifts = 0.3 * spread_draw(key, 32, (5, D))
    return jnp.concatenate([gain_rows, shifts], axis=0).astype(jnp.float32)


def draw_channel_vectors(key, part):
    taps = 0.3 * spread_draw(key, 41, (KERNEL, D))
    gain_rows = gain_draw(key, 42, (1, D))
    shifts = 0.3 * spread_draw(key, 43, (1, D))
    return jnp.concatenate([taps, gain_rows, shifts], axis=0).astype(jnp.float32)


def gradient_size():
    return (TOK_DEV * N_DP) ** 0.5


def moment_draw(key, salt_value, array_shape, scales, squared):
    if squared:
        factor = jnp.exp(jax.random.uniform(jax.random.fold_in(key, salt_value), array_shape, jnp.float32, 0.0, math.log(4.0)))
        return (scales * scales * factor).astype(jnp.float32)
    return (scales * clipped_normal(key, salt_value, array_shape)).astype(jnp.float32)


def feed_in_scale():
    return 0.3 * (D / FF) ** 0.5 * gradient_size()


def feed_out_scale():
    return 0.3 * gradient_size()


def mixer_in_scale():
    return jnp.array([1.0, 1.0, 1.0, 0.6, 0.2], jnp.float32)[:, None, None] * gradient_size()


def mixer_out_scale():
    return jnp.array([(2.0 / TOK_DEV) ** 0.5, 0.2], jnp.float32)[:, None, None] * gradient_size()


def draw_feed_in_mean(key, part):
    return moment_draw(key, 51, (2, D, FF), feed_in_scale(), False)


def draw_feed_in_square(key, part):
    return moment_draw(key, 52, (2, D, FF), feed_in_scale(), True)


def draw_feed_out_mean(key, part):
    return moment_draw(key, 53, (2, FF, D), feed_out_scale(), False)


def draw_feed_out_square(key, part):
    return moment_draw(key, 54, (2, FF, D), feed_out_scale(), True)


def draw_mixer_in_mean(key, part):
    return moment_draw(key, 55, (5, D, D), mixer_in_scale(), False)


def draw_mixer_in_square(key, part):
    return moment_draw(key, 56, (5, D, D), mixer_in_scale(), True)


def draw_mixer_out_mean(key, part):
    return moment_draw(key, 57, (2, D, D), mixer_out_scale(), False)


def draw_mixer_out_square(key, part):
    return moment_draw(key, 58, (2, D, D), mixer_out_scale(), True)


def draw_norm_vectors_mean(key, part):
    return moment_draw(key, 59, (10, D), 0.5 * gradient_size(), False)


def draw_norm_vectors_square(key, part):
    return moment_draw(key, 60, (10, D), 0.5 * gradient_size(), True)


def draw_channel_vectors_mean(key, part):
    return moment_draw(key, 61, (KERNEL + 2, D), 0.4 * gradient_size(), False)


def draw_channel_vectors_square(key, part):
    return moment_draw(key, 62, (KERNEL + 2, D), 0.4 * gradient_size(), True)


def block_levels(stream_key, shape, cuts, least, high):
    factor_of = 1.0
    for position, shards_of in cuts:
        draws = jax.random.uniform(jax.random.fold_in(jax.random.fold_in(stream_key, 6), position), (shards_of,), jnp.float32, least / len(cuts), high / len(cuts))
        factor_of = factor_of * jnp.repeat(jnp.exp(draws), shape[position] // shards_of).reshape((-1,) + (1,) * (len(shape) - 1 - position))
    return factor_of


def normal_values(rng, shape, scale, most, shards=(), kind=jnp.bfloat16):
    loudness = block_levels(rng, shape, shards, -0.22, 0.18) if shards else 1.0
    entries = jax.random.normal(rng, shape, jnp.float32) * scale * loudness
    return jnp.minimum(jnp.maximum(entries, -most), most).astype(kind)


def setup_inputs(seed: int = 0) -> dict:
    keys = jax.random.split(jax.random.key(seed), 22)
    return {
        "tokens_in": normal_values(keys[0], (TOKENS, D), 1.0, 6.0, ((0, 16),)),
        "out_cotangent": normal_values(keys[1], (TOKENS, D), 1.0, 6.0, ((0, 16),)),
        "utt_lengths": draw_utt_lengths(jax.random.fold_in(keys[21], 71), 0),
        "feed_in": normal_values(keys[3], (2, D, FF), D ** -0.5, 0.1875, ((1, 16), (2, 2)), jnp.float32),
        "feed_in_mean": draw_feed_in_mean(jax.random.fold_in(keys[21], 71), 0),
        "feed_in_square": draw_feed_in_square(jax.random.fold_in(keys[21], 71), 0),
        "feed_out": normal_values(keys[6], (2, FF, D), FF ** -0.5, 0.09375, ((1, 2), (2, 16)), jnp.float32),
        "feed_out_mean": draw_feed_out_mean(jax.random.fold_in(keys[21], 71), 0),
        "feed_out_square": draw_feed_out_square(jax.random.fold_in(keys[21], 71), 0),
        "mixer_in": normal_values(keys[9], (5, D, D), D ** -0.5, 0.1875, ((1, 16), (2, 2)), jnp.float32),
        "mixer_in_mean": draw_mixer_in_mean(jax.random.fold_in(keys[21], 71), 0),
        "mixer_in_square": draw_mixer_in_square(jax.random.fold_in(keys[21], 71), 0),
        "mixer_out": draw_mixer_out(jax.random.fold_in(keys[21], 71), 0),
        "mixer_out_mean": draw_mixer_out_mean(jax.random.fold_in(keys[21], 71), 0),
        "mixer_out_square": draw_mixer_out_square(jax.random.fold_in(keys[21], 71), 0),
        "norm_vectors": draw_norm_vectors(jax.random.fold_in(keys[21], 71), 0),
        "norm_vectors_mean": draw_norm_vectors_mean(jax.random.fold_in(keys[21], 71), 0),
        "norm_vectors_square": draw_norm_vectors_square(jax.random.fold_in(keys[21], 71), 0),
        "channel_vectors": draw_channel_vectors(jax.random.fold_in(keys[21], 71), 0),
        "channel_vectors_mean": draw_channel_vectors_mean(jax.random.fold_in(keys[21], 71), 0),
        "channel_vectors_square": draw_channel_vectors_square(jax.random.fold_in(keys[21], 71), 0),
    }


@jax.custom_vjp
def low(v):
    return lax.optimization_barrier(v.astype(jnp.bfloat16)).astype(jnp.float32)

@jax.custom_vjp
def low_back(v):
    return v

def low_keep(v):
    return (low(v), None)

def low_pass(kept, grad):
    return (grad,)

def back_keep(v):
    return (v, None)

def back_low(kept, grad):
    return (low(grad),)
low.defvjp(low_keep, low_pass)
low_back.defvjp(back_keep, back_low)
EPS_NORM = 1e-05
EPS_ADAM = 1e-08
DECAY_WEIGHT = 0.01
BETA = 0.5
BIG_NEG = -1e+30
HIGHEST = lax.Precision.HIGHEST

def matmul(left_side, right_side):
    return jnp.dot(left_side, right_side, precision=HIGHEST, preferred_element_type=jnp.float32)

def layer_norm(values, gain_row, shift_row):
    centre = values - lax.optimization_barrier(jnp.mean(values, axis=-1, keepdims=True))
    spread = lax.optimization_barrier(jnp.mean(centre * centre, axis=-1, keepdims=True))
    return centre * lax.rsqrt(spread + EPS_NORM) * gain_row + shift_row

def swish_act(values):
    return values * jax.nn.sigmoid(values)

def rotate(values, cosine, sine_part):
    halfway = values.shape[-1] // 2
    front_half = values[..., :halfway]
    back_half = values[..., halfway:]
    return jnp.concatenate([front_half * cosine - back_half * sine_part, front_half * sine_part + back_half * cosine], axis=-1)

def depthwise(gated_rows, kernel, group_ids):
    count_rows = gated_rows.shape[0]
    reach = KERNEL // 2
    padded = jnp.pad(gated_rows, ((reach, reach), (0, 0)))
    padded_ids = jnp.pad(group_ids, (reach, reach), constant_values=-1)
    summed = jnp.zeros_like(gated_rows)
    for offset in range(KERNEL):
        matched = (padded_ids[offset:offset + count_rows] == group_ids).astype(jnp.float32)
        summed = summed + kernel[offset] * padded[offset:offset + count_rows] * matched[:, None]
    return summed

def attend_block(block_parts):
    queries, key_rows, value_rows, group_ids = block_parts
    scores = low_back(jnp.einsum('qhd,khd->hqk', queries, key_rows, precision=HIGHEST))
    allowed = (group_ids[:, None] == group_ids[None, :])[None]
    scores = jnp.where(allowed, scores, BIG_NEG)
    largest = lax.optimization_barrier(jnp.max(scores, axis=-1, keepdims=True))
    exponent = jnp.exp(scores - largest)
    softmax_rows = exponent / lax.optimization_barrier(jnp.sum(exponent, axis=-1, keepdims=True))
    return jnp.einsum('hqk,khd->qhd', low(softmax_rows), value_rows, precision=HIGHEST)

def layout(utt_lengths):
    first_len = utt_lengths[:, 0:1]
    second = utt_lengths[:, 1:2]
    places = jnp.arange(TOK_DEV, dtype=jnp.int32)[None, :]
    blocks = jnp.arange(N_DP, dtype=jnp.int32)[:, None]
    in_first = (places < first_len).astype(jnp.int32)
    in_live = (places < first_len + second).astype(jnp.int32)
    group_ids = (3 * blocks + in_first + in_live).reshape(TOKENS)
    positions = (places - first_len * (1 - in_first) - second * (1 - in_live)).reshape(TOKENS)
    return (group_ids, positions, in_live.reshape(TOKENS).astype(jnp.float32))

def forward(tokens, feed_in, feed_out, mixer_in, mixer_out, norm_vectors, channel_vectors, group_ids, positions, live_rows):
    weight_in = low(feed_in)
    weight_out = low(feed_out)
    weight_mix = low(mixer_in)
    weight_back = low(mixer_out)
    halfway = HEAD_DIM // 2
    frequency = jnp.exp(jnp.arange(halfway, dtype=jnp.float32) * (-2.0 * math.log(10000.0) / HEAD_DIM))
    angles = positions.astype(jnp.float32)[:, None] * frequency[None, :]
    cosine = jnp.cos(angles)[:, None, :]
    sine_part = jnp.sin(angles)[:, None, :]

    def feed_block(residual, norm_slot, feed_layer):
        normed = low(layer_norm(residual, norm_vectors[norm_slot], norm_vectors[5 + norm_slot]))
        hidden = low_back(matmul(normed, weight_in[feed_layer]))
        branch = low_back(matmul(low(swish_act(hidden)), weight_out[feed_layer]))
        return residual + 0.5 * branch
    section_one = feed_block(tokens, 0, 0)
    normed = low(layer_norm(section_one, norm_vectors[1], norm_vectors[6]))
    heads_shape = (TOKENS, HEADS, HEAD_DIM)
    blocked_shape = (N_DP, TOK_DEV, HEADS, HEAD_DIM)
    queries = low_back(matmul(normed, weight_mix[0])).reshape(heads_shape)
    key_rows = low_back(matmul(normed, weight_mix[1])).reshape(heads_shape)
    value_rows = low(low_back(matmul(normed, weight_mix[2]))).reshape(heads_shape)
    queries = low(rotate(queries, cosine, sine_part) * HEAD_DIM ** (-0.5))
    key_rows = low(rotate(key_rows, cosine, sine_part))
    context = lax.map(jax.checkpoint(attend_block), (queries.reshape(blocked_shape), key_rows.reshape(blocked_shape), value_rows.reshape(blocked_shape), group_ids.reshape(N_DP, TOK_DEV)))
    context = low(low_back(context.reshape(TOKENS, D)))
    section_two = section_one + low_back(matmul(context, weight_back[0]))
    normed = low(layer_norm(section_two, norm_vectors[2], norm_vectors[7]))
    lin_part = low_back(matmul(normed, weight_mix[3]))
    gate_part = low_back(matmul(normed, weight_mix[4]))
    gated_rows = lin_part * jax.nn.sigmoid(gate_part)
    mixed_rows = depthwise(gated_rows, channel_vectors[:KERNEL], group_ids)
    count_live = jnp.sum(live_rows)
    mean_batch = lax.optimization_barrier(jnp.sum(live_rows[:, None] * mixed_rows, axis=0)) / count_live
    second_moment = lax.optimization_barrier(jnp.sum(live_rows[:, None] * mixed_rows * mixed_rows, axis=0)) / count_live
    inverse_batch = lax.rsqrt(second_moment - mean_batch * mean_batch + EPS_NORM)
    batch_out = (mixed_rows - mean_batch) * inverse_batch * channel_vectors[KERNEL] + channel_vectors[KERNEL + 1]
    section_three = section_two + low_back(matmul(low(swish_act(batch_out)), weight_back[1]))
    section_four = feed_block(section_three, 3, 1)
    return layer_norm(section_four, norm_vectors[4], norm_vectors[9])

def rate_table():
    attention_fan = max(2 * D // TOK_DEV, 1)
    mixer_rates = jnp.array([attention_fan ** (-0.5), D ** (-0.5)], dtype=jnp.float32)[:, None, None]
    return (D ** (-0.5), FF ** (-0.5), D ** (-0.5), mixer_rates, 0.3, 0.3)

def adamw_step(weight, mean_state, square_state, gradient, step_rate):
    mean_next = BETA * mean_state + (1.0 - BETA) * gradient
    square_next = BETA * square_state + (1.0 - BETA) * gradient * gradient
    correct = 1.0 - BETA ** STEP_COUNT
    direction = mean_next / correct / (jnp.sqrt(square_next / correct) + EPS_ADAM)
    return (weight - step_rate * (direction + DECAY_WEIGHT * weight), mean_next, square_next)

def reference(tokens_in, out_cotangent, utt_lengths, feed_in, feed_in_mean, feed_in_square, feed_out, feed_out_mean, feed_out_square, mixer_in, mixer_in_mean, mixer_in_square, mixer_out, mixer_out_mean, mixer_out_square, norm_vectors, norm_vectors_mean, norm_vectors_square, channel_vectors, channel_vectors_mean, channel_vectors_square):
    group_ids, positions, live_rows = layout(utt_lengths)
    bound_fwd = partial(forward, group_ids=group_ids, positions=positions, live_rows=live_rows)
    tokens_out, pullback = jax.vjp(bound_fwd, tokens_in.astype(jnp.float32), feed_in, feed_out, mixer_in, mixer_out, norm_vectors, channel_vectors)
    gradients = pullback(out_cotangent.astype(jnp.float32))
    rate_list = rate_table()
    feed_in_next, feed_in_mean_next, feed_in_square_next = adamw_step(feed_in, feed_in_mean, feed_in_square, gradients[1], rate_list[0])
    feed_out_next, feed_out_mean_next, feed_out_square_next = adamw_step(feed_out, feed_out_mean, feed_out_square, gradients[2], rate_list[1])
    mixer_in_next, mixer_in_mean_next, mixer_in_square_next = adamw_step(mixer_in, mixer_in_mean, mixer_in_square, gradients[3], rate_list[2])
    mixer_out_next, mixer_out_mean_next, mixer_out_square_next = adamw_step(mixer_out, mixer_out_mean, mixer_out_square, gradients[4], rate_list[3])
    norm_vectors_next, norm_vectors_mean_next, norm_vectors_square_next = adamw_step(norm_vectors, norm_vectors_mean, norm_vectors_square, gradients[5], rate_list[4])
    channel_vectors_next, channel_vectors_mean_next, channel_vectors_square_next = adamw_step(channel_vectors, channel_vectors_mean, channel_vectors_square, gradients[6], rate_list[5])
    return (tokens_out, gradients[0], feed_in_next, feed_in_mean_next, feed_in_square_next, feed_out_next, feed_out_mean_next, feed_out_square_next, mixer_in_next, mixer_in_mean_next, mixer_in_square_next[:4], mixer_in_square_next[4], mixer_out_next, mixer_out_mean_next, mixer_out_square_next, norm_vectors_next, norm_vectors_mean_next, norm_vectors_square_next, channel_vectors_next, channel_vectors_mean_next, channel_vectors_square_next)
```

```python
import math

import jax
import jax.numpy as jnp
import numpy as np
from jax import lax
from jax.experimental import pallas as pl
from jax.experimental.pallas import tpu as pltpu
from jax.sharding import PartitionSpec as P

D = 1024
FF = 4096
HEAD_DIM = 128
KERNEL = 5
STEP_COUNT = 3
TOK_DEV = 256


EPS_NORM = 1e-05
EPS_ADAM = 1e-08
DECAY_WEIGHT = 0.01
BETA = 0.5
BIG_NEG = -1e30


def product(left_side, right_side):
    return jnp.dot(left_side, right_side, preferred_element_type=jnp.float32)


def weight_grad(inputs, gradients):
    return lax.dot_general(
        inputs, gradients, (((0,), (0,)), ((), ())), preferred_element_type=jnp.float32
    )


def input_grad(gradients, weight):
    return lax.dot_general(
        gradients, weight, (((1,), (1,)), ((), ())), preferred_element_type=jnp.float32
    )


def norm_forward(values, gain_row, shift_row):
    centre = values - jnp.mean(values, axis=-1, keepdims=True)
    inverse = lax.rsqrt(jnp.mean(centre * centre, axis=-1, keepdims=True) + EPS_NORM)
    scaled = centre * inverse
    return (scaled * gain_row + shift_row, scaled, inverse)


def norm_backward(grad_out, scaled, inverse, gain_row):
    grad_gain = jnp.sum(grad_out * scaled, axis=0)
    grad_shift = jnp.sum(grad_out, axis=0)
    grad_scaled = grad_out * gain_row
    grad_in = inverse * (
        grad_scaled
        - jnp.mean(grad_scaled, axis=-1, keepdims=True)
        - scaled * jnp.mean(grad_scaled * scaled, axis=-1, keepdims=True)
    )
    return (grad_in, grad_gain, grad_shift)


def rotate(values, cosine, sine_part):
    halfway = values.shape[-1] // 2
    front_half = values[..., :halfway]
    back_half = values[..., halfway:]
    return jnp.concatenate(
        [front_half * cosine - back_half * sine_part, front_half * sine_part + back_half * cosine],
        axis=-1,
    )


def unrotate(values, cosine, sine_part):
    halfway = values.shape[-1] // 2
    front_half = values[..., :halfway]
    back_half = values[..., halfway:]
    return jnp.concatenate(
        [front_half * cosine + back_half * sine_part, back_half * cosine - front_half * sine_part],
        axis=-1,
    )


def depthwise(gated_rows, kernel, group_ids):
    count_rows = gated_rows.shape[0]
    reach = KERNEL // 2
    padded = jnp.pad(gated_rows, ((reach, reach), (0, 0)))
    padded_ids = jnp.pad(group_ids, (reach, reach), constant_values=-1)
    summed = jnp.zeros_like(gated_rows)
    for offset in range(KERNEL):
        matched = (padded_ids[offset : offset + count_rows] == group_ids).astype(jnp.float32)
        summed = summed + kernel[offset] * padded[offset : offset + count_rows] * matched[:, None]
    return summed


def depthwise_back(grad_mixed, gated_rows, kernel, group_ids):
    count_rows = gated_rows.shape[0]
    reach = KERNEL // 2
    padded = jnp.pad(gated_rows, ((reach, reach), (0, 0)))
    padded_ids = jnp.pad(group_ids, (reach, reach), constant_values=-1)
    grad_padded = jnp.zeros_like(padded)
    kernel_rows = []
    for offset in range(KERNEL):
        matched = (padded_ids[offset : offset + count_rows] == group_ids).astype(jnp.float32)
        weighted = grad_mixed * matched[:, None]
        kernel_rows.append(jnp.sum(weighted * padded[offset : offset + count_rows], axis=0))
        grad_padded = grad_padded.at[offset : offset + count_rows].add(kernel[offset] * weighted)
    return (jnp.stack(kernel_rows), grad_padded[reach : reach + count_rows])


def rate_table():
    attention_fan = max(2 * D // TOK_DEV, 1)
    mixer_rates = jnp.array([attention_fan ** (-0.5), D ** (-0.5)], dtype=jnp.float32)[
        :, None, None
    ]
    return (D ** (-0.5), FF ** (-0.5), D ** (-0.5), mixer_rates, 0.3, 0.3)


def adamw_step(weight, mean_state, square_state, gradient, step_rate):
    mean_next = BETA * mean_state + (1.0 - BETA) * gradient
    square_next = BETA * square_state + (1.0 - BETA) * gradient * gradient
    correct = 1.0 - BETA**STEP_COUNT
    direction = mean_next / correct / (jnp.sqrt(square_next / correct) + EPS_ADAM)
    return (weight - step_rate * (direction + DECAY_WEIGHT * weight), mean_next, square_next)


def branch_total(partial_sum):
    return lax.psum(partial_sum.astype(jnp.bfloat16), "mp").astype(jnp.float32)


def input_total(partial_sum):
    return lax.psum(partial_sum.astype(jnp.bfloat16), "mp").astype(jnp.float32)


def body(
    tokens_in,
    out_cotangent,
    utt_lengths,
    feed_in,
    feed_in_mean,
    feed_in_square,
    feed_out,
    feed_out_mean,
    feed_out_square,
    mixer_in,
    mixer_in_mean,
    mixer_in_square,
    mixer_out,
    mixer_out_mean,
    mixer_out_square,
    norm_vectors,
    norm_vectors_mean,
    norm_vectors_square,
    channel_vectors,
    channel_vectors_mean,
    channel_vectors_square,
):
    count_rows = tokens_in.shape[0]
    local_width = mixer_in.shape[2]
    local_heads = local_width // HEAD_DIM
    heads_shape = (count_rows, local_heads, HEAD_DIM)
    score_scale = HEAD_DIM ** (-0.5)
    first_len = utt_lengths[0, 0]
    second = utt_lengths[0, 1]
    places = jnp.arange(count_rows, dtype=jnp.int32)
    in_first = (places < first_len).astype(jnp.int32)
    in_live = (places < first_len + second).astype(jnp.int32)
    group_ids = in_first + in_live
    positions = places - first_len * (1 - in_first) - second * (1 - in_live)
    live_rows = in_live.astype(jnp.float32)[:, None]
    halfway = HEAD_DIM // 2
    frequency = jnp.exp(
        jnp.arange(halfway, dtype=jnp.float32) * (-2.0 * math.log(10000.0) / HEAD_DIM)
    )
    angles = positions.astype(jnp.float32)[:, None] * frequency[None, :]
    cosine = jnp.cos(angles)[:, None, :]
    sine_part = jnp.sin(angles)[:, None, :]
    allowed = (group_ids[:, None] == group_ids[None, :])[None]
    kernel = channel_vectors[:KERNEL]
    batch_gain = channel_vectors[KERNEL]
    batch_shift = channel_vectors[KERNEL + 1]
    weight_in, weight_out, weight_mix, weight_back = (
        lax.all_gather(feed_in.astype(jnp.bfloat16), "dp", axis=1, tiled=True),
        lax.all_gather(feed_out.astype(jnp.bfloat16), "dp", axis=2, tiled=True),
        lax.all_gather(mixer_in.astype(jnp.bfloat16), "dp", axis=1, tiled=True),
        lax.all_gather(mixer_out.astype(jnp.bfloat16), "dp", axis=2, tiled=True),
    )

    def feed_forward(residual, norm_slot, feed_layer):
        normed, scaled, inverse = norm_forward(
            residual, norm_vectors[norm_slot], norm_vectors[5 + norm_slot]
        )
        normed_low = normed.astype(jnp.bfloat16)
        hidden = product(normed_low, weight_in[feed_layer])
        active = (hidden * jax.nn.sigmoid(hidden)).astype(jnp.bfloat16)
        branch = branch_total(product(active, weight_out[feed_layer]))
        return (residual + 0.5 * branch, (scaled, inverse, normed_low, hidden, active))

    section_zero = tokens_in.astype(jnp.float32)
    section_one, kept_first = feed_forward(section_zero, 0, 0)
    normed, scaled_att, inverse_att = norm_forward(section_one, norm_vectors[1], norm_vectors[6])
    normed_att = normed.astype(jnp.bfloat16)
    projected = jnp.einsum(
        "td,sdc->stc", normed_att, weight_mix[:3], preferred_element_type=jnp.float32
    )
    queries = (rotate(projected[0].reshape(heads_shape), cosine, sine_part) * score_scale).astype(
        jnp.bfloat16
    )
    key_rows = rotate(projected[1].reshape(heads_shape), cosine, sine_part).astype(jnp.bfloat16)
    value_rows = projected[2].reshape(heads_shape).astype(jnp.bfloat16)
    scores = jnp.where(
        allowed,
        jnp.einsum("qhd,khd->hqk", queries, key_rows, preferred_element_type=jnp.float32),
        BIG_NEG,
    )
    largest = jnp.max(scores, axis=-1, keepdims=True)
    exponent = jnp.exp(scores - largest)
    totals = jnp.sum(exponent, axis=-1, keepdims=True)
    softmax_rows = exponent / totals
    log_total = largest + jnp.log(totals)
    context = jnp.einsum(
        "hqk,khd->qhd",
        softmax_rows.astype(jnp.bfloat16),
        value_rows,
        preferred_element_type=jnp.float32,
    )
    context_low = context.reshape(count_rows, local_width).astype(jnp.bfloat16)
    section_two = section_one + branch_total(product(context_low, weight_back[0]))
    normed, scaled_conv, inverse_conv = norm_forward(section_two, norm_vectors[2], norm_vectors[7])
    normed_conv = normed.astype(jnp.bfloat16)
    conv_proj = jnp.einsum(
        "td,sdc->stc", normed_conv, weight_mix[3:], preferred_element_type=jnp.float32
    )
    gate_sig = jax.nn.sigmoid(conv_proj[1])
    gated_rows = conv_proj[0] * gate_sig
    mixed_rows = depthwise(gated_rows, kernel, group_ids)
    batch_stats = lax.psum(
        (
            jnp.sum(live_rows * mixed_rows, axis=0),
            jnp.sum(live_rows * mixed_rows * mixed_rows, axis=0),
            jnp.sum(live_rows),
        ),
        "dp",
    )
    count_live = batch_stats[2]
    mean_batch = batch_stats[0] / count_live
    inverse_batch = lax.rsqrt(batch_stats[1] / count_live - mean_batch * mean_batch + EPS_NORM)
    centred = mixed_rows - mean_batch
    batch_out = centred * inverse_batch * batch_gain + batch_shift
    batch_sig = jax.nn.sigmoid(batch_out)
    active_conv = (batch_out * batch_sig).astype(jnp.bfloat16)
    section_three = section_two + branch_total(product(active_conv, weight_back[1]))
    section_four, kept_second = feed_forward(section_three, 3, 1)
    tokens_out, scaled_last, inverse_last = norm_forward(
        section_four, norm_vectors[4], norm_vectors[9]
    )

    def feed_backward(grad_residual, kept, norm_slot, feed_layer):
        scaled, inverse, normed_low, hidden, active = kept
        grad_branch = (0.5 * grad_residual).astype(jnp.bfloat16)
        grad_down = weight_grad(active, grad_branch)
        hidden_sig = jax.nn.sigmoid(hidden)
        grad_hidden = (
            input_grad(grad_branch, weight_out[feed_layer])
            * hidden_sig
            * (1.0 + hidden * (1.0 - hidden_sig))
        ).astype(jnp.bfloat16)
        grad_up = weight_grad(normed_low, grad_hidden)
        grad_normed = input_total(input_grad(grad_hidden, weight_in[feed_layer]))
        grad_in, grad_gain, grad_shift = norm_backward(
            grad_normed, scaled, inverse, norm_vectors[norm_slot]
        )
        return (grad_residual + grad_in, grad_up, grad_down, grad_gain, grad_shift)

    grad_residual, gain_last, shift_last = norm_backward(
        out_cotangent.astype(jnp.float32), scaled_last, inverse_last, norm_vectors[4]
    )
    grad_residual, up_second, down_second, gain_three, shift_three = feed_backward(
        grad_residual, kept_second, 3, 1
    )
    grad_branch = grad_residual.astype(jnp.bfloat16)
    grad_conv_down = weight_grad(active_conv, grad_branch)
    grad_batch = (
        input_grad(grad_branch, weight_back[1]) * batch_sig * (1.0 + batch_out * (1.0 - batch_sig))
    )
    batch_sums = lax.psum(
        (jnp.sum(grad_batch, axis=0), jnp.sum(grad_batch * centred, axis=0)), "dp"
    )
    grad_var = -0.5 * inverse_batch**3 * batch_gain * batch_sums[1]
    grad_mean = -inverse_batch * batch_gain * batch_sums[0] - 2.0 * mean_batch * grad_var
    grad_mixed = (
        grad_batch * batch_gain * inverse_batch
        + live_rows * (grad_mean + 2.0 * mixed_rows * grad_var) / count_live
    )
    kernel_grads, grad_gated = depthwise_back(grad_mixed, gated_rows, kernel, group_ids)
    grad_conv_up = jnp.stack(
        [grad_gated * gate_sig, grad_gated * conv_proj[0] * gate_sig * (1.0 - gate_sig)]
    ).astype(jnp.bfloat16)
    grad_conv_in = jnp.einsum(
        "td,stc->sdc", normed_conv, grad_conv_up, preferred_element_type=jnp.float32
    )
    grad_normed = input_total(
        jnp.einsum("stc,sdc->td", grad_conv_up, weight_mix[3:], preferred_element_type=jnp.float32)
    )
    grad_in, gain_two, shift_two = norm_backward(
        grad_normed, scaled_conv, inverse_conv, norm_vectors[2]
    )
    grad_residual = grad_residual + grad_in
    grad_branch = grad_residual.astype(jnp.bfloat16)
    grad_att_down = weight_grad(context_low, grad_branch)
    grad_context = input_grad(grad_branch, weight_back[0]).astype(jnp.bfloat16).reshape(heads_shape)
    scores_again = jnp.where(
        allowed,
        jnp.einsum("qhd,khd->hqk", queries, key_rows, preferred_element_type=jnp.float32),
        BIG_NEG,
    )
    softmax_again = jnp.exp(scores_again - log_total)
    grad_softmax = jnp.einsum(
        "qhd,khd->hqk", grad_context, value_rows, preferred_element_type=jnp.float32
    )
    grad_values = jnp.einsum(
        "hqk,qhd->khd",
        softmax_again.astype(jnp.bfloat16),
        grad_context,
        preferred_element_type=jnp.float32,
    )
    grad_scores = (
        softmax_again
        * (grad_softmax - jnp.sum(softmax_again * grad_softmax, axis=-1, keepdims=True))
    ).astype(jnp.bfloat16)
    grad_queries = unrotate(
        jnp.einsum("hqk,khd->qhd", grad_scores, key_rows, preferred_element_type=jnp.float32)
        * score_scale,
        cosine,
        sine_part,
    )
    grad_keys = unrotate(
        jnp.einsum("hqk,qhd->khd", grad_scores, queries, preferred_element_type=jnp.float32),
        cosine,
        sine_part,
    )
    grad_att_up = (
        jnp.stack([grad_queries, grad_keys, grad_values])
        .reshape(3, count_rows, local_width)
        .astype(jnp.bfloat16)
    )
    grad_att_in = jnp.einsum(
        "td,stc->sdc", normed_att, grad_att_up, preferred_element_type=jnp.float32
    )
    grad_normed = input_total(
        jnp.einsum("stc,sdc->td", grad_att_up, weight_mix[:3], preferred_element_type=jnp.float32)
    )
    grad_in, gain_one, shift_one = norm_backward(
        grad_normed, scaled_att, inverse_att, norm_vectors[1]
    )
    grad_residual = grad_residual + grad_in
    grad_residual, up_first, down_first, gain_zero, shift_zero = feed_backward(
        grad_residual, kept_first, 0, 0
    )
    feed_in_grad, feed_out_grad, mixer_in_grad, mixer_out_grad = (
        lax.psum_scatter(jnp.stack([up_first, up_second]), "dp", scatter_dimension=1, tiled=True),
        lax.psum_scatter(
            jnp.stack([down_first, down_second]), "dp", scatter_dimension=2, tiled=True
        ),
        lax.psum_scatter(
            jnp.concatenate([grad_att_in, grad_conv_in], axis=0),
            "dp",
            scatter_dimension=1,
            tiled=True,
        ),
        lax.psum_scatter(
            jnp.stack([grad_att_down, grad_conv_down]), "dp", scatter_dimension=2, tiled=True
        ),
    )
    norm_grads = jnp.stack(
        [
            gain_zero,
            gain_one,
            gain_two,
            gain_three,
            gain_last,
            shift_zero,
            shift_one,
            shift_two,
            shift_three,
            shift_last,
        ]
    )
    norm_total, kernel_total = lax.psum((norm_grads, kernel_grads), "dp")
    channel_grads = jnp.concatenate(
        [kernel_total, (inverse_batch * batch_sums[1])[None], batch_sums[0][None]], axis=0
    )
    rate_list = rate_table()
    feed_in_next, feed_in_mean_next, feed_in_square_next = adamw_step(
        feed_in, feed_in_mean, feed_in_square, feed_in_grad, rate_list[0]
    )
    feed_out_next, feed_out_mean_next, feed_out_square_next = adamw_step(
        feed_out, feed_out_mean, feed_out_square, feed_out_grad, rate_list[1]
    )
    mixer_in_next, mixer_in_mean_next, mixer_in_square_next = adamw_step(
        mixer_in, mixer_in_mean, mixer_in_square, mixer_in_grad, rate_list[2]
    )
    mixer_out_next, mixer_out_mean_next, mixer_out_square_next = adamw_step(
        mixer_out, mixer_out_mean, mixer_out_square, mixer_out_grad, rate_list[3]
    )
    norm_vectors_next, norm_vectors_mean_next, norm_vectors_square_next = adamw_step(
        norm_vectors, norm_vectors_mean, norm_vectors_square, norm_total, rate_list[4]
    )
    channel_vectors_next, channel_vectors_mean_next, channel_vectors_square_next = adamw_step(
        channel_vectors, channel_vectors_mean, channel_vectors_square, channel_grads, rate_list[5]
    )
    return (
        tokens_out,
        grad_residual,
        feed_in_next,
        feed_in_mean_next,
        feed_in_square_next,
        feed_out_next,
        feed_out_mean_next,
        feed_out_square_next,
        mixer_in_next,
        mixer_in_mean_next,
        mixer_in_square_next[:4],
        mixer_in_square_next[4],
        mixer_out_next,
        mixer_out_mean_next,
        mixer_out_square_next,
        norm_vectors_next,
        norm_vectors_mean_next,
        norm_vectors_square_next,
        channel_vectors_next,
        channel_vectors_mean_next,
        channel_vectors_square_next,
    )


MESH = pl.DeviceIdType.MESH
F32 = jnp.float32
BF16 = jnp.bfloat16
ROWS = 256
HALF = 128
QUAD = 64
SHARD = 64
G_IN0, G_OUT0, G_ATT, G_CONV, G_IN1, G_OUT1 = range(6)


def dot_nn(a, b):
    return lax.dot_general(a, b, (((1,), (0,)), ((), ())), preferred_element_type=F32)


def dot_nt(a, b):
    return lax.dot_general(a, b, (((1,), (1,)), ((), ())), preferred_element_type=F32)


def dot_tn(a, b):
    return lax.dot_general(a, b, (((0,), (0,)), ((), ())), preferred_element_type=F32)


def sigm(v):
    return 1.0 / (1.0 + jnp.exp(-v))


def fused_kernel(
    tok, cot, lens, rot_hi, rot_lo, nv, cv, fi_b, fo_b, mi_b, mo_b,
    tout, tgrad, gfi, gfo, gmi, gmo, ngrad, cgrad,
    w0, w1, w2, w3, w4, w5, xg0, xg1, xg2, xg3, xb0, xb1,
    fh0, fh1, fs0, fs1, hb, qr, kr, vr, ctx, dqkv, pf,
    cu, sg, glu, zc, dd, cw, du, gid, live, rc_t, rs_t, lb,
    xh, inv, res, so, si, sd, hx, hy, sx, sy, rx, ry, keep, part,
    gs0, gs1, gs2, gs3, gs4, gs5, gi0, gi1, gi2, gi3, gi4, gi5,
    ac0, ac1, ac2, ac3, ac4, ac5, stats, tapm, ngm, nsib, nx, ny, nz, cgm, tstage,
    ags, agr, rss, rsr, was, war, zs, zr, grs, grr, gas, gar, lss, lsr,
    bns, bnr, nss, nsr, cgs, cgr, outs, outr, loc,
):
    w = (w0, w1, w2, w3, w4, w5)
    gst = (gs0, gs1, gs2, gs3, gs4, gs5)
    gin = (gi0, gi1, gi2, gi3, gi4, gi5)
    acc = (ac0, ac1, ac2, ac3, ac4, ac5)
    dp = lax.axis_index("dp")
    m = lax.axis_index("mp")
    x = dp % 2
    y = (dp // 2) % 2
    z = dp // 4
    p = dp % 4
    base = z * 4
    px = p + 1 - 2 * x
    py = p + 2 - 4 * y
    pd = 3 - p
    sib = (dp, 1 - m)
    xn = (base + px, m)
    yn = (base + py, m)
    dn = (base + pd, m)
    plane = ((px, xn), (py, yn), (pd, dn))
    inner = (z + 1) // 2 % 2
    others = tuple((z + k) % 4 for k in (1, 2, 3))

    def zdev(zz):
        return (zz * 4 + p, m)

    def remote(src, dst, ssem, rsem, dev):
        return pltpu.make_async_remote_copy(
            src_ref=src, dst_ref=dst, send_sem=ssem, recv_sem=rsem, device_id=dev, device_id_type=MESH
        )

    def rows(start, size):
        return pl.ds(pl.multiple_of(start, size), size)

    def block(b):
        return rows(b * ROWS, ROWS)

    pending = []

    def go_send(copy):
        copy.start()
        pending.append(copy)

    barrier = pltpu.get_barrier_semaphore()
    greet = (sib, xn, yn, dn) + tuple(zdev(k) for k in others)
    for dev in greet:
        pl.semaphore_signal(barrier, inc=1, device_id=dev, device_id_type=MESH)
    pl.semaphore_wait(barrier, len(greet))

    def wview(g, start, size):
        r = pl.ds(pl.multiple_of(start, SHARD), size)
        return w[g].at[:, r] if g in (G_ATT, G_CONV) else w[g].at[r]

    def columns(i, wd):
        return pl.ds(pl.multiple_of(i * wd, 128), wd)

    def wpieces(g, peer, owner):
        r = pl.ds(pl.multiple_of(z * ROWS + owner * SHARD, SHARD), SHARD)
        if g == G_ATT:
            return (
                (mi_b.at[0:3, :, columns(peer, 128)], w[g].at[0:3, r]),
                (mo_b.at[0, :, columns(peer, 128)], w[g].at[3, r]),
            )
        if g == G_CONV:
            return (
                (mi_b.at[3:5, :, columns(peer, 128)], w[g].at[0:2, r]),
                (mo_b.at[1, :, columns(peer, 128)], w[g].at[2, r]),
            )
        src = fi_b if g in (G_IN0, G_IN1) else fo_b
        layer = 0 if g in (G_IN0, G_OUT0) else 1
        return ((src.at[layer, :, columns(peer, 512)], w[g].at[r]),)

    def plane_start(g):
        for r, (peer, dev) in enumerate(plane):
            for k, (src, dst) in enumerate(wpieces(g, peer, p)):
                go_send(remote(src, dst, was.at[g, r, k], war.at[g, r, k], dev))
        for k, (src, dst) in enumerate(wpieces(g, p, p)):
            pltpu.make_async_copy(src, dst, was.at[g, 3, k]).start()

    def plane_wait(g):
        for r, (peer, dev) in enumerate(plane):
            for k, (_, dst) in enumerate(wpieces(g, peer, peer)):
                remote(dst, dst, was.at[g, r, k], war.at[g, r, k], dev).wait_recv()
        for k, (src, dst) in enumerate(wpieces(g, p, p)):
            pltpu.make_async_copy(src, dst, was.at[g, 3, k]).wait()

    targets = {0: (2, 1), 1: (3, 0, 2), 2: (0, 3, 1), 3: (1, 2)}
    far = {1: (3, 0), 2: (0, 3)}

    def zcopy(g, owner, k, to):
        part_w = wview(g, owner * ROWS, ROWS)
        return remote(part_w, part_w, zs.at[g, k], zr.at[g, owner], zdev(to))

    def line_start(g):
        plane_wait(g)
        for zz, tos in targets.items():

            @pl.when(z == zz)
            def _():
                for k, to in enumerate(tos):
                    zcopy(g, zz, k, to).start()

    def line_pass(g):
        for zz, (owner, to) in far.items():

            @pl.when(z == zz)
            def _():
                zcopy(g, owner, 3, to).wait_recv()
                zcopy(g, owner, 3, to).start()

    def line_ready(g):
        for zz in range(4):

            @pl.when(z == zz)
            def _():
                for owner in range(4):
                    if owner != zz and (zz not in far or far[zz][0] != owner):
                        zcopy(g, owner, 0, zz).wait_recv()

    def line_done(g):
        for zz, tos in targets.items():

            @pl.when(z == zz)
            def _():
                for k, to in enumerate(tos):
                    zcopy(g, zz, k, to).wait_send()
                if zz in far:
                    zcopy(g, far[zz][0], 3, far[zz][1]).wait_send()

    def own_rows(b, c, off=0, size=HALF):
        return rows(b * ROWS + c * HALF + off, size) if off == 0 else pl.ds(
            pl.multiple_of(b * ROWS + c * HALF + off, QUAD), size
        )

    mine = rows(p * ROWS + m * HALF, HALF)

    def gather(xg, compute, fill0=None, fill1=None, fill2=None):
        def c(i, b, core, off, size, dev):
            r = xg.at[own_rows(b, core, off, size)]
            return remote(r, r, ags.at[i], agr.at[i], dev)

        n = 1 - m
        sends = []

        def start(*a):
            k = c(*a)
            k.start()
            sends.append(k)

        start(0, p, m, 0, HALF, sib)
        start(1, p, m, 0, QUAD, xn)
        start(3, p, m, QUAD, QUAD, yn)
        start(2, p, m, QUAD, QUAD, xn)
        start(4, p, m, 0, QUAD, yn)
        if fill0 is not None:
            fill0()
        c(0, p, n, 0, HALF, sib).wait_recv()
        compute(p)
        c(1, px, m, 0, QUAD, xn).wait_recv()
        start(5, px, m, 0, QUAD, yn)
        c(3, py, m, QUAD, QUAD, yn).wait_recv()
        start(6, py, m, QUAD, QUAD, xn)
        if fill1 is not None:
            fill1()
        c(2, px, m, QUAD, QUAD, xn).wait_recv()
        start(7, px, m, 0, HALF, sib)
        c(4, py, m, 0, QUAD, yn).wait_recv()
        start(8, py, m, 0, HALF, sib)
        c(7, px, n, 0, HALF, sib).wait_recv()
        compute(px)
        c(8, py, n, 0, HALF, sib).wait_recv()
        compute(py)
        c(5, pd, m, 0, QUAD, yn).wait_recv()
        start(9, pd, m, 0, QUAD, sib)
        c(6, pd, m, QUAD, QUAD, xn).wait_recv()
        start(10, pd, m, QUAD, QUAD, sib)
        if fill2 is not None:
            fill2()
        c(9, pd, n, 0, QUAD, sib).wait_recv()
        c(10, pd, n, QUAD, QUAD, sib).wait_recv()
        compute(pd)
        for k in sends:
            k.wait_send()

    def scatter(compute, fill0=None, fill1=None):
        keep_rows = rows(m * HALF, HALF)
        give_rows = rows((1 - m) * HALF, HALF)
        sends = []

        def start(k):
            k.start()
            sends.append(k)

        def csib(i):
            return remote(so.at[i], si.at[i], rss.at[i], rsr.at[i], sib)

        def term(i, b):
            compute(b)
            so[i] = part[give_rows, :].astype(BF16)
            start(csib(i))
            keep[i] = part[keep_rows, :]

        a = slice(0, QUAD)
        bb = slice(QUAD, HALF)
        chx = remote(sd.at[a], hx, rss.at[4], rsr.at[4], xn)
        chy = remote(sd.at[bb], hy, rss.at[5], rsr.at[5], yn)
        cxa = remote(sx.at[a], rx.at[a], rss.at[6], rsr.at[6], xn)
        cxb = remote(sx.at[bb], rx.at[bb], rss.at[7], rsr.at[7], xn)
        cyb = remote(sy.at[bb], ry.at[bb], rss.at[8], rsr.at[8], yn)
        cya = remote(sy.at[a], ry.at[a], rss.at[9], rsr.at[9], yn)
        term(0, pd)
        term(1, px)
        csib(0).wait_recv()
        sd[...] = (keep[0] + si[0].astype(F32)).astype(BF16)
        start(chx)
        start(chy)
        term(2, py)
        csib(1).wait_recv()
        sx[a, :] = (keep[1, a, :] + si[1, a, :].astype(F32)).astype(BF16)
        start(cxa)
        csib(2).wait_recv()
        sy[bb, :] = (keep[2, bb, :] + si[2, bb, :].astype(F32)).astype(BF16)
        start(cyb)
        term(3, p)
        if fill0 is not None:
            fill0()
        chy.wait_recv()
        sx[bb, :] = (keep[1, bb, :] + si[1, bb, :].astype(F32) + hy[...].astype(F32)).astype(BF16)
        start(cxb)
        chx.wait_recv()
        sy[a, :] = (keep[2, a, :] + si[2, a, :].astype(F32) + hx[...].astype(F32)).astype(BF16)
        start(cya)
        if fill1 is not None:
            fill1()
        csib(3).wait_recv()
        cxa.wait_recv()
        cyb.wait_recv()
        cxb.wait_recv()
        cya.wait_recv()
        total = keep[3] + si[3].astype(F32) + rx[...].astype(F32) + ry[...].astype(F32)
        for k in sends:
            k.wait_send()
        return total

    def norm(v, i):
        centre = v - jnp.mean(v, axis=-1, keepdims=True)
        scale = lax.rsqrt(jnp.mean(centre * centre, axis=-1, keepdims=True) + EPS_NORM)
        hat = centre * scale
        xh[i] = hat
        inv[i] = jnp.broadcast_to(scale, (HALF, 128))
        return hat * nv[i : i + 1, :] + nv[5 + i : 6 + i, :]

    def norm_back(g, i):
        hat = xh[i]
        scale = inv[i, :, 0:1]
        ngm[i : i + 1, :] = jnp.sum(g * hat, axis=0, keepdims=True)
        ngm[5 + i : 6 + i, :] = jnp.sum(g, axis=0, keepdims=True)
        e = g * nv[i : i + 1, :]
        return scale * (
            e
            - jnp.mean(e, axis=-1, keepdims=True)
            - hat * jnp.mean(e * hat, axis=-1, keepdims=True)
        )

    outer = 1 - inner
    c0 = 3 * (1 - z // 2)
    c1 = 2 - z // 2
    c2 = z + 1 - 2 * (z % 2)
    order = (c0, c1, c2, z)

    def grad_chunk(g, k):
        zz = order[k]
        cols = pl.ds(pl.multiple_of(zz * ROWS, ROWS), ROWS)
        if g == G_IN0:
            v = dot_tn(xg0[:, cols], hb[...])
        elif g == G_OUT0:
            v = dot_tn(xb1[:, cols], fs0[...])
        elif g == G_IN1:
            v = dot_tn(xg3[:, cols], hb[...])
        elif g == G_OUT1:
            v = dot_tn(xb0[:, cols], fs1[...])
        if g == G_ATT:
            v = dot_tn(xg1[:, cols], dqkv[...]).astype(BF16)
            for k in range(3):
                gst[g][zz, k] = v[:, k * 128 : (k + 1) * 128]
            gst[g][zz, 3] = dot_tn(xb0[:, cols], ctx[...]).astype(BF16)
        elif g == G_CONV:
            v = dot_tn(xg2[:, cols], du[...]).astype(BF16)
            for k in range(2):
                gst[g][zz, k] = v[:, k * 128 : (k + 1) * 128]
            gst[g][zz, 2] = dot_tn(xb1[:, cols], cw[...]).astype(BF16)
        else:
            gst[g][zz] = v.astype(BF16)

    neighbour = 1 + z // 2

    def acc_copy(g):
        return remote(gst[g].at[c0], acc[g], grs.at[g, 0], grr.at[g, 3], zdev(neighbour))

    def slot_copy(g, k):
        zz = order[k]
        if k == 0:
            slot = 1
        elif k == 1:
            slot = 1 + outer
        else:
            slot = 0
        return remote(gst[g].at[zz], gin[g].at[slot], grs.at[g, k], grr.at[g, slot], zdev(zz))

    def grad_send(g, k):
        if k == 0:

            @pl.when(outer == 1)
            def _():
                acc_copy(g).start()
        elif k < 3:
            slot_copy(g, k).start()

    def grad_acc(g):
        @pl.when(inner == 1)
        def _():
            acc_copy(g).wait_recv()
            gst[g][c0] = (gst[g][c0].astype(F32) + acc[g][...].astype(F32)).astype(BF16)
            slot_copy(g, 0).start()

    def gpieces(g, peer, owner):
        r = pl.ds(pl.multiple_of(peer * SHARD, SHARD), SHARD)
        if g == G_ATT:
            return (
                (gst[g].at[z, 0:3, r], gmi.at[0:3, :, columns(owner, 128)]),
                (gst[g].at[z, 3, r], gmo.at[0, :, columns(owner, 128)]),
            )
        if g == G_CONV:
            return (
                (gst[g].at[z, 0:2, r], gmi.at[3:5, :, columns(owner, 128)]),
                (gst[g].at[z, 2, r], gmo.at[1, :, columns(owner, 128)]),
            )
        dst = gfi if g in (G_IN0, G_IN1) else gfo
        layer = 0 if g in (G_IN0, G_OUT0) else 1
        return ((gst[g].at[z, r], dst.at[layer, :, columns(owner, 512)]),)

    def gplane(g):
        return [
            remote(src, dst, gas.at[g, r, k], gar.at[g, r, k], dev)
            for r, (peer, dev) in enumerate(plane)
            for k, (src, dst) in enumerate(gpieces(g, peer, p))
        ] + [
            pltpu.make_async_copy(src, dst, gas.at[g, 3, k])
            for k, (src, dst) in enumerate(gpieces(g, p, p))
        ]

    def slot_wait(g, slot):
        remote(gin[g].at[slot], gin[g].at[slot], grs.at[g, 1], grr.at[g, slot], sib).wait_recv()

    def grad_final(g):
        slot_wait(g, 0)
        slot_wait(g, 1)
        t = gst[g][z].astype(F32) + gin[g][0].astype(F32) + gin[g][1].astype(F32)
        keep_t = t

        @pl.when(outer == 1)
        def _():
            gst[g][z] = keep_t.astype(BF16)

        @pl.when(inner == 1)
        def _():
            slot_wait(g, 2)
            gst[g][z] = (keep_t + gin[g][2].astype(F32)).astype(BF16)

        for copy in gplane(g):
            copy.start()

    def grad_done(g):
        for r, (peer, dev) in enumerate(plane):
            for k, (_, dst) in enumerate(gpieces(g, peer, peer)):
                remote(dst, dst, gas.at[g, r, k], gar.at[g, r, k], dev).wait_recv()
        for i, copy in enumerate(gplane(g)):
            if i < 3 * len(gpieces(g, p, p)):
                copy.wait_send()
            else:
                copy.wait()

        @pl.when(outer == 1)
        def _():
            acc_copy(g).wait_send()

        @pl.when(inner == 1)
        def _():
            slot_copy(g, 0).wait_send()

        slot_copy(g, 1).wait_send()
        slot_copy(g, 2).wait_send()

    def line_share(buf, sem_s, sem_r, start):
        for k in range(3):
            to = others[k]
            if start:
                remote(buf.at[z], buf.at[z], sem_s.at[k], sem_r.at[2 - k], zdev(to)).start()
            else:
                frm = others[2 - k]
                remote(buf.at[z], buf.at[z], sem_s.at[k], sem_r.at[2 - k], zdev(to)).wait_send()
                remote(buf.at[frm], buf.at[frm], sem_s.at[k], sem_r.at[2 - k], zdev(frm)).wait_recv()

    stats[...] = jnp.zeros_like(stats)
    tapm[...] = jnp.zeros_like(tapm)
    lb[p] = lens[...]
    for r in range(3):
        peer, dev = plane[r]
        remote(lb.at[p], lb.at[p], lss.at[r], lsr.at[r], dev).start()
    plane_start(G_IN0)
    half_in = rows(m * HALF, HALF)
    first = tok[half_in, :].astype(F32)
    res[...] = first
    xg0[mine, :] = norm(first, 0).astype(BF16)

    def nothing(b):
        return None

    def start_a():
        line_start(G_IN0)
        plane_start(G_OUT0)

    def tables():
        for r in range(3):
            peer, dev = plane[r]
            remote(lb.at[p], lb.at[p], lss.at[r], lsr.at[r], dev).wait_send()
            remote(lb.at[peer], lb.at[peer], lss.at[r], lsr.at[r], dev).wait_recv()
        place = lax.broadcasted_iota(jnp.int32, (ROWS, ROWS), 0).astype(F32)
        lane = lax.broadcasted_iota(jnp.int32, (ROWS, ROWS), 1).astype(F32)
        for b in range(4):
            l0 = lb[b, 0:1, :]
            l1 = lb[b, 1:2, :]
            first_in = jnp.where(place < l0, 1.0, 0.0)
            live_in = jnp.where(place < l0 + l1, 1.0, 0.0)
            at = place - l0 * (1.0 - first_in) - l1 * (1.0 - live_in)
            r = slice(b * ROWS, (b + 1) * ROWS)
            gid[r, :] = 3.0 * b + first_in[:, :128] + live_in[:, :128]
            live[r, :] = live_in[:, :128]
            hot = jnp.where(at == lane, 1.0, 0.0).astype(BF16)
            t = dot_nn(hot, rot_hi[...]) + dot_nn(hot, rot_lo[...])
            rc_t[r, :] = t[:, :128]
            rs_t[r, :] = t[:, 128:]

    def fill_b():
        line_pass(G_IN0)
        line_start(G_OUT0)

    gather(xg0, nothing, start_a, tables, fill_b)
    for g in (G_ATT, G_CONV, G_IN1, G_OUT1):
        plane_start(g)

    def ff_hidden(xg, g, fh, fs):
        def f(b):
            r = block(b)
            h = dot_nn(xg[r, :], w[g][...])
            fh[r, :] = h
            fs[r, :] = (h * sigm(h)).astype(BF16)

        return f

    def wide(g, first, last):
        return jnp.concatenate([w[g][k] for k in range(first, last)], axis=1)

    def part_nt(lhs, weight):
        def f(b):
            part[...] = dot_nt(lhs[block(b), :], weight())

        return f

    def whole(g):
        return lambda: w[g][...]

    line_ready(G_IN0)
    hidden = ff_hidden(xg0, G_IN0, fh0, fs0)
    for b in (pd, px, py, p):
        hidden(b)
    line_pass(G_OUT0)
    line_start(G_ATT)
    line_ready(G_OUT0)

    def fill_c():
        line_pass(G_ATT)
        line_start(G_CONV)

    def fill_d():
        line_pass(G_CONV)
        line_start(G_IN1)

    def fill_e():
        line_pass(G_IN1)
        line_start(G_OUT1)

    def fill_f():
        line_pass(G_OUT1)

    x1 = res[...] + 0.5 * scatter(part_nt(fs0, whole(G_OUT0)), None, fill_c)
    res[...] = x1
    xg1[mine, :] = norm(x1, 1).astype(BF16)

    def turn(v, r):
        return v * rc_t[r, :] + pltpu.roll(v, 64, 1) * rs_t[r, :]

    def turn_back(v, r):
        return v * rc_t[r, :] - pltpu.roll(v, 64, 1) * rs_t[r, :]

    lane_row = lax.broadcasted_iota(jnp.int32, (1, ROWS), 1).astype(F32)

    def attend(b):
        r = block(b)
        t = dot_nn(xg1[r, :], wide(G_ATT, 0, 3))
        q = (turn(t[:, 0:128], r) * (HEAD_DIM**-0.5)).astype(BF16)
        k = turn(t[:, 128:256], r).astype(BF16)
        v = t[:, 256:384].astype(BF16)
        qr[r, :] = q
        kr[r, :] = k
        vr[r, :] = v
        s = dot_nt(q, k)
        l0 = lb[b, 0:1, :]
        l1 = lb[b, 1:2, :]
        gk = (
            3.0 * b.astype(F32)
            + jnp.where(lane_row < l0, 1.0, 0.0)
            + jnp.where(lane_row < l0 + l1, 1.0, 0.0)
        )
        gq = gid[r, :]
        gq = jnp.concatenate([gq, gq], axis=1)
        s = jnp.where(gq == gk, s, BIG_NEG)
        e = jnp.exp(s - jnp.max(s, axis=-1, keepdims=True))
        pr = e / jnp.sum(e, axis=-1, keepdims=True)
        pf[r, :] = pr
        ctx[r, :] = dot_nn(pr.astype(BF16), v).astype(BF16)

    gather(xg1, nothing, None, None, None)
    line_ready(G_ATT)
    for b in (pd, px, py, p):
        attend(b)
    x2 = res[...] + scatter(part_nt(ctx, lambda: w[G_ATT][3]), None, fill_d)
    res[...] = x2
    xg2[mine, :] = norm(x2, 2).astype(BF16)

    chan = pl.ds(pl.multiple_of(p * 128, 128), 128)
    taps = [cv[j : j + 1, chan] for j in range(KERNEL)]
    gain = cv[KERNEL : KERNEL + 1, chan]
    shift = cv[KERNEL + 1 : KERNEL + 2, chan]

    def conv_in(b):
        r = block(b)
        t = dot_nn(xg2[r, :], wide(G_CONV, 0, 2))
        s = sigm(t[:, 128:256])
        cu[r, :] = t[:, 0:128]
        sg[r, :] = s
        glu[r, :] = t[:, 0:128] * s

    gather(xg2, nothing, None, None, None)
    line_ready(G_CONV)
    for b in (pd, px, py, p):
        conv_in(b)
    count = 4 * ROWS

    def same(j):
        ids = gid[...]
        return jnp.where(pltpu.roll(ids, (2 - j) % count, 0) == ids, 1.0, 0.0)

    g_all = glu[...]
    mixed = taps[2] * g_all
    for j in (0, 1, 3, 4):
        mixed = mixed + taps[j] * pltpu.roll(g_all, (2 - j) % count, 0) * same(j)
    zc[...] = mixed
    lv = live[...]
    stats[0, z, 0:1, :] = jnp.sum(lv * mixed, axis=0, keepdims=True)
    stats[0, z, 1:2, :] = jnp.sum(lv * mixed * mixed, axis=0, keepdims=True)
    stats[0, z, 2:3, :] = jnp.sum(lv, axis=0, keepdims=True)
    line_share(stats.at[0], bns.at[0], bnr.at[0], True)
    line_share(stats.at[0], bns.at[0], bnr.at[0], False)
    tot = stats[0, 0] + stats[0, 1] + stats[0, 2] + stats[0, 3]
    n_live = tot[2:3, :]
    mean_b = tot[0:1, :] / n_live
    inv_b = lax.rsqrt(tot[1:2, :] / n_live - mean_b * mean_b + EPS_NORM)

    def conv_out(b):
        r = block(b)
        bn = (zc[r, :] - mean_b) * inv_b * gain + shift
        cw[r, :] = (bn * sigm(bn)).astype(BF16)
        part[...] = dot_nt(cw[r, :], w[G_CONV][2])

    x3 = res[...] + scatter(conv_out, None, fill_e)
    res[...] = x3
    xg3[mine, :] = norm(x3, 3).astype(BF16)
    gather(xg3, nothing, None, None, fill_f)
    line_ready(G_IN1)
    hidden = ff_hidden(xg3, G_IN1, fh1, fs1)
    for b in (pd, px, py, p):
        hidden(b)
    line_ready(G_OUT1)
    x4 = res[...] + 0.5 * scatter(part_nt(fs1, whole(G_OUT1)), None, None)
    tstage[0] = norm(x4, 4)

    def give_out(i, out):
        return (
            pltpu.make_async_copy(tstage.at[i], out.at[half_in], loc.at[6 + i]),
            remote(tstage.at[i], out.at[half_in], outs.at[i], outr.at[i], sib),
        )

    for copy in give_out(0, tout):
        copy.start()

    dx = norm_back(cot[half_in, :].astype(F32), 4)
    res[...] = dx
    xb0[mine, :] = (0.5 * dx).astype(BF16)

    def ff_back(xb, g, fh):
        def f(b):
            r = block(b)
            h = fh[r, :]
            s = sigm(h)
            d = dot_nn(xb[r, :], w[g][...])
            hb[r, :] = (d * s * (1.0 + h * (1.0 - s))).astype(BF16)

        return f

    gather(xb0, ff_back(xb0, G_OUT1, fh1))

    def grads_now(g):
        def f():
            for k in range(4):
                grad_chunk(g, k)
                grad_send(g, k)

        return f

    def grads_later(g):
        def f():
            for k in range(4):
                grad_chunk(g, k)

        return f

    d_norm = scatter(part_nt(hb, whole(G_IN1)), grads_now(G_OUT1), None)
    dx = res[...] + norm_back(d_norm, 3)
    res[...] = dx
    xb1[mine, :] = dx.astype(BF16)

    def conv_back(b):
        r = block(b)
        bn = (zc[r, :] - mean_b) * inv_b * gain + shift
        s = sigm(bn)
        dd[r, :] = dot_nn(xb1[r, :], w[G_CONV][2]) * s * (1.0 + bn * (1.0 - s))

    def fill_g():
        grads_later(G_IN1)()
        grad_acc(G_OUT1)

    gather(xb1, conv_back, fill_g)
    d_all = dd[...]
    z_all = zc[...]
    stats[1, z, 0:1, :] = jnp.sum(d_all, axis=0, keepdims=True)
    stats[1, z, 1:2, :] = jnp.sum(d_all * (z_all - mean_b), axis=0, keepdims=True)
    line_share(stats.at[1], bns.at[1], bnr.at[1], True)
    line_share(stats.at[1], bns.at[1], bnr.at[1], False)
    tot = stats[1, 0] + stats[1, 1] + stats[1, 2] + stats[1, 3]
    s1 = tot[0:1, :]
    s2 = tot[1:2, :]
    d_var = -0.5 * inv_b * inv_b * inv_b * gain * s2
    d_mean = -inv_b * gain * s1 - 2.0 * mean_b * d_var
    dz = d_all * (gain * inv_b) + live[...] * ((d_mean + 2.0 * z_all * d_var) / n_live)
    g_all = glu[...]
    back = jnp.zeros_like(dz)
    for j in range(KERNEL):
        if j == 2:
            weighted = dz
            moved = g_all
        else:
            weighted = dz * same(j)
            moved = pltpu.roll(g_all, (2 - j) % count, 0)
        tapm[z, j : j + 1, :] = jnp.sum(weighted * moved, axis=0, keepdims=True)
        weighted = taps[j] * weighted
        if j != 2:
            weighted = pltpu.roll(weighted, (j - 2) % count, 0)
        back = back + weighted
    line_share(tapm, bns.at[2], bnr.at[2], True)
    for k in range(3):
        grad_send(G_IN1, k)
    s_all = sg[...]
    du[:, 0:128] = (back * s_all).astype(BF16)
    du[:, 128:256] = (back * cu[...] * s_all * (1.0 - s_all)).astype(BF16)

    def fill_h():
        grads_now(G_CONV)()

    def fill_i():
        grad_acc(G_IN1)

    d_norm = scatter(part_nt(du, lambda: wide(G_CONV, 0, 2)), fill_h, fill_i)
    dx = res[...] + norm_back(d_norm, 2)
    res[...] = dx
    xb0[mine, :] = dx.astype(BF16)

    def attend_back(b):
        r = block(b)
        dc = dot_nn(xb0[r, :], w[G_ATT][3]).astype(BF16)
        pr = pf[r, :]
        q = qr[r, :]
        k = kr[r, :]
        dp_ = dot_nt(dc, vr[r, :])
        dqkv[r, 256:384] = dot_tn(pr.astype(BF16), dc).astype(BF16)
        sb = (pr * (dp_ - jnp.sum(pr * dp_, axis=-1, keepdims=True))).astype(BF16)
        dqkv[r, 0:128] = turn_back(dot_nn(sb, k) * (HEAD_DIM**-0.5), r).astype(BF16)
        dqkv[r, 128:256] = turn_back(dot_tn(sb, q), r).astype(BF16)

    def fill_j():
        grad_final(G_OUT1)

    gather(xb0, attend_back, None, None, fill_j)

    def fill_k():
        grads_now(G_ATT)()

    def fill_l():
        grad_acc(G_CONV)

    d_norm = scatter(part_nt(dqkv, lambda: wide(G_ATT, 0, 3)), fill_k, fill_l)
    dx = res[...] + norm_back(d_norm, 1)
    res[...] = dx
    xb1[mine, :] = (0.5 * dx).astype(BF16)

    def fill_m():
        grad_acc(G_ATT)
        grad_final(G_IN1)

    gather(xb1, ff_back(xb1, G_OUT0, fh0), None, None, fill_m)
    grads_now(G_OUT0)()
    grads_now(G_IN0)()

    def fill_n():
        grad_final(G_CONV)
        grad_acc(G_OUT0)

    d_norm = scatter(part_nt(hb, whole(G_IN0)), None, fill_n)
    tstage[1] = res[...] + norm_back(d_norm, 0)
    for copy in give_out(1, tgrad):
        copy.start()
    grad_final(G_ATT)
    grad_acc(G_IN0)

    def swap(src, dst, k, dev):
        copy = remote(src, dst, nss.at[k], nsr.at[k], dev)
        copy.start()
        copy.wait()

    ngm[10:16, :] = jnp.zeros((6, D), F32)
    swap(ngm, nsib, 0, sib)
    ngm[...] = ngm[...] + nsib[...]
    swap(ngm, nx, 1, xn)
    ngm[...] = ngm[...] + nx[...]
    swap(ngm, ny, 2, yn)
    nz[z] = ngm[...] + ny[...]
    line_share(nz, nss.at[pl.ds(3, 3)], nsr.at[pl.ds(3, 3)], True)
    line_share(tapm, bns.at[2], bnr.at[2], False)
    cgm[...] = tapm[0] + tapm[1] + tapm[2] + tapm[3]
    cgm[5:6, :] = inv_b * s2
    cgm[6:7, :] = s1
    cgrad[:, chan] = cgm[...]
    for r in range(3):
        remote(cgm, cgrad.at[:, chan], cgs.at[r], cgr.at[r], plane[r][1]).start()
    grad_final(G_OUT0)
    line_share(nz, nss.at[pl.ds(3, 3)], nsr.at[pl.ds(3, 3)], False)
    ngrad[...] = nz[0] + nz[1] + nz[2] + nz[3]
    for r in range(3):
        peer, dev = plane[r]
        there = cgrad.at[:, pl.ds(pl.multiple_of(peer * 128, 128), 128)]
        remote(there, there, cgs.at[r], cgr.at[r], dev).wait_recv()
        remote(cgm, cgrad.at[:, chan], cgs.at[r], cgr.at[r], dev).wait_send()
    grad_final(G_IN0)
    other_half = rows((1 - m) * HALF, HALF)
    for i, out in enumerate((tout, tgrad)):
        a, b = give_out(i, out)
        a.wait()
        b.wait_send()
        remote(out.at[other_half], out.at[other_half], outs.at[i], outr.at[i], sib).wait_recv()
    for copy in pending:
        copy.wait_send()
    for g in range(6):
        line_done(g)
        grad_done(g)


def group_shape(g, rows):
    if g == G_ATT:
        return (4, rows, 128)
    if g == G_CONV:
        return (3, rows, 128)
    return (rows, 512)


def rotation_tables():
    half = HEAD_DIM // 2
    frequency = np.exp(np.arange(half, dtype=np.float32) * np.float32(-2.0 * math.log(10000.0) / HEAD_DIM))
    angles = np.arange(ROWS, dtype=np.float32)[:, None] * frequency.astype(np.float32)[None, :]
    c = np.cos(angles.astype(np.float64))
    s = np.sin(angles.astype(np.float64))
    table = np.concatenate([c, c, -s, s], axis=1).astype(np.float32)
    high = table.astype(BF16)
    low_part = (table - high.astype(np.float32)).astype(BF16)
    return high, low_part


def fused_call(tok, cot, lens, norm_vectors, channel_vectors, fi_b, fo_b, mi_b, mo_b):
    high, low_part = rotation_tables()
    vm = pl.BlockSpec(memory_space=pltpu.VMEM)
    hbm = pl.BlockSpec(memory_space=pl.ANY)

    def v(shape, dtype):
        return pltpu.VMEM(shape, dtype)

    t16 = (4 * ROWS, D)
    h16 = (4 * ROWS, 512)
    c16 = (4 * ROWS, 128)
    scratch = [v(group_shape(g, D), BF16) for g in range(6)]
    scratch += [v(t16, BF16)] * 6
    scratch += [v(h16, F32)] * 2 + [v(h16, BF16)] * 3
    scratch += [v(c16, BF16)] * 4 + [v((4 * ROWS, 384), BF16), v((4 * ROWS, ROWS), F32)]
    scratch += [v(c16, F32)] * 5 + [v(c16, BF16), v((4 * ROWS, 256), BF16)]
    scratch += [v(c16, F32)] * 4 + [v((4, 8, ROWS), F32)]
    scratch += [v((5, HALF, D), F32), v((5, HALF, 128), F32), v((HALF, D), F32)]
    scratch += [v((4, HALF, D), BF16)] * 2 + [v((HALF, D), BF16)] + [v((QUAD, D), BF16)] * 2
    scratch += [v((HALF, D), BF16)] * 4 + [v((4, HALF, D), F32), v((ROWS, D), F32)]
    scratch += [v((4,) + group_shape(g, ROWS), BF16) for g in range(6)]
    scratch += [v((3,) + group_shape(g, ROWS), BF16) for g in range(6)]
    scratch += [v(group_shape(g, ROWS), BF16) for g in range(6)]
    scratch += [v((2, 4, 8, 128), F32), v((4, 8, 128), F32)]
    scratch += [v((16, D), F32)] * 4 + [v((4, 16, D), F32), v((8, 128), F32), v((2, HALF, D), F32)]
    dma = pltpu.SemaphoreType.DMA
    sems = [(11,), (11,), (10,), (10,), (6, 4, 2), (6, 4, 2), (6, 4), (6, 4), (6, 4), (6, 4)]
    sems += [(6, 4, 2), (6, 4, 2), (3,), (3,), (3, 3), (3, 3), (6,), (6,), (3,), (3,), (2,), (2,), (8,)]
    scratch += [dma(k) for k in sems]
    out_shape = (
        jax.ShapeDtypeStruct((ROWS, D), F32),
        jax.ShapeDtypeStruct((ROWS, D), F32),
        jax.ShapeDtypeStruct((2, SHARD, 2048), BF16),
        jax.ShapeDtypeStruct((2, SHARD, 2048), BF16),
        jax.ShapeDtypeStruct((5, SHARD, 512), BF16),
        jax.ShapeDtypeStruct((2, SHARD, 512), BF16),
        jax.ShapeDtypeStruct((16, D), F32),
        jax.ShapeDtypeStruct((8, 512), F32),
    )
    return pl.pallas_call(
        fused_kernel,
        out_shape=out_shape,
        in_specs=[vm] * 7 + [hbm] * 4,
        out_specs=(hbm,) * 6 + (vm, vm),
        scratch_shapes=scratch,
        compiler_params=pltpu.CompilerParams(
            collective_id=0, has_side_effects=True, vmem_limit_bytes=63 * 2**20
        ),
    )(tok, cot, lens, jnp.asarray(high), jnp.asarray(low_part), norm_vectors, channel_vectors, fi_b, fo_b, mi_b, mo_b)


def fast_body(
    tokens_in, out_cotangent, utt_lengths,
    feed_in, feed_in_mean, feed_in_square,
    feed_out, feed_out_mean, feed_out_square,
    mixer_in, mixer_in_mean, mixer_in_square,
    mixer_out, mixer_out_mean, mixer_out_square,
    norm_vectors, norm_vectors_mean, norm_vectors_square,
    channel_vectors, channel_vectors_mean, channel_vectors_square,
):
    lens = jnp.broadcast_to(
        jnp.pad(utt_lengths[0].astype(F32), (0, 6))[:, None], (8, ROWS)
    )
    tokens_out, tokens_grad, gfi, gfo, gmi, gmo, ngrad, cgrad = fused_call(
        tokens_in,
        out_cotangent,
        lens,
        norm_vectors,
        channel_vectors,
        feed_in.astype(BF16),
        jnp.swapaxes(feed_out, 1, 2).astype(BF16),
        mixer_in.astype(BF16),
        jnp.swapaxes(mixer_out, 1, 2).astype(BF16),
    )
    rates = rate_table()

    def step(weight, mean_state, square_state, gradient, rate):
        return adamw_step(weight, mean_state, square_state, gradient.astype(F32), rate)

    fi = step(feed_in, feed_in_mean, feed_in_square, gfi, rates[0])
    fo = step(feed_out, feed_out_mean, feed_out_square, jnp.swapaxes(gfo, 1, 2), rates[1])
    mi = step(mixer_in, mixer_in_mean, mixer_in_square, gmi, rates[2])
    mo = step(mixer_out, mixer_out_mean, mixer_out_square, jnp.swapaxes(gmo, 1, 2), rates[3])
    nv = step(norm_vectors, norm_vectors_mean, norm_vectors_square, ngrad[:10], rates[4])
    cv = step(channel_vectors, channel_vectors_mean, channel_vectors_square, cgrad[:7], rates[5])
    return (tokens_out, tokens_grad) + fi + fo + mi[:2] + (mi[2][:4], mi[2][4]) + mo + nv + cv


def solution(mesh):
    fits = mesh.shape["dp"] == 16 and mesh.shape["mp"] == 2
    placed = (
        P("dp", None),
        P("dp", None),
        P("dp", None),
        P(None, "dp", "mp"),
        P(None, "dp", "mp"),
        P(None, "dp", "mp"),
        P(None, "mp", "dp"),
        P(None, "mp", "dp"),
        P(None, "mp", "dp"),
        P(None, "dp", "mp"),
        P(None, "dp", "mp"),
        P(None, "dp", "mp"),
        P(None, "mp", "dp"),
        P(None, "mp", "dp"),
        P(None, "mp", "dp"),
        P(),
        P(),
        P(),
        P(None, "mp"),
        P(None, "mp"),
        P(None, "mp"),
    )
    return jax.shard_map(
        fast_body if fits else body,
        mesh=mesh,
        in_specs=placed,
        out_specs=(
            P("dp", None),
            P("dp", None),
            P(None, "dp", "mp"),
            P(None, "dp", "mp"),
            P(None, "dp", "mp"),
            P(None, "mp", "dp"),
            P(None, "mp", "dp"),
            P(None, "mp", "dp"),
            P(None, "dp", "mp"),
            P(None, "dp", "mp"),
            P(None, "dp", "mp"),
            P("dp", "mp"),
            P(None, "mp", "dp"),
            P(None, "mp", "dp"),
            P(None, "mp", "dp"),
            P(),
            P(),
            P(),
            P(None, "mp"),
            P(None, "mp"),
            P(None, "mp"),
        ),
        check_vma=False,
    )
```

```python
import math

import jax
import jax.numpy as jnp
import numpy as np
from jax import lax
from jax.experimental import pallas as pl
from jax.experimental.pallas import tpu as pltpu
from jax.sharding import PartitionSpec as P

D = 1024
FF = 4096
HEAD_DIM = 128
KERNEL = 5
STEP_COUNT = 3
TOK_DEV = 256


EPS_NORM = 1e-05
EPS_ADAM = 1e-08
DECAY_WEIGHT = 0.01
BETA = 0.5
BIG_NEG = -1e30


def product(left_side, right_side):
    return jnp.dot(left_side, right_side, preferred_element_type=jnp.float32)


def weight_grad(inputs, gradients):
    return lax.dot_general(
        inputs, gradients, (((0,), (0,)), ((), ())), preferred_element_type=jnp.float32
    )


def input_grad(gradients, weight):
    return lax.dot_general(
        gradients, weight, (((1,), (1,)), ((), ())), preferred_element_type=jnp.float32
    )


def norm_forward(values, gain_row, shift_row):
    centre = values - jnp.mean(values, axis=-1, keepdims=True)
    inverse = lax.rsqrt(jnp.mean(centre * centre, axis=-1, keepdims=True) + EPS_NORM)
    scaled = centre * inverse
    return (scaled * gain_row + shift_row, scaled, inverse)


def norm_backward(grad_out, scaled, inverse, gain_row):
    grad_gain = jnp.sum(grad_out * scaled, axis=0)
    grad_shift = jnp.sum(grad_out, axis=0)
    grad_scaled = grad_out * gain_row
    grad_in = inverse * (
        grad_scaled
        - jnp.mean(grad_scaled, axis=-1, keepdims=True)
        - scaled * jnp.mean(grad_scaled * scaled, axis=-1, keepdims=True)
    )
    return (grad_in, grad_gain, grad_shift)


def rotate(values, cosine, sine_part):
    halfway = values.shape[-1] // 2
    front_half = values[..., :halfway]
    back_half = values[..., halfway:]
    return jnp.concatenate(
        [front_half * cosine - back_half * sine_part, front_half * sine_part + back_half * cosine],
        axis=-1,
    )


def unrotate(values, cosine, sine_part):
    halfway = values.shape[-1] // 2
    front_half = values[..., :halfway]
    back_half = values[..., halfway:]
    return jnp.concatenate(
        [front_half * cosine + back_half * sine_part, back_half * cosine - front_half * sine_part],
        axis=-1,
    )


def depthwise(gated_rows, kernel, group_ids):
    count_rows = gated_rows.shape[0]
    reach = KERNEL // 2
    padded = jnp.pad(gated_rows, ((reach, reach), (0, 0)))
    padded_ids = jnp.pad(group_ids, (reach, reach), constant_values=-1)
    summed = jnp.zeros_like(gated_rows)
    for offset in range(KERNEL):
        matched = (padded_ids[offset : offset + count_rows] == group_ids).astype(jnp.float32)
        summed = summed + kernel[offset] * padded[offset : offset + count_rows] * matched[:, None]
    return summed


def depthwise_back(grad_mixed, gated_rows, kernel, group_ids):
    count_rows = gated_rows.shape[0]
    reach = KERNEL // 2
    padded = jnp.pad(gated_rows, ((reach, reach), (0, 0)))
    padded_ids = jnp.pad(group_ids, (reach, reach), constant_values=-1)
    grad_padded = jnp.zeros_like(padded)
    kernel_rows = []
    for offset in range(KERNEL):
        matched = (padded_ids[offset : offset + count_rows] == group_ids).astype(jnp.float32)
        weighted = grad_mixed * matched[:, None]
        kernel_rows.append(jnp.sum(weighted * padded[offset : offset + count_rows], axis=0))
        grad_padded = grad_padded.at[offset : offset + count_rows].add(kernel[offset] * weighted)
    return (jnp.stack(kernel_rows), grad_padded[reach : reach + count_rows])


def rate_table():
    attention_fan = max(2 * D // TOK_DEV, 1)
    mixer_rates = jnp.array([attention_fan ** (-0.5), D ** (-0.5)], dtype=jnp.float32)[
        :, None, None
    ]
    return (D ** (-0.5), FF ** (-0.5), D ** (-0.5), mixer_rates, 0.3, 0.3)


def adamw_step(weight, mean_state, square_state, gradient, step_rate):
    mean_next = BETA * mean_state + (1.0 - BETA) * gradient
    square_next = BETA * square_state + (1.0 - BETA) * gradient * gradient
    correct = 1.0 - BETA**STEP_COUNT
    direction = mean_next / correct / (jnp.sqrt(square_next / correct) + EPS_ADAM)
    return (weight - step_rate * (direction + DECAY_WEIGHT * weight), mean_next, square_next)


def branch_total(partial_sum):
    return lax.psum(partial_sum.astype(jnp.bfloat16), "mp").astype(jnp.float32)


def input_total(partial_sum):
    return lax.psum(partial_sum.astype(jnp.bfloat16), "mp").astype(jnp.float32)


def body(
    tokens_in,
    out_cotangent,
    utt_lengths,
    feed_in,
    feed_in_mean,
    feed_in_square,
    feed_out,
    feed_out_mean,
    feed_out_square,
    mixer_in,
    mixer_in_mean,
    mixer_in_square,
    mixer_out,
    mixer_out_mean,
    mixer_out_square,
    norm_vectors,
    norm_vectors_mean,
    norm_vectors_square,
    channel_vectors,
    channel_vectors_mean,
    channel_vectors_square,
):
    count_rows = tokens_in.shape[0]
    local_width = mixer_in.shape[2]
    local_heads = local_width // HEAD_DIM
    heads_shape = (count_rows, local_heads, HEAD_DIM)
    score_scale = HEAD_DIM ** (-0.5)
    first_len = utt_lengths[0, 0]
    second = utt_lengths[0, 1]
    places = jnp.arange(count_rows, dtype=jnp.int32)
    in_first = (places < first_len).astype(jnp.int32)
    in_live = (places < first_len + second).astype(jnp.int32)
    group_ids = in_first + in_live
    positions = places - first_len * (1 - in_first) - second * (1 - in_live)
    live_rows = in_live.astype(jnp.float32)[:, None]
    halfway = HEAD_DIM // 2
    frequency = jnp.exp(
        jnp.arange(halfway, dtype=jnp.float32) * (-2.0 * math.log(10000.0) / HEAD_DIM)
    )
    angles = positions.astype(jnp.float32)[:, None] * frequency[None, :]
    cosine = jnp.cos(angles)[:, None, :]
    sine_part = jnp.sin(angles)[:, None, :]
    allowed = (group_ids[:, None] == group_ids[None, :])[None]
    kernel = channel_vectors[:KERNEL]
    batch_gain = channel_vectors[KERNEL]
    batch_shift = channel_vectors[KERNEL + 1]
    weight_in, weight_out, weight_mix, weight_back = (
        lax.all_gather(feed_in.astype(jnp.bfloat16), "dp", axis=1, tiled=True),
        lax.all_gather(feed_out.astype(jnp.bfloat16), "dp", axis=2, tiled=True),
        lax.all_gather(mixer_in.astype(jnp.bfloat16), "dp", axis=1, tiled=True),
        lax.all_gather(mixer_out.astype(jnp.bfloat16), "dp", axis=2, tiled=True),
    )

    def feed_forward(residual, norm_slot, feed_layer):
        normed, scaled, inverse = norm_forward(
            residual, norm_vectors[norm_slot], norm_vectors[5 + norm_slot]
        )
        normed_low = normed.astype(jnp.bfloat16)
        hidden = product(normed_low, weight_in[feed_layer])
        active = (hidden * jax.nn.sigmoid(hidden)).astype(jnp.bfloat16)
        branch = branch_total(product(active, weight_out[feed_layer]))
        return (residual + 0.5 * branch, (scaled, inverse, normed_low, hidden, active))

    section_zero = tokens_in.astype(jnp.float32)
    section_one, kept_first = feed_forward(section_zero, 0, 0)
    normed, scaled_att, inverse_att = norm_forward(section_one, norm_vectors[1], norm_vectors[6])
    normed_att = normed.astype(jnp.bfloat16)
    projected = jnp.einsum(
        "td,sdc->stc", normed_att, weight_mix[:3], preferred_element_type=jnp.float32
    )
    queries = (rotate(projected[0].reshape(heads_shape), cosine, sine_part) * score_scale).astype(
        jnp.bfloat16
    )
    key_rows = rotate(projected[1].reshape(heads_shape), cosine, sine_part).astype(jnp.bfloat16)
    value_rows = projected[2].reshape(heads_shape).astype(jnp.bfloat16)
    scores = jnp.where(
        allowed,
        jnp.einsum("qhd,khd->hqk", queries, key_rows, preferred_element_type=jnp.float32),
        BIG_NEG,
    )
    largest = jnp.max(scores, axis=-1, keepdims=True)
    exponent = jnp.exp(scores - largest)
    totals = jnp.sum(exponent, axis=-1, keepdims=True)
    softmax_rows = exponent / totals
    log_total = largest + jnp.log(totals)
    context = jnp.einsum(
        "hqk,khd->qhd",
        softmax_rows.astype(jnp.bfloat16),
        value_rows,
        preferred_element_type=jnp.float32,
    )
    context_low = context.reshape(count_rows, local_width).astype(jnp.bfloat16)
    section_two = section_one + branch_total(product(context_low, weight_back[0]))
    normed, scaled_conv, inverse_conv = norm_forward(section_two, norm_vectors[2], norm_vectors[7])
    normed_conv = normed.astype(jnp.bfloat16)
    conv_proj = jnp.einsum(
        "td,sdc->stc", normed_conv, weight_mix[3:], preferred_element_type=jnp.float32
    )
    gate_sig = jax.nn.sigmoid(conv_proj[1])
    gated_rows = conv_proj[0] * gate_sig
    mixed_rows = depthwise(gated_rows, kernel, group_ids)
    batch_stats = lax.psum(
        (
            jnp.sum(live_rows * mixed_rows, axis=0),
            jnp.sum(live_rows * mixed_rows * mixed_rows, axis=0),
            jnp.sum(live_rows),
        ),
        "dp",
    )
    count_live = batch_stats[2]
    mean_batch = batch_stats[0] / count_live
    inverse_batch = lax.rsqrt(batch_stats[1] / count_live - mean_batch * mean_batch + EPS_NORM)
    centred = mixed_rows - mean_batch
    batch_out = centred * inverse_batch * batch_gain + batch_shift
    batch_sig = jax.nn.sigmoid(batch_out)
    active_conv = (batch_out * batch_sig).astype(jnp.bfloat16)
    section_three = section_two + branch_total(product(active_conv, weight_back[1]))
    section_four, kept_second = feed_forward(section_three, 3, 1)
    tokens_out, scaled_last, inverse_last = norm_forward(
        section_four, norm_vectors[4], norm_vectors[9]
    )

    def feed_backward(grad_residual, kept, norm_slot, feed_layer):
        scaled, inverse, normed_low, hidden, active = kept
        grad_branch = (0.5 * grad_residual).astype(jnp.bfloat16)
        grad_down = weight_grad(active, grad_branch)
        hidden_sig = jax.nn.sigmoid(hidden)
        grad_hidden = (
            input_grad(grad_branch, weight_out[feed_layer])
            * hidden_sig
            * (1.0 + hidden * (1.0 - hidden_sig))
        ).astype(jnp.bfloat16)
        grad_up = weight_grad(normed_low, grad_hidden)
        grad_normed = input_total(input_grad(grad_hidden, weight_in[feed_layer]))
        grad_in, grad_gain, grad_shift = norm_backward(
            grad_normed, scaled, inverse, norm_vectors[norm_slot]
        )
        return (grad_residual + grad_in, grad_up, grad_down, grad_gain, grad_shift)

    grad_residual, gain_last, shift_last = norm_backward(
        out_cotangent.astype(jnp.float32), scaled_last, inverse_last, norm_vectors[4]
    )
    grad_residual, up_second, down_second, gain_three, shift_three = feed_backward(
        grad_residual, kept_second, 3, 1
    )
    grad_branch = grad_residual.astype(jnp.bfloat16)
    grad_conv_down = weight_grad(active_conv, grad_branch)
    grad_batch = (
        input_grad(grad_branch, weight_back[1]) * batch_sig * (1.0 + batch_out * (1.0 - batch_sig))
    )
    batch_sums = lax.psum(
        (jnp.sum(grad_batch, axis=0), jnp.sum(grad_batch * centred, axis=0)), "dp"
    )
    grad_var = -0.5 * inverse_batch**3 * batch_gain * batch_sums[1]
    grad_mean = -inverse_batch * batch_gain * batch_sums[0] - 2.0 * mean_batch * grad_var
    grad_mixed = (
        grad_batch * batch_gain * inverse_batch
        + live_rows * (grad_mean + 2.0 * mixed_rows * grad_var) / count_live
    )
    kernel_grads, grad_gated = depthwise_back(grad_mixed, gated_rows, kernel, group_ids)
    grad_conv_up = jnp.stack(
        [grad_gated * gate_sig, grad_gated * conv_proj[0] * gate_sig * (1.0 - gate_sig)]
    ).astype(jnp.bfloat16)
    grad_conv_in = jnp.einsum(
        "td,stc->sdc", normed_conv, grad_conv_up, preferred_element_type=jnp.float32
    )
    grad_normed = input_total(
        jnp.einsum("stc,sdc->td", grad_conv_up, weight_mix[3:], preferred_element_type=jnp.float32)
    )
    grad_in, gain_two, shift_two = norm_backward(
        grad_normed, scaled_conv, inverse_conv, norm_vectors[2]
    )
    grad_residual = grad_residual + grad_in
    grad_branch = grad_residual.astype(jnp.bfloat16)
    grad_att_down = weight_grad(context_low, grad_branch)
    grad_context = input_grad(grad_branch, weight_back[0]).astype(jnp.bfloat16).reshape(heads_shape)
    scores_again = jnp.where(
        allowed,
        jnp.einsum("qhd,khd->hqk", queries, key_rows, preferred_element_type=jnp.float32),
        BIG_NEG,
    )
    softmax_again = jnp.exp(scores_again - log_total)
    grad_softmax = jnp.einsum(
        "qhd,khd->hqk", grad_context, value_rows, preferred_element_type=jnp.float32
    )
    grad_values = jnp.einsum(
        "hqk,qhd->khd",
        softmax_again.astype(jnp.bfloat16),
        grad_context,
        preferred_element_type=jnp.float32,
    )
    grad_scores = (
        softmax_again
        * (grad_softmax - jnp.sum(softmax_again * grad_softmax, axis=-1, keepdims=True))
    ).astype(jnp.bfloat16)
    grad_queries = unrotate(
        jnp.einsum("hqk,khd->qhd", grad_scores, key_rows, preferred_element_type=jnp.float32)
        * score_scale,
        cosine,
        sine_part,
    )
    grad_keys = unrotate(
        jnp.einsum("hqk,qhd->khd", grad_scores, queries, preferred_element_type=jnp.float32),
        cosine,
        sine_part,
    )
    grad_att_up = (
        jnp.stack([grad_queries, grad_keys, grad_values])
        .reshape(3, count_rows, local_width)
        .astype(jnp.bfloat16)
    )
    grad_att_in = jnp.einsum(
        "td,stc->sdc", normed_att, grad_att_up, preferred_element_type=jnp.float32
    )
    grad_normed = input_total(
        jnp.einsum("stc,sdc->td", grad_att_up, weight_mix[:3], preferred_element_type=jnp.float32)
    )
    grad_in, gain_one, shift_one = norm_backward(
        grad_normed, scaled_att, inverse_att, norm_vectors[1]
    )
    grad_residual = grad_residual + grad_in
    grad_residual, up_first, down_first, gain_zero, shift_zero = feed_backward(
        grad_residual, kept_first, 0, 0
    )
    feed_in_grad, feed_out_grad, mixer_in_grad, mixer_out_grad = (
        lax.psum_scatter(jnp.stack([up_first, up_second]), "dp", scatter_dimension=1, tiled=True),
        lax.psum_scatter(
            jnp.stack([down_first, down_second]), "dp", scatter_dimension=2, tiled=True
        ),
        lax.psum_scatter(
            jnp.concatenate([grad_att_in, grad_conv_in], axis=0),
            "dp",
            scatter_dimension=1,
            tiled=True,
        ),
        lax.psum_scatter(
            jnp.stack([grad_att_down, grad_conv_down]), "dp", scatter_dimension=2, tiled=True
        ),
    )
    norm_grads = jnp.stack(
        [
            gain_zero,
            gain_one,
            gain_two,
            gain_three,
            gain_last,
            shift_zero,
            shift_one,
            shift_two,
            shift_three,
            shift_last,
        ]
    )
    norm_total, kernel_total = lax.psum((norm_grads, kernel_grads), "dp")
    channel_grads = jnp.concatenate(
        [kernel_total, (inverse_batch * batch_sums[1])[None], batch_sums[0][None]], axis=0
    )
    rate_list = rate_table()
    feed_in_next, feed_in_mean_next, feed_in_square_next = adamw_step(
        feed_in, feed_in_mean, feed_in_square, feed_in_grad, rate_list[0]
    )
    feed_out_next, feed_out_mean_next, feed_out_square_next = adamw_step(
        feed_out, feed_out_mean, feed_out_square, feed_out_grad, rate_list[1]
    )
    mixer_in_next, mixer_in_mean_next, mixer_in_square_next = adamw_step(
        mixer_in, mixer_in_mean, mixer_in_square, mixer_in_grad, rate_list[2]
    )
    mixer_out_next, mixer_out_mean_next, mixer_out_square_next = adamw_step(
        mixer_out, mixer_out_mean, mixer_out_square, mixer_out_grad, rate_list[3]
    )
    norm_vectors_next, norm_vectors_mean_next, norm_vectors_square_next = adamw_step(
        norm_vectors, norm_vectors_mean, norm_vectors_square, norm_total, rate_list[4]
    )
    channel_vectors_next, channel_vectors_mean_next, channel_vectors_square_next = adamw_step(
        channel_vectors, channel_vectors_mean, channel_vectors_square, channel_grads, rate_list[5]
    )
    return (
        tokens_out,
        grad_residual,
        feed_in_next,
        feed_in_mean_next,
        feed_in_square_next,
        feed_out_next,
        feed_out_mean_next,
        feed_out_square_next,
        mixer_in_next,
        mixer_in_mean_next,
        mixer_in_square_next[:4],
        mixer_in_square_next[4],
        mixer_out_next,
        mixer_out_mean_next,
        mixer_out_square_next,
        norm_vectors_next,
        norm_vectors_mean_next,
        norm_vectors_square_next,
        channel_vectors_next,
        channel_vectors_mean_next,
        channel_vectors_square_next,
    )


MESH = pl.DeviceIdType.MESH
F32 = jnp.float32
BF16 = jnp.bfloat16
ROWS = 256
HALF = 128
QUAD = 64
OCT = 32
SHARD = 64
G_IN0, G_OUT0, G_ATT, G_CONV, G_IN1, G_OUT1 = range(6)


def dot_nn(a, b):
    return lax.dot_general(a, b, (((1,), (0,)), ((), ())), preferred_element_type=F32)


def dot_nt(a, b):
    return lax.dot_general(a, b, (((1,), (1,)), ((), ())), preferred_element_type=F32)


def dot_tn(a, b):
    return lax.dot_general(a, b, (((0,), (0,)), ((), ())), preferred_element_type=F32)


def sigm(v):
    return 1.0 / (1.0 + jnp.exp(-v))


def fused_kernel(
    tok, cot, lens, rot_hi, rot_lo, nv, cv, fi_b, fo_b, mi_b, mo_b,
    tout, tgrad, gfi, gfo, gmi, gmo, ngrad, cgrad,
    w0, w1, w2, w3, w4, w5, xg0, xg1, xg2, xg3, xb0, xb1,
    fh0, fh1, fs0, fs1, hb, qr, kr, vr, ctx, dqkv, pf,
    cu, sg, glu, zc, dd, cw, du, gid, live, rc_t, rs_t, lb,
    xh, inv, res, so, si, sd, hx, hy, sx, sy, rx, ry, keep, part,
    gs0, gs1, gs2, gs3, gs4, gs5, gi0, gi1, gi2, gi3, gi4, gi5,
    ac0, ac1, ac2, ac3, ac4, ac5, stats, tapm, ngm, nsib, nx, ny, nz, cgm, tstage, cotb,
    ags, agr, rss, rsr, was, war, zs, zr, grs, grr, gas, gar, lss, lsr,
    bns, bnr, nss, nsr, cgs, cgr, outs, outr, cts, ctr,
):
    w = (w0, w1, w2, w3, w4, w5)
    gst = (gs0, gs1, gs2, gs3, gs4, gs5)
    gin = (gi0, gi1, gi2, gi3, gi4, gi5)
    acc = (ac0, ac1, ac2, ac3, ac4, ac5)
    dp = lax.axis_index("dp")
    m = lax.axis_index("mp")
    x = dp % 2
    y = (dp // 2) % 2
    z = dp // 4
    p = dp % 4
    base = z * 4
    px = p + 1 - 2 * x
    py = p + 2 - 4 * y
    pd = 3 - p
    sib = (dp, 1 - m)
    xn = (base + px, m)
    yn = (base + py, m)
    dn = (base + pd, m)
    plane = ((px, xn), (py, yn), (pd, dn))
    inner = (z + 1) // 2 % 2
    others = tuple((z + k) % 4 for k in (1, 2, 3))

    def zdev(zz):
        return (zz * 4 + p, m)

    def remote(src, dst, ssem, rsem, dev):
        return pltpu.make_async_remote_copy(
            src_ref=src, dst_ref=dst, send_sem=ssem, recv_sem=rsem, device_id=dev, device_id_type=MESH
        )

    def rows(start, size):
        return pl.ds(pl.multiple_of(start, size), size)

    def block(b):
        return rows(b * ROWS, ROWS)

    pending = []

    def go_send(copy):
        copy.start()
        pending.append(copy)

    barrier = pltpu.get_barrier_semaphore()
    greet = (sib, xn, yn, dn) + tuple(zdev(k) for k in others)
    greet += tuple((base + k, 1 - m) for k in (px, py, pd))
    for dev in greet:
        pl.semaphore_signal(barrier, inc=1, device_id=dev, device_id_type=MESH)
    pl.semaphore_wait(barrier, len(greet))

    def wview(g, start, size):
        r = pl.ds(pl.multiple_of(start, SHARD), size)
        return w[g].at[:, r] if g in (G_ATT, G_CONV) else w[g].at[r]

    def columns(i, wd):
        return pl.ds(pl.multiple_of(i * wd, 128), wd)

    def wpieces(g, peer, owner):
        r = pl.ds(pl.multiple_of(z * ROWS + owner * SHARD, SHARD), SHARD)
        if g == G_ATT:
            return (
                (mi_b.at[0:3, :, columns(peer, 128)], w[g].at[0:3, r]),
                (mo_b.at[0, :, columns(peer, 128)], w[g].at[3, r]),
            )
        if g == G_CONV:
            return (
                (mi_b.at[3:5, :, columns(peer, 128)], w[g].at[0:2, r]),
                (mo_b.at[1, :, columns(peer, 128)], w[g].at[2, r]),
            )
        src = fi_b if g in (G_IN0, G_IN1) else fo_b
        layer = 0 if g in (G_IN0, G_OUT0) else 1
        return ((src.at[layer, :, columns(peer, 512)], w[g].at[r]),)

    def plane_start(g):
        for r, (peer, dev) in enumerate(plane):
            for k, (src, dst) in enumerate(wpieces(g, peer, p)):
                go_send(remote(src, dst, was.at[g, r, k], war.at[g, r, k], dev))
        for k, (src, dst) in enumerate(wpieces(g, p, p)):
            pltpu.make_async_copy(src, dst, was.at[g, 3, k]).start()

    def plane_wait(g):
        for r, (peer, dev) in enumerate(plane):
            for k, (_, dst) in enumerate(wpieces(g, peer, peer)):
                remote(dst, dst, was.at[g, r, k], war.at[g, r, k], dev).wait_recv()
        for k, (src, dst) in enumerate(wpieces(g, p, p)):
            pltpu.make_async_copy(src, dst, was.at[g, 3, k]).wait()

    targets = {0: (2, 1), 1: (3, 0, 2), 2: (0, 3, 1), 3: (1, 2)}
    far = {1: (3, 0), 2: (0, 3)}

    def zcopy(g, owner, k, to):
        part_w = wview(g, owner * ROWS, ROWS)
        return remote(part_w, part_w, zs.at[g, k], zr.at[g, owner], zdev(to))

    def line_start(g):
        plane_wait(g)
        for zz, tos in targets.items():

            @pl.when(z == zz)
            def _():
                for k, to in enumerate(tos):
                    zcopy(g, zz, k, to).start()

    def line_pass(g):
        for zz, (owner, to) in far.items():

            @pl.when(z == zz)
            def _():
                zcopy(g, owner, 3, to).wait_recv()
                zcopy(g, owner, 3, to).start()

    def line_ready(g):
        for zz in range(4):

            @pl.when(z == zz)
            def _():
                for owner in range(4):
                    if owner != zz and (zz not in far or far[zz][0] != owner):
                        zcopy(g, owner, 0, zz).wait_recv()

    def line_done(g):
        for zz, tos in targets.items():

            @pl.when(z == zz)
            def _():
                for k, to in enumerate(tos):
                    zcopy(g, zz, k, to).wait_send()
                if zz in far:
                    zcopy(g, far[zz][0], 3, far[zz][1]).wait_send()

    def pieces(s):
        return lambda b, c, off, size: pl.ds(
            pl.multiple_of(s * 2 * ROWS + b * HALF + c * QUAD + off, OCT), size
        )

    def blocks_of_chips(b, c, off, size):
        return pl.ds(pl.multiple_of(place_of(b) * ROWS + c * HALF + off, QUAD), size)

    def place_of(b):
        return b % 2 * 2 + b // 2

    def mine(s):
        return pieces(s)(p, m, 0, QUAD)

    def settle(sends):
        for k in sends:
            k.wait_send()
        sends.clear()

    def gather(xg, where, half, sem, near, far_piece, name, sends):
        quad = half // 2

        def c(i, b, core, off, size, dev):
            r = xg.at[where(b, core, off, size)]
            return remote(r, r, ags.at[sem, i], agr.at[sem, i], dev)

        def start(*a):
            k = c(*a)
            k.start()
            sends.append(k)

        n = 1 - m
        settle(sends)
        start(0, p, m, 0, half, sib)
        start(1, p, m, 0, quad, xn)
        start(3, p, m, quad, quad, yn)
        start(2, p, m, quad, quad, xn)
        start(4, p, m, 0, quad, yn)
        yield name + ".0"
        c(1, px, m, 0, quad, xn).wait_recv()
        start(5, px, m, 0, quad, yn)
        c(3, py, m, quad, quad, yn).wait_recv()
        start(6, py, m, quad, quad, xn)
        yield name + ".1"
        c(2, px, m, quad, quad, xn).wait_recv()
        start(7, px, m, 0, half, sib)
        c(4, py, m, 0, quad, yn).wait_recv()
        start(8, py, m, 0, half, sib)
        c(0, p, n, 0, half, sib).wait_recv()
        c(7, px, n, 0, half, sib).wait_recv()
        near()
        yield name + ".2"
        c(5, pd, m, 0, quad, yn).wait_recv()
        start(9, pd, m, 0, quad, sib)
        c(6, pd, m, quad, quad, xn).wait_recv()
        start(10, pd, m, quad, quad, sib)
        yield name + ".3"
        c(8, py, n, 0, half, sib).wait_recv()
        c(9, pd, n, 0, quad, sib).wait_recv()
        c(10, pd, n, quad, quad, sib).wait_recv()
        far_piece()

    def scatter(s, compute, name, sends):
        def csib(i):
            return remote(so.at[s, i], si.at[s, i], rss.at[s, i], rsr.at[s, i], sib)

        def start(k):
            k.start()
            sends.append(k)

        def term(i, chip_x):
            give = pl.ds(pl.multiple_of(chip_x * HALF + (1 - m) * QUAD, QUAD), QUAD)
            hold = pl.ds(pl.multiple_of(chip_x * HALF + m * QUAD, QUAD), QUAD)
            so[s, i] = part[give, :].astype(BF16)
            start(csib(i))
            keep[s, i] = part[hold, :]

        a = slice(0, OCT)
        bb = slice(OCT, QUAD)
        chx = remote(sd.at[s, a], hx.at[s], rss.at[s, 4], rsr.at[s, 4], xn)
        chy = remote(sd.at[s, bb], hy.at[s], rss.at[s, 5], rsr.at[s, 5], yn)
        cxa = remote(sx.at[s, a], rx.at[s, a], rss.at[s, 6], rsr.at[s, 6], xn)
        cxb = remote(sx.at[s, bb], rx.at[s, bb], rss.at[s, 7], rsr.at[s, 7], xn)
        cyb = remote(sy.at[s, bb], ry.at[s, bb], rss.at[s, 8], rsr.at[s, 8], yn)
        cya = remote(sy.at[s, a], ry.at[s, a], rss.at[s, 9], rsr.at[s, 9], yn)
        settle(sends)
        compute(1 - y)
        term(0, 1 - x)
        term(2, x)
        compute(y)
        term(1, 1 - x)
        term(3, x)
        yield name + ".0"
        csib(0).wait_recv()
        sd[s] = (keep[s, 0] + si[s, 0].astype(F32)).astype(BF16)
        start(chx)
        start(chy)
        csib(1).wait_recv()
        sx[s, a, :] = (keep[s, 1, a, :] + si[s, 1, a, :].astype(F32)).astype(BF16)
        start(cxa)
        csib(2).wait_recv()
        sy[s, bb, :] = (keep[s, 2, bb, :] + si[s, 2, bb, :].astype(F32)).astype(BF16)
        start(cyb)
        yield name + ".1"
        chy.wait_recv()
        sx[s, bb, :] = (
            keep[s, 1, bb, :] + si[s, 1, bb, :].astype(F32) + hy[s].astype(F32)
        ).astype(BF16)
        start(cxb)
        chx.wait_recv()
        sy[s, a, :] = (
            keep[s, 2, a, :] + si[s, 2, a, :].astype(F32) + hx[s].astype(F32)
        ).astype(BF16)
        start(cya)
        yield name + ".2"
        csib(3).wait_recv()
        cxa.wait_recv()
        cyb.wait_recv()
        cxb.wait_recv()
        cya.wait_recv()
        return keep[s, 3] + si[s, 3].astype(F32) + rx[s].astype(F32) + ry[s].astype(F32)

    def hats(v):
        centre = v - jnp.mean(v, axis=-1, keepdims=True)
        scale = lax.rsqrt(jnp.mean(centre * centre, axis=-1, keepdims=True) + EPS_NORM)
        return centre * scale, scale

    def norm(v, i, s):
        hat, scale = hats(v)
        xh[i, s] = hat
        inv[i, s] = jnp.broadcast_to(scale, (QUAD, 128))
        return hat * nv[i : i + 1, :] + nv[5 + i : 6 + i, :]

    def norm_back(g, i, s):
        hat = xh[i, s]
        scale = inv[i, s, :, 0:1]
        gains = jnp.sum(g * hat, axis=0, keepdims=True)
        shifts = jnp.sum(g, axis=0, keepdims=True)
        if s == 0:
            ngm[i : i + 1, :] = gains
            ngm[5 + i : 6 + i, :] = shifts
        else:
            ngm[i : i + 1, :] = ngm[i : i + 1, :] + gains
            ngm[5 + i : 6 + i, :] = ngm[5 + i : 6 + i, :] + shifts
        e = g * nv[i : i + 1, :]
        return scale * (
            e
            - jnp.mean(e, axis=-1, keepdims=True)
            - hat * jnp.mean(e * hat, axis=-1, keepdims=True)
        )

    outer = 1 - inner
    c0 = 3 * (1 - z // 2)
    c1 = 2 - z // 2
    c2 = z + 1 - 2 * (z % 2)
    order = (c0, c1, c2, z)

    def grad_chunk(g, k):
        zz = order[k]
        cols = pl.ds(pl.multiple_of(zz * ROWS, ROWS), ROWS)
        if g == G_IN0:
            v = dot_tn(xg0[:, cols], hb[...])
        elif g == G_OUT0:
            v = dot_tn(xb1[:, cols], fs0[...])
        elif g == G_IN1:
            v = dot_tn(xg3[:, cols], hb[...])
        elif g == G_OUT1:
            v = dot_tn(xb0[:, cols], fs1[...])
        if g == G_ATT:
            v = dot_tn(xg1[:, cols], dqkv[...]).astype(BF16)
            for k in range(3):
                gst[g][zz, k] = v[:, k * 128 : (k + 1) * 128]
            gst[g][zz, 3] = dot_tn(xb0[:, cols], ctx[...]).astype(BF16)
        elif g == G_CONV:
            v = dot_tn(xg2[:, cols], du[...]).astype(BF16)
            for k in range(2):
                gst[g][zz, k] = v[:, k * 128 : (k + 1) * 128]
            gst[g][zz, 2] = dot_tn(xb1[:, cols], cw[...]).astype(BF16)
        else:
            gst[g][zz] = v.astype(BF16)

    neighbour = 1 + z // 2

    def acc_copy(g):
        return remote(gst[g].at[c0], acc[g], grs.at[g, 0], grr.at[g, 3], zdev(neighbour))

    def slot_copy(g, k):
        zz = order[k]
        if k == 0:
            slot = 1
        elif k == 1:
            slot = 1 + outer
        else:
            slot = 0
        return remote(gst[g].at[zz], gin[g].at[slot], grs.at[g, k], grr.at[g, slot], zdev(zz))

    def grad_send(g, k):
        if k == 0:

            @pl.when(outer == 1)
            def _():
                acc_copy(g).start()
        elif k < 3:
            slot_copy(g, k).start()

    def grad_acc(g):
        @pl.when(inner == 1)
        def _():
            acc_copy(g).wait_recv()
            gst[g][c0] = (gst[g][c0].astype(F32) + acc[g][...].astype(F32)).astype(BF16)
            slot_copy(g, 0).start()

    def gpieces(g, peer, owner):
        r = pl.ds(pl.multiple_of(peer * SHARD, SHARD), SHARD)
        if g == G_ATT:
            return (
                (gst[g].at[z, 0:3, r], gmi.at[0:3, :, columns(owner, 128)]),
                (gst[g].at[z, 3, r], gmo.at[0, :, columns(owner, 128)]),
            )
        if g == G_CONV:
            return (
                (gst[g].at[z, 0:2, r], gmi.at[3:5, :, columns(owner, 128)]),
                (gst[g].at[z, 2, r], gmo.at[1, :, columns(owner, 128)]),
            )
        dst = gfi if g in (G_IN0, G_IN1) else gfo
        layer = 0 if g in (G_IN0, G_OUT0) else 1
        return ((gst[g].at[z, r], dst.at[layer, :, columns(owner, 512)]),)

    def gplane(g):
        return [
            remote(src, dst, gas.at[g, r, k], gar.at[g, r, k], dev)
            for r, (peer, dev) in enumerate(plane)
            for k, (src, dst) in enumerate(gpieces(g, peer, p))
        ] + [
            pltpu.make_async_copy(src, dst, gas.at[g, 3, k])
            for k, (src, dst) in enumerate(gpieces(g, p, p))
        ]

    def slot_wait(g, slot):
        remote(gin[g].at[slot], gin[g].at[slot], grs.at[g, 1], grr.at[g, slot], sib).wait_recv()

    def grad_final(g):
        slot_wait(g, 0)
        slot_wait(g, 1)
        t = gst[g][z].astype(F32) + gin[g][0].astype(F32) + gin[g][1].astype(F32)
        keep_t = t

        @pl.when(outer == 1)
        def _():
            gst[g][z] = keep_t.astype(BF16)

        @pl.when(inner == 1)
        def _():
            slot_wait(g, 2)
            gst[g][z] = (keep_t + gin[g][2].astype(F32)).astype(BF16)

        for copy in gplane(g):
            copy.start()

    def grad_done(g):
        for r, (peer, dev) in enumerate(plane):
            for k, (_, dst) in enumerate(gpieces(g, peer, peer)):
                remote(dst, dst, gas.at[g, r, k], gar.at[g, r, k], dev).wait_recv()
        for i, copy in enumerate(gplane(g)):
            if i < 3 * len(gpieces(g, p, p)):
                copy.wait_send()
            else:
                copy.wait()

        @pl.when(outer == 1)
        def _():
            acc_copy(g).wait_send()

        @pl.when(inner == 1)
        def _():
            slot_copy(g, 0).wait_send()

        slot_copy(g, 1).wait_send()
        slot_copy(g, 2).wait_send()

    def line_share(buf, sem_s, sem_r, start):
        for k in range(3):
            to = others[k]
            if start:
                remote(buf.at[z], buf.at[z], sem_s.at[k], sem_r.at[2 - k], zdev(to)).start()
            else:
                frm = others[2 - k]
                remote(buf.at[z], buf.at[z], sem_s.at[k], sem_r.at[2 - k], zdev(to)).wait_send()
                remote(buf.at[frm], buf.at[frm], sem_s.at[k], sem_r.at[2 - k], zdev(frm)).wait_recv()

    stats[...] = jnp.zeros_like(stats)
    tapm[...] = jnp.zeros_like(tapm)
    ngm[10:16, :] = jnp.zeros((6, D), F32)
    lb[p] = lens[...]
    plane_start(G_IN0)
    for r in range(3):
        peer, dev = plane[r]
        remote(lb.at[p], lb.at[p], lss.at[r], lsr.at[r], dev).start()
    xg0[blocks_of_chips(p, m, 0, HALF), :] = tok[
        pl.ds(pl.multiple_of(m * HALF, HALF), HALF), :
    ]

    def nothing():
        return None

    def either(here, a, b):
        @pl.when(here)
        def _():
            a()

        @pl.when(jnp.logical_not(here))
        def _():
            b()

    def cot_rows(owner_x):
        return cot.at[pl.ds(pl.multiple_of(owner_x * HALF + m * QUAD, QUAD), QUAD)]

    def cot_away():
        return remote(cot_rows(1 - x), cotb.at[x], cts.at[0], ctr.at[0], xn)

    def cot_local():
        return pltpu.make_async_copy(cot_rows(x), cotb.at[x], ctr.at[1])

    def cot_start():
        cot_away().start()
        cot_local().start()

    def cot_wait():
        cot_away().wait_send()
        remote(cotb.at[1 - x], cotb.at[1 - x], cts.at[0], ctr.at[0], xn).wait_recv()
        cot_local().wait()

    def tables():
        for r in range(3):
            peer, dev = plane[r]
            remote(lb.at[p], lb.at[p], lss.at[r], lsr.at[r], dev).wait_send()
            remote(lb.at[peer], lb.at[peer], lss.at[r], lsr.at[r], dev).wait_recv()
        place = lax.broadcasted_iota(jnp.int32, (ROWS, ROWS), 0).astype(F32)
        lane = lax.broadcasted_iota(jnp.int32, (ROWS, ROWS), 1).astype(F32)
        for b in range(4):
            l0 = lb[b % 2 * 2 + b // 2, 0:1, :]
            l1 = lb[b % 2 * 2 + b // 2, 1:2, :]
            first_in = jnp.where(place < l0, 1.0, 0.0)
            live_in = jnp.where(place < l0 + l1, 1.0, 0.0)
            at = place - l0 * (1.0 - first_in) - l1 * (1.0 - live_in)
            r = slice(b * ROWS, (b + 1) * ROWS)
            gid[r, :] = 3.0 * b + first_in[:, :128] + live_in[:, :128]
            live[r, :] = live_in[:, :128]
            hot = jnp.where(at == lane, 1.0, 0.0).astype(BF16)
            t = dot_nn(hot, rot_hi[...]) + dot_nn(hot, rot_lo[...])
            rc_t[r, :] = t[:, :128]
            rs_t[r, :] = t[:, 128:]

    first_sends = []
    opening = gather(xg0, blocks_of_chips, HALF, 2, nothing, nothing, "G0", first_sends)
    next(opening)
    line_start(G_IN0)
    next(opening)
    plane_start(G_OUT0)
    next(opening)
    tables()
    next(opening)
    line_pass(G_IN0)
    line_start(G_OUT0)
    for _ in opening:
        pass
    settle(first_sends)
    for g in (G_ATT, G_CONV, G_IN1, G_OUT1):
        plane_start(g)
    cot_start()
    for s in range(2):
        first = xg0[mine(s), :].astype(F32)
        res[s] = first
        norm(first, 0, s)

    @pl.loop(0, 8)
    def _(i):
        r = rows(i * HALF, HALF)
        hat, _ = hats(xg0[r, :].astype(F32))
        xg0[r, :] = (hat * nv[0:1, :] + nv[5:6, :]).astype(BF16)

    def block_rows(s, q):
        return pl.ds(pl.multiple_of((2 * s + q) * ROWS, ROWS), ROWS)

    def ff_hidden(s, xg, g, fh, fs):
        def f(q):
            r = block_rows(s, q)
            h = dot_nn(xg[r, :], w[g][...])
            fh[r, :] = h
            fs[r, :] = (h * sigm(h)).astype(BF16)

        return f

    def wide(g, first, last):
        return jnp.concatenate([w[g][k] for k in range(first, last)], axis=1)

    def part_nt(s, lhs, weight):
        def f(q):
            part[...] = dot_nt(lhs[block_rows(s, q), :], weight())

        return f

    def whole(g):
        return lambda: w[g][...]

    def turn(v, r):
        return v * rc_t[r, :] + pltpu.roll(v, 64, 1) * rs_t[r, :]

    def turn_back(v, r):
        return v * rc_t[r, :] - pltpu.roll(v, 64, 1) * rs_t[r, :]

    lane_row = lax.broadcasted_iota(jnp.int32, (1, ROWS), 1).astype(F32)

    def attend(s):
        def f(q):
            r = block_rows(s, q)
            b = 2 * q + s
            t = dot_nn(xg1[r, :], wide(G_ATT, 0, 3))
            qs = (turn(t[:, 0:128], r) * (HEAD_DIM**-0.5)).astype(BF16)
            k = turn(t[:, 128:256], r).astype(BF16)
            v = t[:, 256:384].astype(BF16)
            qr[r, :] = qs
            kr[r, :] = k
            vr[r, :] = v
            sc = dot_nt(qs, k)
            l0 = lb[b, 0:1, :]
            l1 = lb[b, 1:2, :]
            gk = (
                3.0 * (2 * s + q).astype(F32)
                + jnp.where(lane_row < l0, 1.0, 0.0)
                + jnp.where(lane_row < l0 + l1, 1.0, 0.0)
            )
            gq = gid[r, :]
            gq = jnp.concatenate([gq, gq], axis=1)
            sc = jnp.where(gq == gk, sc, BIG_NEG)
            e = jnp.exp(sc - jnp.max(sc, axis=-1, keepdims=True))
            pr = e / jnp.sum(e, axis=-1, keepdims=True)
            pf[r, :] = pr
            ctx[r, :] = dot_nn(pr.astype(BF16), v).astype(BF16)

        return f

    def attend_back(s):
        def f(q):
            r = block_rows(s, q)
            dc = dot_nn(xb0[r, :], w[G_ATT][3]).astype(BF16)
            pr = pf[r, :]
            k = kr[r, :]
            dp_ = dot_nt(dc, vr[r, :])
            dqkv[r, 256:384] = dot_tn(pr.astype(BF16), dc).astype(BF16)
            sb = (pr * (dp_ - jnp.sum(pr * dp_, axis=-1, keepdims=True))).astype(BF16)
            dqkv[r, 0:128] = turn_back(dot_nn(sb, k) * (HEAD_DIM**-0.5), r).astype(BF16)
            dqkv[r, 128:256] = turn_back(dot_tn(sb, qr[r, :]), r).astype(BF16)

        return f

    chan = pl.ds(pl.multiple_of(p * 128, 128), 128)
    taps = [cv[j : j + 1, chan] for j in range(KERNEL)]
    gain = cv[KERNEL : KERNEL + 1, chan]
    shift = cv[KERNEL + 1 : KERNEL + 2, chan]
    count = 2 * ROWS
    bn = {}

    def conv_in(s):
        def f(q):
            r = block_rows(s, q)
            t = dot_nn(xg2[r, :], wide(G_CONV, 0, 2))
            sig = sigm(t[:, 128:256])
            cu[r, :] = t[:, 0:128]
            sg[r, :] = sig
            glu[r, :] = t[:, 0:128] * sig

        return f

    def span(s):
        return slice(s * count, (s + 1) * count)

    def same(s, j):
        ids = gid[span(s), :]
        return jnp.where(pltpu.roll(ids, (2 - j) % count, 0) == ids, 1.0, 0.0)

    def add_row(ref, z_, row, value, s):
        at = slice(row, row + 1)
        ref[z_, at, :] = value if s == 0 else ref[z_, at, :] + value

    def mix(s):
        g_all = glu[span(s), :]
        mixed = taps[2] * g_all
        for j in (0, 1, 3, 4):
            mixed = mixed + taps[j] * pltpu.roll(g_all, (2 - j) % count, 0) * same(s, j)
        zc[span(s), :] = mixed
        lv = live[span(s), :]
        add_row(stats.at[0], z, 0, jnp.sum(lv * mixed, axis=0, keepdims=True), s)
        add_row(stats.at[0], z, 1, jnp.sum(lv * mixed * mixed, axis=0, keepdims=True), s)
        add_row(stats.at[0], z, 2, jnp.sum(lv, axis=0, keepdims=True), s)

    def bn_forward():
        line_share(stats.at[0], bns.at[0], bnr.at[0], True)
        line_pass(G_IN1)
        line_start(G_OUT1)
        line_share(stats.at[0], bns.at[0], bnr.at[0], False)
        tot = stats[0, 0] + stats[0, 1] + stats[0, 2] + stats[0, 3]
        bn["n"] = tot[2:3, :]
        bn["mean"] = tot[0:1, :] / bn["n"]
        bn["inv"] = lax.rsqrt(tot[1:2, :] / bn["n"] - bn["mean"] * bn["mean"] + EPS_NORM)

    def conv_out(s):
        def f(q):
            r = block_rows(s, q)
            v = (zc[r, :] - bn["mean"]) * bn["inv"] * gain + shift
            cw[r, :] = (v * sigm(v)).astype(BF16)
            part[...] = dot_nt(cw[r, :], w[G_CONV][2])

        return f

    def conv_back(s):
        def f(q):
            r = block_rows(s, q)
            v = (zc[r, :] - bn["mean"]) * bn["inv"] * gain + shift
            sig = sigm(v)
            dd[r, :] = dot_nn(xb1[r, :], w[G_CONV][2]) * sig * (1.0 + v * (1.0 - sig))

        return f

    def batch_sums(s):
        d_all = dd[span(s), :]
        add_row(stats.at[1], z, 0, jnp.sum(d_all, axis=0, keepdims=True), s)
        centred = zc[span(s), :] - bn["mean"]
        add_row(stats.at[1], z, 1, jnp.sum(d_all * centred, axis=0, keepdims=True), s)

    def bn_backward():
        line_share(stats.at[1], bns.at[1], bnr.at[1], True)
        for k in range(4):
            grad_chunk(G_IN1, k)
        line_share(stats.at[1], bns.at[1], bnr.at[1], False)
        tot = stats[1, 0] + stats[1, 1] + stats[1, 2] + stats[1, 3]
        i = bn["inv"]
        bn["s1"] = tot[0:1, :]
        bn["s2"] = tot[1:2, :]
        bn["dv"] = -0.5 * i * i * i * gain * bn["s2"]
        bn["dm"] = -i * gain * bn["s1"] - 2.0 * bn["mean"] * bn["dv"]

    def unmix(s):
        r = span(s)
        dz = dd[r, :] * (gain * bn["inv"]) + live[r, :] * (
            (bn["dm"] + 2.0 * zc[r, :] * bn["dv"]) / bn["n"]
        )
        g_all = glu[r, :]
        back = jnp.zeros_like(dz)
        for j in range(KERNEL):
            if j == 2:
                weighted = dz
                moved = g_all
            else:
                weighted = dz * same(s, j)
                moved = pltpu.roll(g_all, (2 - j) % count, 0)
            add_row(tapm, z, j, jnp.sum(weighted * moved, axis=0, keepdims=True), s)
            weighted = taps[j] * weighted
            if j != 2:
                weighted = pltpu.roll(weighted, (j - 2) % count, 0)
            back = back + weighted
        s_all = sg[r, :]
        du[r, 0:128] = (back * s_all).astype(BF16)
        du[r, 128:256] = (back * cu[r, :] * s_all * (1.0 - s_all)).astype(BF16)

    def ff_back(s, xb, g, fh):
        def f(q):
            r = block_rows(s, q)
            h = fh[r, :]
            sig = sigm(h)
            d = dot_nn(xb[r, :], w[g][...])
            hb[r, :] = (d * sig * (1.0 + h * (1.0 - sig))).astype(BF16)

        return f

    def out_rows(out, owner_x, core):
        return out.at[pl.ds(pl.multiple_of(owner_x * HALF + core * QUAD, QUAD), QUAD)]

    def give_out(i, s, out):
        there = out_rows(out, x, m)
        src = tstage.at[i, s]
        r_sem = outr.at[i, x, m]

        def a():
            pltpu.make_async_copy(src, there, r_sem).start()
            remote(src, there, outs.at[i, s, 0], r_sem, sib).start()

        def b():
            remote(src, there, outs.at[i, s, 0], r_sem, xn).start()
            remote(src, there, outs.at[i, s, 1], r_sem, (base + px, 1 - m)).start()

        either(x == s, a, b)

    def out_wait(i, out):
        there = out_rows(out, x, m)
        for s in range(2):
            src = tstage.at[i, s]
            remote(src, there, outs.at[i, s, 0], outr.at[i, x, m], xn).wait_send()

            @pl.when(x != s)
            def _():
                remote(src, there, outs.at[i, s, 1], outr.at[i, x, m], xn).wait_send()

        for cx in range(2):
            for cm in range(2):
                here = out.at[cx * HALF + cm * QUAD : cx * HALF + (cm + 1) * QUAD]
                remote(here, here, outs.at[i, 0, 0], outr.at[i, cx, cm], sib).wait_recv()

    def stream(s):
        g_sends = []
        r_sends = []
        at = mine(s)

        def take(xg, compute, name, ready=None):
            def near():
                if ready is not None and s == 0:
                    line_ready(ready)
                compute(y)

            return gather(xg, pieces(s), QUAD, s, near, lambda: compute(1 - y), name, g_sends)

        def give(compute, name):
            return scatter(s, compute, name, r_sends)

        hidden = ff_hidden(s, xg0, G_IN0, fh0, fs0)
        hidden(0)
        hidden(1)
        yield "W"
        t = yield from give(part_nt(s, fs0, whole(G_OUT0)), "R0")
        v = res[s] + 0.5 * t
        res[s] = v
        xg1[at, :] = norm(v, 1, s).astype(BF16)
        yield from take(xg1, attend(s), "G1", G_ATT)
        t = yield from give(part_nt(s, ctx, lambda: w[G_ATT][3]), "R1")
        v = res[s] + t
        res[s] = v
        xg2[at, :] = norm(v, 2, s).astype(BF16)
        yield from take(xg2, conv_in(s), "G2", G_CONV)
        mix(s)
        yield "BN1"
        t = yield from give(conv_out(s), "R2")
        v = res[s] + t
        res[s] = v
        xg3[at, :] = norm(v, 3, s).astype(BF16)
        yield from take(xg3, ff_hidden(s, xg3, G_IN1, fh1, fs1), "G3", G_IN1)
        if s == 0:
            line_ready(G_OUT1)
        t = yield from give(part_nt(s, fs1, whole(G_OUT1)), "R3")
        tstage[0, s] = norm(res[s] + 0.5 * t, 4, s).astype(BF16)
        if s == 0:
            cot_wait()
        v = norm_back(cotb[s].astype(F32), 4, s)
        res[s] = v
        xb0[at, :] = (0.5 * v).astype(BF16)
        yield from take(xb0, ff_back(s, xb0, G_OUT1, fh1), "H3")
        t = yield from give(part_nt(s, hb, whole(G_IN1)), "Q3")
        v = res[s] + norm_back(t, 3, s)
        res[s] = v
        xb1[at, :] = v.astype(BF16)
        yield from take(xb1, conv_back(s), "H2")
        batch_sums(s)
        yield "BN2"
        unmix(s)
        yield "TAPS"
        t = yield from give(part_nt(s, du, lambda: wide(G_CONV, 0, 2)), "Q2")
        v = res[s] + norm_back(t, 2, s)
        res[s] = v
        xb0[at, :] = v.astype(BF16)
        yield from take(xb0, attend_back(s), "H1")
        t = yield from give(part_nt(s, dqkv, lambda: wide(G_ATT, 0, 3)), "Q1")
        v = res[s] + norm_back(t, 1, s)
        res[s] = v
        xb1[at, :] = (0.5 * v).astype(BF16)
        yield from take(xb1, ff_back(s, xb1, G_OUT0, fh0), "H0")
        yield "TAIL"
        t = yield from give(part_nt(s, hb, whole(G_IN0)), "Q0")
        tstage[1, s] = (res[s] + norm_back(t, 0, s)).astype(BF16)
        give_out(1, s, tgrad)
        settle(g_sends)
        settle(r_sends)

    queue = []

    def chunks(g, send):
        def one(k):
            def f():
                grad_chunk(g, k)
                if send:
                    grad_send(g, k)

            return f

        return [one(k) for k in range(4)]

    def first_feed():
        line_pass(G_OUT0)
        line_start(G_ATT)
        line_ready(G_OUT0)

    def tap_share():
        line_share(tapm, bns.at[2], bnr.at[2], True)
        for k in range(3):
            grad_send(G_IN1, k)

    def tail():
        for f in chunks(G_OUT0, True) + chunks(G_IN0, True):
            f()
        for s in range(2):
            give_out(0, s, tout)

    def passing(g, following):
        def f():
            line_pass(g)
            if following is not None:
                line_start(following)

        return f

    meet = {
        "W": first_feed, "BN1": bn_forward, "BN2": bn_backward, "TAPS": tap_share, "TAIL": tail,
    }
    after = {
        "R0.2": [passing(G_ATT, G_CONV)],
        "R1.1": [passing(G_CONV, G_IN1)],
        "G3.0": [passing(G_OUT1, None)],
        "Q3.0": chunks(G_OUT1, True),
        "H2.0": [lambda: grad_acc(G_OUT1)],
        "Q2.0": chunks(G_CONV, True),
        "Q2.2": [lambda: grad_acc(G_IN1)],
        "H1.1": [lambda: grad_final(G_OUT1)],
        "H1.2": [lambda: grad_acc(G_CONV)],
        "Q1.0": chunks(G_ATT, True),
        "Q1.2": [lambda: grad_final(G_IN1)],
        "H0.1": [lambda: grad_acc(G_ATT)],
        "H0.2": [lambda: grad_final(G_CONV)],
        "Q0.1": [lambda: grad_acc(G_OUT0)],
    }
    line_ready(G_IN0)
    streams = [stream(0), stream(1)]
    state = ["", ""]
    while streams[1] is not None:
        for s in range(2):
            if streams[s] is None:
                continue
            try:
                state[s] = next(streams[s])
            except StopIteration:
                streams[s] = None
                continue
            if s == 1:
                queue.extend(after.get(state[s], []))
            if queue:
                queue.pop(0)()
            if s == 1 and state[s] in meet:
                while queue:
                    queue.pop(0)()
                meet[state[s]]()
    while queue:
        queue.pop(0)()
    grad_final(G_ATT)
    grad_acc(G_IN0)

    def swap(src, dst, k, dev):
        copy = remote(src, dst, nss.at[k], nsr.at[k], dev)
        copy.start()
        copy.wait()

    swap(ngm, nsib, 0, sib)
    ngm[...] = ngm[...] + nsib[...]
    swap(ngm, nx, 1, xn)
    ngm[...] = ngm[...] + nx[...]
    swap(ngm, ny, 2, yn)
    nz[z] = ngm[...] + ny[...]
    line_share(nz, nss.at[pl.ds(3, 3)], nsr.at[pl.ds(3, 3)], True)
    line_share(tapm, bns.at[2], bnr.at[2], False)
    cgm[...] = tapm[0] + tapm[1] + tapm[2] + tapm[3]
    cgm[5:6, :] = bn["inv"] * bn["s2"]
    cgm[6:7, :] = bn["s1"]
    cgrad[:, chan] = cgm[...]
    for r in range(3):
        remote(cgm, cgrad.at[:, chan], cgs.at[r], cgr.at[r], plane[r][1]).start()
    grad_final(G_OUT0)
    line_share(nz, nss.at[pl.ds(3, 3)], nsr.at[pl.ds(3, 3)], False)
    ngrad[...] = nz[0] + nz[1] + nz[2] + nz[3]
    for r in range(3):
        peer, dev = plane[r]
        there = cgrad.at[:, pl.ds(pl.multiple_of(peer * 128, 128), 128)]
        remote(there, there, cgs.at[r], cgr.at[r], dev).wait_recv()
        remote(cgm, cgrad.at[:, chan], cgs.at[r], cgr.at[r], dev).wait_send()
    grad_final(G_IN0)
    out_wait(0, tout)
    out_wait(1, tgrad)
    for copy in pending:
        copy.wait_send()
    for g in range(6):
        line_done(g)
        grad_done(g)


def group_shape(g, rows):
    if g == G_ATT:
        return (4, rows, 128)
    if g == G_CONV:
        return (3, rows, 128)
    return (rows, 512)


def rotation_tables():
    half = HEAD_DIM // 2
    frequency = np.exp(np.arange(half, dtype=np.float32) * np.float32(-2.0 * math.log(10000.0) / HEAD_DIM))
    angles = np.arange(ROWS, dtype=np.float32)[:, None] * frequency.astype(np.float32)[None, :]
    c = np.cos(angles.astype(np.float64))
    s = np.sin(angles.astype(np.float64))
    table = np.concatenate([c, c, -s, s], axis=1).astype(np.float32)
    high = table.astype(BF16)
    low_part = (table - high.astype(np.float32)).astype(BF16)
    return high, low_part


def fused_call(tok, cot, lens, norm_vectors, channel_vectors, fi_b, fo_b, mi_b, mo_b):
    high, low_part = rotation_tables()
    vm = pl.BlockSpec(memory_space=pltpu.VMEM)
    hbm = pl.BlockSpec(memory_space=pl.ANY)

    def v(shape, dtype):
        return pltpu.VMEM(shape, dtype)

    t16 = (4 * ROWS, D)
    h16 = (4 * ROWS, 512)
    c16 = (4 * ROWS, 128)
    scratch = [v(group_shape(g, D), BF16) for g in range(6)]
    scratch += [v(t16, BF16)] * 6
    scratch += [v(h16, F32)] * 2 + [v(h16, BF16)] * 3
    scratch += [v(c16, BF16)] * 4 + [v((4 * ROWS, 384), BF16), v((4 * ROWS, ROWS), F32)]
    scratch += [v(c16, F32)] * 5 + [v(c16, BF16), v((4 * ROWS, 256), BF16)]
    scratch += [v(c16, F32)] * 4 + [v((4, 8, ROWS), F32)]
    scratch += [v((5, 2, QUAD, D), F32), v((5, 2, QUAD, 128), F32), v((2, QUAD, D), F32)]
    scratch += [v((2, 4, QUAD, D), BF16)] * 2 + [v((2, QUAD, D), BF16)] + [v((2, OCT, D), BF16)] * 2
    scratch += [v((2, QUAD, D), BF16)] * 4 + [v((2, 4, QUAD, D), F32), v((ROWS, D), F32)]
    scratch += [v((4,) + group_shape(g, ROWS), BF16) for g in range(6)]
    scratch += [v((3,) + group_shape(g, ROWS), BF16) for g in range(6)]
    scratch += [v(group_shape(g, ROWS), BF16) for g in range(6)]
    scratch += [v((2, 4, 8, 128), F32), v((4, 8, 128), F32)]
    scratch += [v((16, D), F32)] * 4 + [v((4, 16, D), F32), v((8, 128), F32), v((2, 2, QUAD, D), BF16)]
    scratch += [v((2, QUAD, D), BF16)]
    dma = pltpu.SemaphoreType.DMA
    sems = [(3, 11), (3, 11), (2, 10), (2, 10), (6, 4, 2), (6, 4, 2), (6, 4), (6, 4), (6, 4), (6, 4)]
    sems += [(6, 4, 2), (6, 4, 2), (3,), (3,), (3, 3), (3, 3), (6,), (6,), (3,), (3,), (2, 2, 2), (2, 2, 2), (2,), (2,)]
    scratch += [dma(k) for k in sems]
    out_shape = (
        jax.ShapeDtypeStruct((ROWS, D), BF16),
        jax.ShapeDtypeStruct((ROWS, D), BF16),
        jax.ShapeDtypeStruct((2, SHARD, 2048), BF16),
        jax.ShapeDtypeStruct((2, SHARD, 2048), BF16),
        jax.ShapeDtypeStruct((5, SHARD, 512), BF16),
        jax.ShapeDtypeStruct((2, SHARD, 512), BF16),
        jax.ShapeDtypeStruct((16, D), F32),
        jax.ShapeDtypeStruct((8, 512), F32),
    )
    return pl.pallas_call(
        fused_kernel,
        out_shape=out_shape,
        in_specs=[vm] * 7 + [hbm] * 4,
        out_specs=(hbm,) * 6 + (vm, vm),
        scratch_shapes=scratch,
        compiler_params=pltpu.CompilerParams(
            collective_id=0, has_side_effects=True, vmem_limit_bytes=63 * 2**20
        ),
    )(tok, cot, lens, jnp.asarray(high), jnp.asarray(low_part), norm_vectors, channel_vectors, fi_b, fo_b, mi_b, mo_b)


def fast_body(
    tokens_in, out_cotangent, utt_lengths,
    feed_in, feed_in_mean, feed_in_square,
    feed_out, feed_out_mean, feed_out_square,
    mixer_in, mixer_in_mean, mixer_in_square,
    mixer_out, mixer_out_mean, mixer_out_square,
    norm_vectors, norm_vectors_mean, norm_vectors_square,
    channel_vectors, channel_vectors_mean, channel_vectors_square,
):
    lens = jnp.broadcast_to(
        jnp.pad(utt_lengths[0].astype(F32), (0, 6))[:, None], (8, ROWS)
    )
    tokens_out, tokens_grad, gfi, gfo, gmi, gmo, ngrad, cgrad = fused_call(
        tokens_in,
        out_cotangent,
        lens,
        norm_vectors,
        channel_vectors,
        feed_in.astype(BF16),
        jnp.swapaxes(feed_out, 1, 2).astype(BF16),
        mixer_in.astype(BF16),
        jnp.swapaxes(mixer_out, 1, 2).astype(BF16),
    )
    rates = rate_table()

    def step(weight, mean_state, square_state, gradient, rate):
        return adamw_step(weight, mean_state, square_state, gradient.astype(F32), rate)

    fi = step(feed_in, feed_in_mean, feed_in_square, gfi, rates[0])
    fo = step(feed_out, feed_out_mean, feed_out_square, jnp.swapaxes(gfo, 1, 2), rates[1])
    mi = step(mixer_in, mixer_in_mean, mixer_in_square, gmi, rates[2])
    mo = step(mixer_out, mixer_out_mean, mixer_out_square, jnp.swapaxes(gmo, 1, 2), rates[3])
    nv = step(norm_vectors, norm_vectors_mean, norm_vectors_square, ngrad[:10], rates[4])
    cv = step(channel_vectors, channel_vectors_mean, channel_vectors_square, cgrad[:7], rates[5])
    return (tokens_out.astype(F32), tokens_grad.astype(F32)) + fi + fo + mi[:2] + (mi[2][:4], mi[2][4]) + mo + nv + cv


def solution(mesh):
    fits = mesh.shape["dp"] == 16 and mesh.shape["mp"] == 2
    placed = (
        P("dp", None),
        P("dp", None),
        P("dp", None),
        P(None, "dp", "mp"),
        P(None, "dp", "mp"),
        P(None, "dp", "mp"),
        P(None, "mp", "dp"),
        P(None, "mp", "dp"),
        P(None, "mp", "dp"),
        P(None, "dp", "mp"),
        P(None, "dp", "mp"),
        P(None, "dp", "mp"),
        P(None, "mp", "dp"),
        P(None, "mp", "dp"),
        P(None, "mp", "dp"),
        P(),
        P(),
        P(),
        P(None, "mp"),
        P(None, "mp"),
        P(None, "mp"),
    )
    return jax.shard_map(
        fast_body if fits else body,
        mesh=mesh,
        in_specs=placed,
        out_specs=(
            P("dp", None),
            P("dp", None),
            P(None, "dp", "mp"),
            P(None, "dp", "mp"),
            P(None, "dp", "mp"),
            P(None, "mp", "dp"),
            P(None, "mp", "dp"),
            P(None, "mp", "dp"),
            P(None, "dp", "mp"),
            P(None, "dp", "mp"),
            P(None, "dp", "mp"),
            P("dp", "mp"),
            P(None, "mp", "dp"),
            P(None, "mp", "dp"),
            P(None, "mp", "dp"),
            P(),
            P(),
            P(),
            P(None, "mp"),
            P(None, "mp"),
            P(None, "mp"),
        ),
        check_vma=False,
    )
```

```python
import math

import jax
import jax.numpy as jnp
import numpy as np
from jax import lax
from jax.experimental import pallas as pl
from jax.experimental.pallas import tpu as pltpu
from jax.sharding import PartitionSpec as P

D = 1024
FF = 4096
HEAD_DIM = 128
KERNEL = 5
STEP_COUNT = 3
TOK_DEV = 256


EPS_NORM = 1e-05
EPS_ADAM = 1e-08
DECAY_WEIGHT = 0.01
BETA = 0.5
BIG_NEG = -1e30


def product(left_side, right_side):
    return jnp.dot(left_side, right_side, preferred_element_type=jnp.float32)


def weight_grad(inputs, gradients):
    return lax.dot_general(
        inputs, gradients, (((0,), (0,)), ((), ())), preferred_element_type=jnp.float32
    )


def input_grad(gradients, weight):
    return lax.dot_general(
        gradients, weight, (((1,), (1,)), ((), ())), preferred_element_type=jnp.float32
    )


def norm_forward(values, gain_row, shift_row):
    centre = values - jnp.mean(values, axis=-1, keepdims=True)
    inverse = lax.rsqrt(jnp.mean(centre * centre, axis=-1, keepdims=True) + EPS_NORM)
    scaled = centre * inverse
    return (scaled * gain_row + shift_row, scaled, inverse)


def norm_backward(grad_out, scaled, inverse, gain_row):
    grad_gain = jnp.sum(grad_out * scaled, axis=0)
    grad_shift = jnp.sum(grad_out, axis=0)
    grad_scaled = grad_out * gain_row
    grad_in = inverse * (
        grad_scaled
        - jnp.mean(grad_scaled, axis=-1, keepdims=True)
        - scaled * jnp.mean(grad_scaled * scaled, axis=-1, keepdims=True)
    )
    return (grad_in, grad_gain, grad_shift)


def rotate(values, cosine, sine_part):
    halfway = values.shape[-1] // 2
    front_half = values[..., :halfway]
    back_half = values[..., halfway:]
    return jnp.concatenate(
        [front_half * cosine - back_half * sine_part, front_half * sine_part + back_half * cosine],
        axis=-1,
    )


def unrotate(values, cosine, sine_part):
    halfway = values.shape[-1] // 2
    front_half = values[..., :halfway]
    back_half = values[..., halfway:]
    return jnp.concatenate(
        [front_half * cosine + back_half * sine_part, back_half * cosine - front_half * sine_part],
        axis=-1,
    )


def depthwise(gated_rows, kernel, group_ids):
    count_rows = gated_rows.shape[0]
    reach = KERNEL // 2
    padded = jnp.pad(gated_rows, ((reach, reach), (0, 0)))
    padded_ids = jnp.pad(group_ids, (reach, reach), constant_values=-1)
    summed = jnp.zeros_like(gated_rows)
    for offset in range(KERNEL):
        matched = (padded_ids[offset : offset + count_rows] == group_ids).astype(jnp.float32)
        summed = summed + kernel[offset] * padded[offset : offset + count_rows] * matched[:, None]
    return summed


def depthwise_back(grad_mixed, gated_rows, kernel, group_ids):
    count_rows = gated_rows.shape[0]
    reach = KERNEL // 2
    padded = jnp.pad(gated_rows, ((reach, reach), (0, 0)))
    padded_ids = jnp.pad(group_ids, (reach, reach), constant_values=-1)
    grad_padded = jnp.zeros_like(padded)
    kernel_rows = []
    for offset in range(KERNEL):
        matched = (padded_ids[offset : offset + count_rows] == group_ids).astype(jnp.float32)
        weighted = grad_mixed * matched[:, None]
        kernel_rows.append(jnp.sum(weighted * padded[offset : offset + count_rows], axis=0))
        grad_padded = grad_padded.at[offset : offset + count_rows].add(kernel[offset] * weighted)
    return (jnp.stack(kernel_rows), grad_padded[reach : reach + count_rows])


def rate_table():
    attention_fan = max(2 * D // TOK_DEV, 1)
    mixer_rates = jnp.array([attention_fan ** (-0.5), D ** (-0.5)], dtype=jnp.float32)[
        :, None, None
    ]
    return (D ** (-0.5), FF ** (-0.5), D ** (-0.5), mixer_rates, 0.3, 0.3)


def adamw_step(weight, mean_state, square_state, gradient, step_rate):
    mean_next = BETA * mean_state + (1.0 - BETA) * gradient
    square_next = BETA * square_state + (1.0 - BETA) * gradient * gradient
    correct = 1.0 - BETA**STEP_COUNT
    direction = mean_next / correct / (jnp.sqrt(square_next / correct) + EPS_ADAM)
    return (weight - step_rate * (direction + DECAY_WEIGHT * weight), mean_next, square_next)


def branch_total(partial_sum):
    return lax.psum(partial_sum.astype(jnp.bfloat16), "mp").astype(jnp.float32)


def input_total(partial_sum):
    return lax.psum(partial_sum.astype(jnp.bfloat16), "mp").astype(jnp.float32)


def body(
    tokens_in,
    out_cotangent,
    utt_lengths,
    feed_in,
    feed_in_mean,
    feed_in_square,
    feed_out,
    feed_out_mean,
    feed_out_square,
    mixer_in,
    mixer_in_mean,
    mixer_in_square,
    mixer_out,
    mixer_out_mean,
    mixer_out_square,
    norm_vectors,
    norm_vectors_mean,
    norm_vectors_square,
    channel_vectors,
    channel_vectors_mean,
    channel_vectors_square,
):
    count_rows = tokens_in.shape[0]
    local_width = mixer_in.shape[2]
    local_heads = local_width // HEAD_DIM
    heads_shape = (count_rows, local_heads, HEAD_DIM)
    score_scale = HEAD_DIM ** (-0.5)
    first_len = utt_lengths[0, 0]
    second = utt_lengths[0, 1]
    places = jnp.arange(count_rows, dtype=jnp.int32)
    in_first = (places < first_len).astype(jnp.int32)
    in_live = (places < first_len + second).astype(jnp.int32)
    group_ids = in_first + in_live
    positions = places - first_len * (1 - in_first) - second * (1 - in_live)
    live_rows = in_live.astype(jnp.float32)[:, None]
    halfway = HEAD_DIM // 2
    frequency = jnp.exp(
        jnp.arange(halfway, dtype=jnp.float32) * (-2.0 * math.log(10000.0) / HEAD_DIM)
    )
    angles = positions.astype(jnp.float32)[:, None] * frequency[None, :]
    cosine = jnp.cos(angles)[:, None, :]
    sine_part = jnp.sin(angles)[:, None, :]
    allowed = (group_ids[:, None] == group_ids[None, :])[None]
    kernel = channel_vectors[:KERNEL]
    batch_gain = channel_vectors[KERNEL]
    batch_shift = channel_vectors[KERNEL + 1]
    weight_in, weight_out, weight_mix, weight_back = (
        lax.all_gather(feed_in.astype(jnp.bfloat16), "dp", axis=1, tiled=True),
        lax.all_gather(feed_out.astype(jnp.bfloat16), "dp", axis=2, tiled=True),
        lax.all_gather(mixer_in.astype(jnp.bfloat16), "dp", axis=1, tiled=True),
        lax.all_gather(mixer_out.astype(jnp.bfloat16), "dp", axis=2, tiled=True),
    )

    def feed_forward(residual, norm_slot, feed_layer):
        normed, scaled, inverse = norm_forward(
            residual, norm_vectors[norm_slot], norm_vectors[5 + norm_slot]
        )
        normed_low = normed.astype(jnp.bfloat16)
        hidden = product(normed_low, weight_in[feed_layer])
        active = (hidden * jax.nn.sigmoid(hidden)).astype(jnp.bfloat16)
        branch = branch_total(product(active, weight_out[feed_layer]))
        return (residual + 0.5 * branch, (scaled, inverse, normed_low, hidden, active))

    section_zero = tokens_in.astype(jnp.float32)
    section_one, kept_first = feed_forward(section_zero, 0, 0)
    normed, scaled_att, inverse_att = norm_forward(section_one, norm_vectors[1], norm_vectors[6])
    normed_att = normed.astype(jnp.bfloat16)
    projected = jnp.einsum(
        "td,sdc->stc", normed_att, weight_mix[:3], preferred_element_type=jnp.float32
    )
    queries = (rotate(projected[0].reshape(heads_shape), cosine, sine_part) * score_scale).astype(
        jnp.bfloat16
    )
    key_rows = rotate(projected[1].reshape(heads_shape), cosine, sine_part).astype(jnp.bfloat16)
    value_rows = projected[2].reshape(heads_shape).astype(jnp.bfloat16)
    scores = jnp.where(
        allowed,
        jnp.einsum("qhd,khd->hqk", queries, key_rows, preferred_element_type=jnp.float32),
        BIG_NEG,
    )
    largest = jnp.max(scores, axis=-1, keepdims=True)
    exponent = jnp.exp(scores - largest)
    totals = jnp.sum(exponent, axis=-1, keepdims=True)
    softmax_rows = exponent / totals
    log_total = largest + jnp.log(totals)
    context = jnp.einsum(
        "hqk,khd->qhd",
        softmax_rows.astype(jnp.bfloat16),
        value_rows,
        preferred_element_type=jnp.float32,
    )
    context_low = context.reshape(count_rows, local_width).astype(jnp.bfloat16)
    section_two = section_one + branch_total(product(context_low, weight_back[0]))
    normed, scaled_conv, inverse_conv = norm_forward(section_two, norm_vectors[2], norm_vectors[7])
    normed_conv = normed.astype(jnp.bfloat16)
    conv_proj = jnp.einsum(
        "td,sdc->stc", normed_conv, weight_mix[3:], preferred_element_type=jnp.float32
    )
    gate_sig = jax.nn.sigmoid(conv_proj[1])
    gated_rows = conv_proj[0] * gate_sig
    mixed_rows = depthwise(gated_rows, kernel, group_ids)
    batch_stats = lax.psum(
        (
            jnp.sum(live_rows * mixed_rows, axis=0),
            jnp.sum(live_rows * mixed_rows * mixed_rows, axis=0),
            jnp.sum(live_rows),
        ),
        "dp",
    )
    count_live = batch_stats[2]
    mean_batch = batch_stats[0] / count_live
    inverse_batch = lax.rsqrt(batch_stats[1] / count_live - mean_batch * mean_batch + EPS_NORM)
    centred = mixed_rows - mean_batch
    batch_out = centred * inverse_batch * batch_gain + batch_shift
    batch_sig = jax.nn.sigmoid(batch_out)
    active_conv = (batch_out * batch_sig).astype(jnp.bfloat16)
    section_three = section_two + branch_total(product(active_conv, weight_back[1]))
    section_four, kept_second = feed_forward(section_three, 3, 1)
    tokens_out, scaled_last, inverse_last = norm_forward(
        section_four, norm_vectors[4], norm_vectors[9]
    )

    def feed_backward(grad_residual, kept, norm_slot, feed_layer):
        scaled, inverse, normed_low, hidden, active = kept
        grad_branch = (0.5 * grad_residual).astype(jnp.bfloat16)
        grad_down = weight_grad(active, grad_branch)
        hidden_sig = jax.nn.sigmoid(hidden)
        grad_hidden = (
            input_grad(grad_branch, weight_out[feed_layer])
            * hidden_sig
            * (1.0 + hidden * (1.0 - hidden_sig))
        ).astype(jnp.bfloat16)
        grad_up = weight_grad(normed_low, grad_hidden)
        grad_normed = input_total(input_grad(grad_hidden, weight_in[feed_layer]))
        grad_in, grad_gain, grad_shift = norm_backward(
            grad_normed, scaled, inverse, norm_vectors[norm_slot]
        )
        return (grad_residual + grad_in, grad_up, grad_down, grad_gain, grad_shift)

    grad_residual, gain_last, shift_last = norm_backward(
        out_cotangent.astype(jnp.float32), scaled_last, inverse_last, norm_vectors[4]
    )
    grad_residual, up_second, down_second, gain_three, shift_three = feed_backward(
        grad_residual, kept_second, 3, 1
    )
    grad_branch = grad_residual.astype(jnp.bfloat16)
    grad_conv_down = weight_grad(active_conv, grad_branch)
    grad_batch = (
        input_grad(grad_branch, weight_back[1]) * batch_sig * (1.0 + batch_out * (1.0 - batch_sig))
    )
    batch_sums = lax.psum(
        (jnp.sum(grad_batch, axis=0), jnp.sum(grad_batch * centred, axis=0)), "dp"
    )
    grad_var = -0.5 * inverse_batch**3 * batch_gain * batch_sums[1]
    grad_mean = -inverse_batch * batch_gain * batch_sums[0] - 2.0 * mean_batch * grad_var
    grad_mixed = (
        grad_batch * batch_gain * inverse_batch
        + live_rows * (grad_mean + 2.0 * mixed_rows * grad_var) / count_live
    )
    kernel_grads, grad_gated = depthwise_back(grad_mixed, gated_rows, kernel, group_ids)
    grad_conv_up = jnp.stack(
        [grad_gated * gate_sig, grad_gated * conv_proj[0] * gate_sig * (1.0 - gate_sig)]
    ).astype(jnp.bfloat16)
    grad_conv_in = jnp.einsum(
        "td,stc->sdc", normed_conv, grad_conv_up, preferred_element_type=jnp.float32
    )
    grad_normed = input_total(
        jnp.einsum("stc,sdc->td", grad_conv_up, weight_mix[3:], preferred_element_type=jnp.float32)
    )
    grad_in, gain_two, shift_two = norm_backward(
        grad_normed, scaled_conv, inverse_conv, norm_vectors[2]
    )
    grad_residual = grad_residual + grad_in
    grad_branch = grad_residual.astype(jnp.bfloat16)
    grad_att_down = weight_grad(context_low, grad_branch)
    grad_context = input_grad(grad_branch, weight_back[0]).astype(jnp.bfloat16).reshape(heads_shape)
    scores_again = jnp.where(
        allowed,
        jnp.einsum("qhd,khd->hqk", queries, key_rows, preferred_element_type=jnp.float32),
        BIG_NEG,
    )
    softmax_again = jnp.exp(scores_again - log_total)
    grad_softmax = jnp.einsum(
        "qhd,khd->hqk", grad_context, value_rows, preferred_element_type=jnp.float32
    )
    grad_values = jnp.einsum(
        "hqk,qhd->khd",
        softmax_again.astype(jnp.bfloat16),
        grad_context,
        preferred_element_type=jnp.float32,
    )
    grad_scores = (
        softmax_again
        * (grad_softmax - jnp.sum(softmax_again * grad_softmax, axis=-1, keepdims=True))
    ).astype(jnp.bfloat16)
    grad_queries = unrotate(
        jnp.einsum("hqk,khd->qhd", grad_scores, key_rows, preferred_element_type=jnp.float32)
        * score_scale,
        cosine,
        sine_part,
    )
    grad_keys = unrotate(
        jnp.einsum("hqk,qhd->khd", grad_scores, queries, preferred_element_type=jnp.float32),
        cosine,
        sine_part,
    )
    grad_att_up = (
        jnp.stack([grad_queries, grad_keys, grad_values])
        .reshape(3, count_rows, local_width)
        .astype(jnp.bfloat16)
    )
    grad_att_in = jnp.einsum(
        "td,stc->sdc", normed_att, grad_att_up, preferred_element_type=jnp.float32
    )
    grad_normed = input_total(
        jnp.einsum("stc,sdc->td", grad_att_up, weight_mix[:3], preferred_element_type=jnp.float32)
    )
    grad_in, gain_one, shift_one = norm_backward(
        grad_normed, scaled_att, inverse_att, norm_vectors[1]
    )
    grad_residual = grad_residual + grad_in
    grad_residual, up_first, down_first, gain_zero, shift_zero = feed_backward(
        grad_residual, kept_first, 0, 0
    )
    feed_in_grad, feed_out_grad, mixer_in_grad, mixer_out_grad = (
        lax.psum_scatter(jnp.stack([up_first, up_second]), "dp", scatter_dimension=1, tiled=True),
        lax.psum_scatter(
            jnp.stack([down_first, down_second]), "dp", scatter_dimension=2, tiled=True
        ),
        lax.psum_scatter(
            jnp.concatenate([grad_att_in, grad_conv_in], axis=0),
            "dp",
            scatter_dimension=1,
            tiled=True,
        ),
        lax.psum_scatter(
            jnp.stack([grad_att_down, grad_conv_down]), "dp", scatter_dimension=2, tiled=True
        ),
    )
    norm_grads = jnp.stack(
        [
            gain_zero,
            gain_one,
            gain_two,
            gain_three,
            gain_last,
            shift_zero,
            shift_one,
            shift_two,
            shift_three,
            shift_last,
        ]
    )
    norm_total, kernel_total = lax.psum((norm_grads, kernel_grads), "dp")
    channel_grads = jnp.concatenate(
        [kernel_total, (inverse_batch * batch_sums[1])[None], batch_sums[0][None]], axis=0
    )
    rate_list = rate_table()
    feed_in_next, feed_in_mean_next, feed_in_square_next = adamw_step(
        feed_in, feed_in_mean, feed_in_square, feed_in_grad, rate_list[0]
    )
    feed_out_next, feed_out_mean_next, feed_out_square_next = adamw_step(
        feed_out, feed_out_mean, feed_out_square, feed_out_grad, rate_list[1]
    )
    mixer_in_next, mixer_in_mean_next, mixer_in_square_next = adamw_step(
        mixer_in, mixer_in_mean, mixer_in_square, mixer_in_grad, rate_list[2]
    )
    mixer_out_next, mixer_out_mean_next, mixer_out_square_next = adamw_step(
        mixer_out, mixer_out_mean, mixer_out_square, mixer_out_grad, rate_list[3]
    )
    norm_vectors_next, norm_vectors_mean_next, norm_vectors_square_next = adamw_step(
        norm_vectors, norm_vectors_mean, norm_vectors_square, norm_total, rate_list[4]
    )
    channel_vectors_next, channel_vectors_mean_next, channel_vectors_square_next = adamw_step(
        channel_vectors, channel_vectors_mean, channel_vectors_square, channel_grads, rate_list[5]
    )
    return (
        tokens_out,
        grad_residual,
        feed_in_next,
        feed_in_mean_next,
        feed_in_square_next,
        feed_out_next,
        feed_out_mean_next,
        feed_out_square_next,
        mixer_in_next,
        mixer_in_mean_next,
        mixer_in_square_next[:4],
        mixer_in_square_next[4],
        mixer_out_next,
        mixer_out_mean_next,
        mixer_out_square_next,
        norm_vectors_next,
        norm_vectors_mean_next,
        norm_vectors_square_next,
        channel_vectors_next,
        channel_vectors_mean_next,
        channel_vectors_square_next,
    )


MESH = pl.DeviceIdType.MESH
F32 = jnp.float32
BF16 = jnp.bfloat16
ROWS = 256
HALF = 128
QUAD = 64
OCT = 32
SHARD = 64
G_IN0, G_OUT0, G_ATT, G_CONV, G_IN1, G_OUT1 = range(6)


def dot_nn(a, b):
    return lax.dot_general(a, b, (((1,), (0,)), ((), ())), preferred_element_type=F32)


def dot_nt(a, b):
    return lax.dot_general(a, b, (((1,), (1,)), ((), ())), preferred_element_type=F32)


def dot_tn(a, b):
    return lax.dot_general(a, b, (((0,), (0,)), ((), ())), preferred_element_type=F32)


def sigm(v):
    return 1.0 / (1.0 + jnp.exp(-v))


def fused_kernel(
    tok, cot, lens, rot_hi, rot_lo, nv, cv, fi_h, fo_h, mi_h, mo_h,
    tout, tgrad, gfi, gfo, gmi, gmo, ngrad, cgrad,
    fi_f, fo_f, mi_f, mo_f, fi_b, fo_b, mi_b, mo_b,
    w0, w1, w2, w3, w4, w5, xg0, xg1, xg2, xg3, xb0, xb1,
    fh0, fh1, fs0, fs1, hb, qr, kr, vr, ctx, dqkv, pf,
    cu, sg, glu, zc, dd, cw, du, gid, live, rc_t, rs_t, lb,
    xh, inv, res, so, si, sd, hx, hy, sx, sy, rx, ry, keep, part,
    gs0, gs1, gs2, gs3, gs4, gs5, gi0, gi1, gi2, gi3, gi4, gi5,
    ac0, ac1, ac2, ac3, ac4, ac5, stats, tapm, ngm, nsib, nx, ny, nz, cgm, tstage, cotb,
    ags, agr, rss, rsr, was, war, zs, zr, grs, grr, gas, gar, lss, lsr,
    bns, bnr, nss, nsr, cgs, cgr, outs, outr, cts, ctr, lds,
):
    w = (w0, w1, w2, w3, w4, w5)
    gst = (gs0, gs1, gs2, gs3, gs4, gs5)
    gin = (gi0, gi1, gi2, gi3, gi4, gi5)
    acc = (ac0, ac1, ac2, ac3, ac4, ac5)
    dp = lax.axis_index("dp")
    m = lax.axis_index("mp")
    x = dp % 2
    y = (dp // 2) % 2
    z = dp // 4
    p = dp % 4
    base = z * 4
    px = p + 1 - 2 * x
    py = p + 2 - 4 * y
    pd = 3 - p
    sib = (dp, 1 - m)
    xn = (base + px, m)
    yn = (base + py, m)
    dn = (base + pd, m)
    plane = ((px, xn), (py, yn), (pd, dn))
    inner = (z + 1) // 2 % 2
    others = tuple((z + k) % 4 for k in (1, 2, 3))

    def zdev(zz):
        return (zz * 4 + p, m)

    def remote(src, dst, ssem, rsem, dev):
        return pltpu.make_async_remote_copy(
            src_ref=src, dst_ref=dst, send_sem=ssem, recv_sem=rsem, device_id=dev, device_id_type=MESH
        )

    def rows(start, size):
        return pl.ds(pl.multiple_of(start, size), size)

    def block(b):
        return rows(b * ROWS, ROWS)

    pending = []

    def go_send(copy):
        copy.start()
        pending.append(copy)

    shards = {
        G_IN0: ((fi_h, fi_f, fi_b, slice(0, 1)),),
        G_OUT0: ((fo_h, fo_f, fo_b, slice(0, 1)),),
        G_ATT: ((mi_h, mi_f, mi_b, slice(0, 3)), (mo_h, mo_f, mo_b, slice(0, 1))),
        G_CONV: ((mi_h, mi_f, mi_b, slice(3, 5)), (mo_h, mo_f, mo_b, slice(1, 2))),
        G_IN1: ((fi_h, fi_f, fi_b, slice(1, 2)),),
        G_OUT1: ((fo_h, fo_f, fo_b, slice(1, 2)),),
    }

    def shard_copies(g):
        return [
            pltpu.make_async_copy(src.at[r], dst.at[r], lds.at[g, k])
            for k, (src, dst, _, r) in enumerate(shards[g])
        ]

    for g in range(6):
        for copy in shard_copies(g):
            copy.start()

    def round_shard(g):
        for copy in shard_copies(g):
            copy.wait()
        for _, src, dst, r in shards[g]:
            dst[r] = src[r].astype(BF16)

    barrier = pltpu.get_barrier_semaphore()
    greet = (sib, xn, yn, dn) + tuple(zdev(k) for k in others)
    greet += tuple((base + k, 1 - m) for k in (px, py, pd))
    for dev in greet:
        pl.semaphore_signal(barrier, inc=1, device_id=dev, device_id_type=MESH)
    pl.semaphore_wait(barrier, len(greet))

    def wview(g, start, size):
        r = pl.ds(pl.multiple_of(start, SHARD), size)
        return w[g].at[:, r] if g in (G_ATT, G_CONV) else w[g].at[r]

    def columns(i, wd):
        return pl.ds(pl.multiple_of(i * wd, 128), wd)

    def wpieces(g, peer, owner):
        r = pl.ds(pl.multiple_of(z * ROWS + owner * SHARD, SHARD), SHARD)
        if g == G_ATT:
            return (
                (mi_b.at[0:3, :, columns(peer, 128)], w[g].at[0:3, r]),
                (mo_b.at[0, :, columns(peer, 128)], w[g].at[3, r]),
            )
        if g == G_CONV:
            return (
                (mi_b.at[3:5, :, columns(peer, 128)], w[g].at[0:2, r]),
                (mo_b.at[1, :, columns(peer, 128)], w[g].at[2, r]),
            )
        src = fi_b if g in (G_IN0, G_IN1) else fo_b
        layer = 0 if g in (G_IN0, G_OUT0) else 1
        return ((src.at[layer, :, columns(peer, 512)], w[g].at[r]),)

    def plane_start(g):
        round_shard(g)
        for r, (peer, dev) in enumerate(plane):
            for k, (src, dst) in enumerate(wpieces(g, peer, p)):
                go_send(remote(src, dst, was.at[g, r, k], war.at[g, r, k], dev))
        for k, (src, dst) in enumerate(wpieces(g, p, p)):
            pltpu.make_async_copy(src, dst, was.at[g, 3, k]).start()

    def plane_wait(g):
        for r, (peer, dev) in enumerate(plane):
            for k, (_, dst) in enumerate(wpieces(g, peer, peer)):
                remote(dst, dst, was.at[g, r, k], war.at[g, r, k], dev).wait_recv()
        for k, (src, dst) in enumerate(wpieces(g, p, p)):
            pltpu.make_async_copy(src, dst, was.at[g, 3, k]).wait()

    targets = {0: (2, 1), 1: (3, 0, 2), 2: (0, 3, 1), 3: (1, 2)}
    far = {1: (3, 0), 2: (0, 3)}

    def zcopy(g, owner, k, to):
        part_w = wview(g, owner * ROWS, ROWS)
        return remote(part_w, part_w, zs.at[g, k], zr.at[g, owner], zdev(to))

    def line_start(g):
        plane_wait(g)
        for zz, tos in targets.items():

            @pl.when(z == zz)
            def _():
                for k, to in enumerate(tos):
                    zcopy(g, zz, k, to).start()

    def line_pass(g):
        for zz, (owner, to) in far.items():

            @pl.when(z == zz)
            def _():
                zcopy(g, owner, 3, to).wait_recv()
                zcopy(g, owner, 3, to).start()

    def line_ready(g):
        for zz in range(4):

            @pl.when(z == zz)
            def _():
                for owner in range(4):
                    if owner != zz and (zz not in far or far[zz][0] != owner):
                        zcopy(g, owner, 0, zz).wait_recv()

    def line_done(g):
        for zz, tos in targets.items():

            @pl.when(z == zz)
            def _():
                for k, to in enumerate(tos):
                    zcopy(g, zz, k, to).wait_send()
                if zz in far:
                    zcopy(g, far[zz][0], 3, far[zz][1]).wait_send()

    def pieces(s):
        return lambda b, c, off, size: pl.ds(
            pl.multiple_of(s * 2 * ROWS + b * HALF + c * QUAD + off, OCT), size
        )

    def blocks_of_chips(b, c, off, size):
        return pl.ds(pl.multiple_of(place_of(b) * ROWS + c * HALF + off, QUAD), size)

    def place_of(b):
        return b % 2 * 2 + b // 2

    def mine(s):
        return pieces(s)(p, m, 0, QUAD)

    def settle(sends):
        for k in sends:
            k.wait_send()
        sends.clear()

    def gather(xg, where, half, sem, near, far_piece, name, sends):
        quad = half // 2

        def c(i, b, core, off, size, dev):
            r = xg.at[where(b, core, off, size)]
            return remote(r, r, ags.at[sem, i], agr.at[sem, i], dev)

        def start(*a):
            k = c(*a)
            k.start()
            sends.append(k)

        n = 1 - m
        settle(sends)
        start(0, p, m, 0, half, sib)
        start(1, p, m, 0, quad, xn)
        start(3, p, m, quad, quad, yn)
        start(2, p, m, quad, quad, xn)
        start(4, p, m, 0, quad, yn)
        yield name + ".0"
        c(1, px, m, 0, quad, xn).wait_recv()
        start(5, px, m, 0, quad, yn)
        c(3, py, m, quad, quad, yn).wait_recv()
        start(6, py, m, quad, quad, xn)
        yield name + ".1"
        c(2, px, m, quad, quad, xn).wait_recv()
        start(7, px, m, 0, half, sib)
        c(4, py, m, 0, quad, yn).wait_recv()
        start(8, py, m, 0, half, sib)
        c(0, p, n, 0, half, sib).wait_recv()
        c(7, px, n, 0, half, sib).wait_recv()
        near()
        yield name + ".2"
        c(5, pd, m, 0, quad, yn).wait_recv()
        start(9, pd, m, 0, quad, sib)
        c(6, pd, m, quad, quad, xn).wait_recv()
        start(10, pd, m, quad, quad, sib)
        yield name + ".3"
        c(8, py, n, 0, half, sib).wait_recv()
        c(9, pd, n, 0, quad, sib).wait_recv()
        c(10, pd, n, quad, quad, sib).wait_recv()
        far_piece()

    def scatter(s, compute, name, sends):
        def csib(i):
            return remote(so.at[s, i], si.at[s, i], rss.at[s, i], rsr.at[s, i], sib)

        def start(k):
            k.start()
            sends.append(k)

        def term(i, chip_x):
            give = pl.ds(pl.multiple_of(chip_x * HALF + (1 - m) * QUAD, QUAD), QUAD)
            hold = pl.ds(pl.multiple_of(chip_x * HALF + m * QUAD, QUAD), QUAD)
            so[s, i] = part[give, :].astype(BF16)
            start(csib(i))
            keep[s, i] = part[hold, :]

        a = slice(0, OCT)
        bb = slice(OCT, QUAD)
        chx = remote(sd.at[s, a], hx.at[s], rss.at[s, 4], rsr.at[s, 4], xn)
        chy = remote(sd.at[s, bb], hy.at[s], rss.at[s, 5], rsr.at[s, 5], yn)
        cxa = remote(sx.at[s, a], rx.at[s, a], rss.at[s, 6], rsr.at[s, 6], xn)
        cxb = remote(sx.at[s, bb], rx.at[s, bb], rss.at[s, 7], rsr.at[s, 7], xn)
        cyb = remote(sy.at[s, bb], ry.at[s, bb], rss.at[s, 8], rsr.at[s, 8], yn)
        cya = remote(sy.at[s, a], ry.at[s, a], rss.at[s, 9], rsr.at[s, 9], yn)
        settle(sends)
        compute(1 - y)
        term(0, 1 - x)
        term(2, x)
        compute(y)
        term(1, 1 - x)
        term(3, x)
        yield name + ".0"
        csib(0).wait_recv()
        sd[s] = (keep[s, 0] + si[s, 0].astype(F32)).astype(BF16)
        start(chx)
        start(chy)
        csib(1).wait_recv()
        sx[s, a, :] = (keep[s, 1, a, :] + si[s, 1, a, :].astype(F32)).astype(BF16)
        start(cxa)
        csib(2).wait_recv()
        sy[s, bb, :] = (keep[s, 2, bb, :] + si[s, 2, bb, :].astype(F32)).astype(BF16)
        start(cyb)
        yield name + ".1"
        chy.wait_recv()
        sx[s, bb, :] = (
            keep[s, 1, bb, :] + si[s, 1, bb, :].astype(F32) + hy[s].astype(F32)
        ).astype(BF16)
        start(cxb)
        chx.wait_recv()
        sy[s, a, :] = (
            keep[s, 2, a, :] + si[s, 2, a, :].astype(F32) + hx[s].astype(F32)
        ).astype(BF16)
        start(cya)
        yield name + ".2"
        csib(3).wait_recv()
        cxa.wait_recv()
        cyb.wait_recv()
        cxb.wait_recv()
        cya.wait_recv()
        return keep[s, 3] + si[s, 3].astype(F32) + rx[s].astype(F32) + ry[s].astype(F32)

    def hats(v):
        centre = v - jnp.mean(v, axis=-1, keepdims=True)
        scale = lax.rsqrt(jnp.mean(centre * centre, axis=-1, keepdims=True) + EPS_NORM)
        return centre * scale, scale

    def norm(v, i, s):
        hat, scale = hats(v)
        xh[i, s] = hat
        inv[i, s] = jnp.broadcast_to(scale, (QUAD, 128))
        return hat * nv[i : i + 1, :] + nv[5 + i : 6 + i, :]

    def norm_back(g, i, s):
        hat = xh[i, s]
        scale = inv[i, s, :, 0:1]
        gains = jnp.sum(g * hat, axis=0, keepdims=True)
        shifts = jnp.sum(g, axis=0, keepdims=True)
        if s == 0:
            ngm[i : i + 1, :] = gains
            ngm[5 + i : 6 + i, :] = shifts
        else:
            ngm[i : i + 1, :] = ngm[i : i + 1, :] + gains
            ngm[5 + i : 6 + i, :] = ngm[5 + i : 6 + i, :] + shifts
        e = g * nv[i : i + 1, :]
        return scale * (
            e
            - jnp.mean(e, axis=-1, keepdims=True)
            - hat * jnp.mean(e * hat, axis=-1, keepdims=True)
        )

    outer = 1 - inner
    c0 = 3 * (1 - z // 2)
    c1 = 2 - z // 2
    c2 = z + 1 - 2 * (z % 2)
    order = (c0, c1, c2, z)

    def grad_chunk(g, k):
        zz = order[k]
        cols = pl.ds(pl.multiple_of(zz * ROWS, ROWS), ROWS)
        if g == G_IN0:
            v = dot_tn(xg0[:, cols], hb[...])
        elif g == G_OUT0:
            v = dot_tn(xb1[:, cols], fs0[...])
        elif g == G_IN1:
            v = dot_tn(xg3[:, cols], hb[...])
        elif g == G_OUT1:
            v = dot_tn(xb0[:, cols], fs1[...])
        if g == G_ATT:
            v = dot_tn(xg1[:, cols], dqkv[...]).astype(BF16)
            for k in range(3):
                gst[g][zz, k] = v[:, k * 128 : (k + 1) * 128]
            gst[g][zz, 3] = dot_tn(xb0[:, cols], ctx[...]).astype(BF16)
        elif g == G_CONV:
            v = dot_tn(xg2[:, cols], du[...]).astype(BF16)
            for k in range(2):
                gst[g][zz, k] = v[:, k * 128 : (k + 1) * 128]
            gst[g][zz, 2] = dot_tn(xb1[:, cols], cw[...]).astype(BF16)
        else:
            gst[g][zz] = v.astype(BF16)

    neighbour = 1 + z // 2

    def acc_copy(g):
        return remote(gst[g].at[c0], acc[g], grs.at[g, 0], grr.at[g, 3], zdev(neighbour))

    def slot_copy(g, k):
        zz = order[k]
        if k == 0:
            slot = 1
        elif k == 1:
            slot = 1 + outer
        else:
            slot = 0
        return remote(gst[g].at[zz], gin[g].at[slot], grs.at[g, k], grr.at[g, slot], zdev(zz))

    def grad_send(g, k):
        if k == 0:

            @pl.when(outer == 1)
            def _():
                acc_copy(g).start()
        elif k < 3:
            slot_copy(g, k).start()

    def grad_acc(g):
        @pl.when(inner == 1)
        def _():
            acc_copy(g).wait_recv()
            gst[g][c0] = (gst[g][c0].astype(F32) + acc[g][...].astype(F32)).astype(BF16)
            slot_copy(g, 0).start()

    def gpieces(g, peer, owner):
        r = pl.ds(pl.multiple_of(peer * SHARD, SHARD), SHARD)
        if g == G_ATT:
            return (
                (gst[g].at[z, 0:3, r], gmi.at[0:3, :, columns(owner, 128)]),
                (gst[g].at[z, 3, r], gmo.at[0, :, columns(owner, 128)]),
            )
        if g == G_CONV:
            return (
                (gst[g].at[z, 0:2, r], gmi.at[3:5, :, columns(owner, 128)]),
                (gst[g].at[z, 2, r], gmo.at[1, :, columns(owner, 128)]),
            )
        dst = gfi if g in (G_IN0, G_IN1) else gfo
        layer = 0 if g in (G_IN0, G_OUT0) else 1
        return ((gst[g].at[z, r], dst.at[layer, :, columns(owner, 512)]),)

    def gplane(g):
        return [
            remote(src, dst, gas.at[g, r, k], gar.at[g, r, k], dev)
            for r, (peer, dev) in enumerate(plane)
            for k, (src, dst) in enumerate(gpieces(g, peer, p))
        ] + [
            pltpu.make_async_copy(src, dst, gas.at[g, 3, k])
            for k, (src, dst) in enumerate(gpieces(g, p, p))
        ]

    def slot_wait(g, slot):
        remote(gin[g].at[slot], gin[g].at[slot], grs.at[g, 1], grr.at[g, slot], sib).wait_recv()

    def grad_final(g):
        slot_wait(g, 0)
        slot_wait(g, 1)
        t = gst[g][z].astype(F32) + gin[g][0].astype(F32) + gin[g][1].astype(F32)
        keep_t = t

        @pl.when(outer == 1)
        def _():
            gst[g][z] = keep_t.astype(BF16)

        @pl.when(inner == 1)
        def _():
            slot_wait(g, 2)
            gst[g][z] = (keep_t + gin[g][2].astype(F32)).astype(BF16)

        for copy in gplane(g):
            copy.start()

    def grad_done(g):
        for r, (peer, dev) in enumerate(plane):
            for k, (_, dst) in enumerate(gpieces(g, peer, peer)):
                remote(dst, dst, gas.at[g, r, k], gar.at[g, r, k], dev).wait_recv()
        for i, copy in enumerate(gplane(g)):
            if i < 3 * len(gpieces(g, p, p)):
                copy.wait_send()
            else:
                copy.wait()

        @pl.when(outer == 1)
        def _():
            acc_copy(g).wait_send()

        @pl.when(inner == 1)
        def _():
            slot_copy(g, 0).wait_send()

        slot_copy(g, 1).wait_send()
        slot_copy(g, 2).wait_send()

    def line_share(buf, sem_s, sem_r, start):
        for k in range(3):
            to = others[k]
            if start:
                remote(buf.at[z], buf.at[z], sem_s.at[k], sem_r.at[2 - k], zdev(to)).start()
            else:
                frm = others[2 - k]
                remote(buf.at[z], buf.at[z], sem_s.at[k], sem_r.at[2 - k], zdev(to)).wait_send()
                remote(buf.at[frm], buf.at[frm], sem_s.at[k], sem_r.at[2 - k], zdev(frm)).wait_recv()

    stats[...] = jnp.zeros_like(stats)
    tapm[...] = jnp.zeros_like(tapm)
    ngm[10:16, :] = jnp.zeros((6, D), F32)
    lb[p, 0:1, :] = jnp.broadcast_to(lens[0:1, 0:1].astype(F32), (1, ROWS))
    lb[p, 1:2, :] = jnp.broadcast_to(lens[0:1, 1:2].astype(F32), (1, ROWS))
    lb[p, 2:8, :] = jnp.zeros((6, ROWS), F32)
    plane_start(G_IN0)
    for r in range(3):
        peer, dev = plane[r]
        remote(lb.at[p], lb.at[p], lss.at[r], lsr.at[r], dev).start()
    load = pltpu.make_async_copy(
        tok.at[pl.ds(pl.multiple_of(m * HALF, HALF), HALF)],
        xg0.at[blocks_of_chips(p, m, 0, HALF)],
        cts.at[1],
    )
    load.start()
    load.wait()

    def nothing():
        return None

    def either(here, a, b):
        @pl.when(here)
        def _():
            a()

        @pl.when(jnp.logical_not(here))
        def _():
            b()

    def cot_rows(owner_x):
        return cot.at[pl.ds(pl.multiple_of(owner_x * HALF + m * QUAD, QUAD), QUAD)]

    def cot_away():
        return remote(cot_rows(1 - x), cotb.at[x], cts.at[0], ctr.at[0], xn)

    def cot_local():
        return pltpu.make_async_copy(cot_rows(x), cotb.at[x], ctr.at[1])

    def cot_start():
        cot_away().start()
        cot_local().start()

    def cot_wait():
        cot_away().wait_send()
        remote(cotb.at[1 - x], cotb.at[1 - x], cts.at[0], ctr.at[0], xn).wait_recv()
        cot_local().wait()

    def tables():
        for r in range(3):
            peer, dev = plane[r]
            remote(lb.at[p], lb.at[p], lss.at[r], lsr.at[r], dev).wait_send()
            remote(lb.at[peer], lb.at[peer], lss.at[r], lsr.at[r], dev).wait_recv()
        place = lax.broadcasted_iota(jnp.int32, (ROWS, ROWS), 0).astype(F32)
        lane = lax.broadcasted_iota(jnp.int32, (ROWS, ROWS), 1).astype(F32)
        for b in range(4):
            l0 = lb[b % 2 * 2 + b // 2, 0:1, :]
            l1 = lb[b % 2 * 2 + b // 2, 1:2, :]
            first_in = jnp.where(place < l0, 1.0, 0.0)
            live_in = jnp.where(place < l0 + l1, 1.0, 0.0)
            at = place - l0 * (1.0 - first_in) - l1 * (1.0 - live_in)
            r = slice(b * ROWS, (b + 1) * ROWS)
            gid[r, :] = 3.0 * b + first_in[:, :128] + live_in[:, :128]
            live[r, :] = live_in[:, :128]
            hot = jnp.where(at == lane, 1.0, 0.0).astype(BF16)
            t = dot_nn(hot, rot_hi[...]) + dot_nn(hot, rot_lo[...])
            rc_t[r, :] = t[:, :128]
            rs_t[r, :] = t[:, 128:]

    first_sends = []
    opening = gather(xg0, blocks_of_chips, HALF, 2, nothing, nothing, "G0", first_sends)
    next(opening)
    line_start(G_IN0)
    next(opening)
    plane_start(G_OUT0)
    next(opening)
    tables()
    next(opening)
    line_pass(G_IN0)
    line_start(G_OUT0)
    for _ in opening:
        pass
    settle(first_sends)
    for g in (G_ATT, G_CONV, G_IN1, G_OUT1):
        plane_start(g)
    cot_start()
    for s in range(2):
        first = xg0[mine(s), :].astype(F32)
        res[s] = first
        norm(first, 0, s)

    @pl.loop(0, 8)
    def _(i):
        r = rows(i * HALF, HALF)
        hat, _ = hats(xg0[r, :].astype(F32))
        xg0[r, :] = (hat * nv[0:1, :] + nv[5:6, :]).astype(BF16)

    def block_rows(s, q):
        return pl.ds(pl.multiple_of((2 * s + q) * ROWS, ROWS), ROWS)

    def ff_hidden(s, xg, g, fh, fs):
        def f(q):
            r = block_rows(s, q)
            h = dot_nn(xg[r, :], w[g][...])
            fh[r, :] = h
            fs[r, :] = (h * sigm(h)).astype(BF16)

        return f

    def wide(g, first, last):
        return jnp.concatenate([w[g][k] for k in range(first, last)], axis=1)

    def part_nt(s, lhs, weight):
        def f(q):
            part[...] = dot_nt(lhs[block_rows(s, q), :], weight())

        return f

    def whole(g):
        return lambda: w[g][...]

    def turn(v, r):
        return v * rc_t[r, :] + pltpu.roll(v, 64, 1) * rs_t[r, :]

    def turn_back(v, r):
        return v * rc_t[r, :] - pltpu.roll(v, 64, 1) * rs_t[r, :]

    lane_row = lax.broadcasted_iota(jnp.int32, (1, ROWS), 1).astype(F32)

    def attend(s):
        def f(q):
            r = block_rows(s, q)
            b = 2 * q + s
            t = dot_nn(xg1[r, :], wide(G_ATT, 0, 3))
            qs = (turn(t[:, 0:128], r) * (HEAD_DIM**-0.5)).astype(BF16)
            k = turn(t[:, 128:256], r).astype(BF16)
            v = t[:, 256:384].astype(BF16)
            qr[r, :] = qs
            kr[r, :] = k
            vr[r, :] = v
            sc = dot_nt(qs, k)
            l0 = lb[b, 0:1, :]
            l1 = lb[b, 1:2, :]
            gk = (
                3.0 * (2 * s + q).astype(F32)
                + jnp.where(lane_row < l0, 1.0, 0.0)
                + jnp.where(lane_row < l0 + l1, 1.0, 0.0)
            )
            gq = gid[r, :]
            gq = jnp.concatenate([gq, gq], axis=1)
            sc = jnp.where(gq == gk, sc, BIG_NEG)
            e = jnp.exp(sc - jnp.max(sc, axis=-1, keepdims=True))
            pr = e / jnp.sum(e, axis=-1, keepdims=True)
            pf[r, :] = pr
            ctx[r, :] = dot_nn(pr.astype(BF16), v).astype(BF16)

        return f

    def attend_back(s):
        def f(q):
            r = block_rows(s, q)
            dc = dot_nn(xb0[r, :], w[G_ATT][3]).astype(BF16)
            pr = pf[r, :]
            k = kr[r, :]
            dp_ = dot_nt(dc, vr[r, :])
            dqkv[r, 256:384] = dot_tn(pr.astype(BF16), dc).astype(BF16)
            sb = (pr * (dp_ - jnp.sum(pr * dp_, axis=-1, keepdims=True))).astype(BF16)
            dqkv[r, 0:128] = turn_back(dot_nn(sb, k) * (HEAD_DIM**-0.5), r).astype(BF16)
            dqkv[r, 128:256] = turn_back(dot_tn(sb, qr[r, :]), r).astype(BF16)

        return f

    chan = pl.ds(pl.multiple_of(p * 128, 128), 128)
    taps = [cv[j : j + 1, chan] for j in range(KERNEL)]
    gain = cv[KERNEL : KERNEL + 1, chan]
    shift = cv[KERNEL + 1 : KERNEL + 2, chan]
    count = 2 * ROWS
    bn = {}

    def conv_in(s):
        def f(q):
            r = block_rows(s, q)
            t = dot_nn(xg2[r, :], wide(G_CONV, 0, 2))
            sig = sigm(t[:, 128:256])
            cu[r, :] = t[:, 0:128]
            sg[r, :] = sig
            glu[r, :] = t[:, 0:128] * sig

        return f

    def span(s):
        return slice(s * count, (s + 1) * count)

    def same(s, j):
        ids = gid[span(s), :]
        return jnp.where(pltpu.roll(ids, (2 - j) % count, 0) == ids, 1.0, 0.0)

    def add_row(ref, z_, row, value, s):
        at = slice(row, row + 1)
        ref[z_, at, :] = value if s == 0 else ref[z_, at, :] + value

    def mix(s):
        g_all = glu[span(s), :]
        mixed = taps[2] * g_all
        for j in (0, 1, 3, 4):
            mixed = mixed + taps[j] * pltpu.roll(g_all, (2 - j) % count, 0) * same(s, j)
        zc[span(s), :] = mixed
        lv = live[span(s), :]
        add_row(stats.at[0], z, 0, jnp.sum(lv * mixed, axis=0, keepdims=True), s)
        add_row(stats.at[0], z, 1, jnp.sum(lv * mixed * mixed, axis=0, keepdims=True), s)
        add_row(stats.at[0], z, 2, jnp.sum(lv, axis=0, keepdims=True), s)

    def bn_forward():
        line_share(stats.at[0], bns.at[0], bnr.at[0], True)
        line_pass(G_IN1)
        line_start(G_OUT1)
        line_share(stats.at[0], bns.at[0], bnr.at[0], False)
        tot = stats[0, 0] + stats[0, 1] + stats[0, 2] + stats[0, 3]
        bn["n"] = tot[2:3, :]
        bn["mean"] = tot[0:1, :] / bn["n"]
        bn["inv"] = lax.rsqrt(tot[1:2, :] / bn["n"] - bn["mean"] * bn["mean"] + EPS_NORM)

    def conv_out(s):
        def f(q):
            r = block_rows(s, q)
            v = (zc[r, :] - bn["mean"]) * bn["inv"] * gain + shift
            cw[r, :] = (v * sigm(v)).astype(BF16)
            part[...] = dot_nt(cw[r, :], w[G_CONV][2])

        return f

    def conv_back(s):
        def f(q):
            r = block_rows(s, q)
            v = (zc[r, :] - bn["mean"]) * bn["inv"] * gain + shift
            sig = sigm(v)
            dd[r, :] = dot_nn(xb1[r, :], w[G_CONV][2]) * sig * (1.0 + v * (1.0 - sig))

        return f

    def batch_sums(s):
        d_all = dd[span(s), :]
        add_row(stats.at[1], z, 0, jnp.sum(d_all, axis=0, keepdims=True), s)
        centred = zc[span(s), :] - bn["mean"]
        add_row(stats.at[1], z, 1, jnp.sum(d_all * centred, axis=0, keepdims=True), s)

    def bn_backward():
        line_share(stats.at[1], bns.at[1], bnr.at[1], True)
        for k in range(4):
            grad_chunk(G_IN1, k)
        line_share(stats.at[1], bns.at[1], bnr.at[1], False)
        tot = stats[1, 0] + stats[1, 1] + stats[1, 2] + stats[1, 3]
        i = bn["inv"]
        bn["s1"] = tot[0:1, :]
        bn["s2"] = tot[1:2, :]
        bn["dv"] = -0.5 * i * i * i * gain * bn["s2"]
        bn["dm"] = -i * gain * bn["s1"] - 2.0 * bn["mean"] * bn["dv"]

    def unmix(s):
        r = span(s)
        dz = dd[r, :] * (gain * bn["inv"]) + live[r, :] * (
            (bn["dm"] + 2.0 * zc[r, :] * bn["dv"]) / bn["n"]
        )
        g_all = glu[r, :]
        back = jnp.zeros_like(dz)
        for j in range(KERNEL):
            if j == 2:
                weighted = dz
                moved = g_all
            else:
                weighted = dz * same(s, j)
                moved = pltpu.roll(g_all, (2 - j) % count, 0)
            add_row(tapm, z, j, jnp.sum(weighted * moved, axis=0, keepdims=True), s)
            weighted = taps[j] * weighted
            if j != 2:
                weighted = pltpu.roll(weighted, (j - 2) % count, 0)
            back = back + weighted
        s_all = sg[r, :]
        du[r, 0:128] = (back * s_all).astype(BF16)
        du[r, 128:256] = (back * cu[r, :] * s_all * (1.0 - s_all)).astype(BF16)

    def ff_back(s, xb, g, fh):
        def f(q):
            r = block_rows(s, q)
            h = fh[r, :]
            sig = sigm(h)
            d = dot_nn(xb[r, :], w[g][...])
            hb[r, :] = (d * sig * (1.0 + h * (1.0 - sig))).astype(BF16)

        return f

    def out_rows(out, owner_x, core):
        return out.at[pl.ds(pl.multiple_of(owner_x * HALF + core * QUAD, QUAD), QUAD)]

    def give_out(i, s, out):
        there = out_rows(out, x, m)
        src = tstage.at[i, s]
        r_sem = outr.at[i, x, m]

        def a():
            pltpu.make_async_copy(src, there, r_sem).start()
            remote(src, there, outs.at[i, s, 0], r_sem, sib).start()

        def b():
            remote(src, there, outs.at[i, s, 0], r_sem, xn).start()
            remote(src, there, outs.at[i, s, 1], r_sem, (base + px, 1 - m)).start()

        either(x == s, a, b)

    def out_wait(i, out):
        there = out_rows(out, x, m)
        for s in range(2):
            src = tstage.at[i, s]
            remote(src, there, outs.at[i, s, 0], outr.at[i, x, m], xn).wait_send()

            @pl.when(x != s)
            def _():
                remote(src, there, outs.at[i, s, 1], outr.at[i, x, m], xn).wait_send()

        for cx in range(2):
            for cm in range(2):
                here = out.at[cx * HALF + cm * QUAD : cx * HALF + (cm + 1) * QUAD]
                remote(here, here, outs.at[i, 0, 0], outr.at[i, cx, cm], sib).wait_recv()

    def stream(s):
        g_sends = []
        r_sends = []
        at = mine(s)

        def take(xg, compute, name, ready=None):
            def near():
                if ready is not None and s == 0:
                    line_ready(ready)
                compute(y)

            return gather(xg, pieces(s), QUAD, s, near, lambda: compute(1 - y), name, g_sends)

        def give(compute, name):
            return scatter(s, compute, name, r_sends)

        hidden = ff_hidden(s, xg0, G_IN0, fh0, fs0)
        hidden(0)
        hidden(1)
        yield "W"
        t = yield from give(part_nt(s, fs0, whole(G_OUT0)), "R0")
        v = res[s] + 0.5 * t
        res[s] = v
        xg1[at, :] = norm(v, 1, s).astype(BF16)
        yield from take(xg1, attend(s), "G1", G_ATT)
        t = yield from give(part_nt(s, ctx, lambda: w[G_ATT][3]), "R1")
        v = res[s] + t
        res[s] = v
        xg2[at, :] = norm(v, 2, s).astype(BF16)
        yield from take(xg2, conv_in(s), "G2", G_CONV)
        mix(s)
        yield "BN1"
        t = yield from give(conv_out(s), "R2")
        v = res[s] + t
        res[s] = v
        xg3[at, :] = norm(v, 3, s).astype(BF16)
        yield from take(xg3, ff_hidden(s, xg3, G_IN1, fh1, fs1), "G3", G_IN1)
        if s == 0:
            line_ready(G_OUT1)
        t = yield from give(part_nt(s, fs1, whole(G_OUT1)), "R3")
        tstage[0, s] = norm(res[s] + 0.5 * t, 4, s).astype(BF16)
        if s == 0:
            cot_wait()
        v = norm_back(cotb[s].astype(F32), 4, s)
        res[s] = v
        xb0[at, :] = (0.5 * v).astype(BF16)
        yield from take(xb0, ff_back(s, xb0, G_OUT1, fh1), "H3")
        t = yield from give(part_nt(s, hb, whole(G_IN1)), "Q3")
        v = res[s] + norm_back(t, 3, s)
        res[s] = v
        xb1[at, :] = v.astype(BF16)
        yield from take(xb1, conv_back(s), "H2")
        batch_sums(s)
        yield "BN2"
        unmix(s)
        yield "TAPS"
        t = yield from give(part_nt(s, du, lambda: wide(G_CONV, 0, 2)), "Q2")
        v = res[s] + norm_back(t, 2, s)
        res[s] = v
        xb0[at, :] = v.astype(BF16)
        yield from take(xb0, attend_back(s), "H1")
        t = yield from give(part_nt(s, dqkv, lambda: wide(G_ATT, 0, 3)), "Q1")
        v = res[s] + norm_back(t, 1, s)
        res[s] = v
        xb1[at, :] = (0.5 * v).astype(BF16)
        yield from take(xb1, ff_back(s, xb1, G_OUT0, fh0), "H0")
        yield "TAIL"
        t = yield from give(part_nt(s, hb, whole(G_IN0)), "Q0")
        tstage[1, s] = (res[s] + norm_back(t, 0, s)).astype(BF16)
        give_out(1, s, tgrad)
        settle(g_sends)
        settle(r_sends)

    queue = []

    def chunks(g, send):
        def one(k):
            def f():
                grad_chunk(g, k)
                if send:
                    grad_send(g, k)

            return f

        return [one(k) for k in range(4)]

    def first_feed():
        line_pass(G_OUT0)
        line_start(G_ATT)
        line_ready(G_OUT0)

    def tap_share():
        line_share(tapm, bns.at[2], bnr.at[2], True)
        for k in range(3):
            grad_send(G_IN1, k)

    def tail():
        for f in chunks(G_OUT0, True) + chunks(G_IN0, True):
            f()
        for s in range(2):
            give_out(0, s, tout)

    def passing(g, following):
        def f():
            line_pass(g)
            if following is not None:
                line_start(following)

        return f

    meet = {
        "W": first_feed, "BN1": bn_forward, "BN2": bn_backward, "TAPS": tap_share, "TAIL": tail,
    }
    after = {
        "R0.2": [passing(G_ATT, G_CONV)],
        "R1.1": [passing(G_CONV, G_IN1)],
        "G3.0": [passing(G_OUT1, None)],
        "Q3.0": chunks(G_OUT1, True),
        "H2.0": [lambda: grad_acc(G_OUT1)],
        "Q2.0": chunks(G_CONV, True),
        "Q2.2": [lambda: grad_acc(G_IN1)],
        "H1.1": [lambda: grad_final(G_OUT1)],
        "H1.2": [lambda: grad_acc(G_CONV)],
        "Q1.0": chunks(G_ATT, True),
        "Q1.2": [lambda: grad_final(G_IN1)],
        "H0.1": [lambda: grad_acc(G_ATT)],
        "H0.2": [lambda: grad_final(G_CONV)],
        "Q0.1": [lambda: grad_acc(G_OUT0)],
    }
    line_ready(G_IN0)
    streams = [stream(0), stream(1)]
    state = ["", ""]
    while streams[1] is not None:
        for s in range(2):
            if streams[s] is None:
                continue
            try:
                state[s] = next(streams[s])
            except StopIteration:
                streams[s] = None
                continue
            if s == 1:
                queue.extend(after.get(state[s], []))
            if queue:
                queue.pop(0)()
            if s == 1 and state[s] in meet:
                while queue:
                    queue.pop(0)()
                meet[state[s]]()
    while queue:
        queue.pop(0)()
    grad_final(G_ATT)
    grad_acc(G_IN0)

    def swap(src, dst, k, dev):
        copy = remote(src, dst, nss.at[k], nsr.at[k], dev)
        copy.start()
        copy.wait()

    swap(ngm, nsib, 0, sib)
    ngm[...] = ngm[...] + nsib[...]
    swap(ngm, nx, 1, xn)
    ngm[...] = ngm[...] + nx[...]
    swap(ngm, ny, 2, yn)
    nz[z] = ngm[...] + ny[...]
    line_share(nz, nss.at[pl.ds(3, 3)], nsr.at[pl.ds(3, 3)], True)
    line_share(tapm, bns.at[2], bnr.at[2], False)
    cgm[...] = tapm[0] + tapm[1] + tapm[2] + tapm[3]
    cgm[5:6, :] = bn["inv"] * bn["s2"]
    cgm[6:7, :] = bn["s1"]
    cgrad[:, chan] = cgm[...]
    for r in range(3):
        remote(cgm, cgrad.at[:, chan], cgs.at[r], cgr.at[r], plane[r][1]).start()
    grad_final(G_OUT0)
    line_share(nz, nss.at[pl.ds(3, 3)], nsr.at[pl.ds(3, 3)], False)
    ngrad[...] = nz[0] + nz[1] + nz[2] + nz[3]
    for r in range(3):
        peer, dev = plane[r]
        there = cgrad.at[:, pl.ds(pl.multiple_of(peer * 128, 128), 128)]
        remote(there, there, cgs.at[r], cgr.at[r], dev).wait_recv()
        remote(cgm, cgrad.at[:, chan], cgs.at[r], cgr.at[r], dev).wait_send()
    grad_final(G_IN0)
    out_wait(0, tout)
    out_wait(1, tgrad)
    for copy in pending:
        copy.wait_send()
    for g in range(6):
        line_done(g)
        grad_done(g)


def group_shape(g, rows):
    if g == G_ATT:
        return (4, rows, 128)
    if g == G_CONV:
        return (3, rows, 128)
    return (rows, 512)


def rotation_tables():
    half = HEAD_DIM // 2
    frequency = np.exp(np.arange(half, dtype=np.float32) * np.float32(-2.0 * math.log(10000.0) / HEAD_DIM))
    angles = np.arange(ROWS, dtype=np.float32)[:, None] * frequency.astype(np.float32)[None, :]
    c = np.cos(angles.astype(np.float64))
    s = np.sin(angles.astype(np.float64))
    table = np.concatenate([c, c, -s, s], axis=1).astype(np.float32)
    high = table.astype(BF16)
    low_part = (table - high.astype(np.float32)).astype(BF16)
    return high, low_part


def fused_call(tok, cot, lens, norm_vectors, channel_vectors, fi, fo, mi, mo):
    high, low_part = rotation_tables()
    vm = pl.BlockSpec(memory_space=pltpu.VMEM)
    hbm = pl.BlockSpec(memory_space=pl.ANY)

    def v(shape, dtype):
        return pltpu.VMEM(shape, dtype)

    t16 = (4 * ROWS, D)
    h16 = (4 * ROWS, 512)
    c16 = (4 * ROWS, 128)
    shapes = ((2, SHARD, 2048), (2, SHARD, 2048), (5, SHARD, 512), (2, SHARD, 512))
    scratch = [v(k, F32) for k in shapes] + [v(k, BF16) for k in shapes]
    scratch += [v(group_shape(g, D), BF16) for g in range(6)]
    scratch += [v(t16, BF16)] * 6
    scratch += [v(h16, F32)] * 2 + [v(h16, BF16)] * 3
    scratch += [v(c16, BF16)] * 4 + [v((4 * ROWS, 384), BF16), v((4 * ROWS, ROWS), F32)]
    scratch += [v(c16, F32)] * 5 + [v(c16, BF16), v((4 * ROWS, 256), BF16)]
    scratch += [v(c16, F32)] * 4 + [v((4, 8, ROWS), F32)]
    scratch += [v((5, 2, QUAD, D), F32), v((5, 2, QUAD, 128), F32), v((2, QUAD, D), F32)]
    scratch += [v((2, 4, QUAD, D), BF16)] * 2 + [v((2, QUAD, D), BF16)] + [v((2, OCT, D), BF16)] * 2
    scratch += [v((2, QUAD, D), BF16)] * 4 + [v((2, 4, QUAD, D), F32), v((ROWS, D), F32)]
    scratch += [v((4,) + group_shape(g, ROWS), BF16) for g in range(6)]
    scratch += [v((3,) + group_shape(g, ROWS), BF16) for g in range(6)]
    scratch += [v(group_shape(g, ROWS), BF16) for g in range(6)]
    scratch += [v((2, 4, 8, 128), F32), v((4, 8, 128), F32)]
    scratch += [v((16, D), F32)] * 4 + [v((4, 16, D), F32), v((8, 128), F32), v((2, 2, QUAD, D), BF16)]
    scratch += [v((2, QUAD, D), BF16)]
    dma = pltpu.SemaphoreType.DMA
    sems = [(3, 11), (3, 11), (2, 10), (2, 10), (6, 4, 2), (6, 4, 2), (6, 4), (6, 4), (6, 4), (6, 4)]
    sems += [(6, 4, 2), (6, 4, 2), (3,), (3,), (3, 3), (3, 3), (6,), (6,), (3,), (3,), (2, 2, 2), (2, 2, 2), (2,), (2,), (6, 2)]
    scratch += [dma(k) for k in sems]
    out_shape = (
        jax.ShapeDtypeStruct((ROWS, D), BF16),
        jax.ShapeDtypeStruct((ROWS, D), BF16),
        jax.ShapeDtypeStruct((2, SHARD, 2048), BF16),
        jax.ShapeDtypeStruct((2, SHARD, 2048), BF16),
        jax.ShapeDtypeStruct((5, SHARD, 512), BF16),
        jax.ShapeDtypeStruct((2, SHARD, 512), BF16),
        jax.ShapeDtypeStruct((16, D), F32),
        jax.ShapeDtypeStruct((8, 512), F32),
    )
    return pl.pallas_call(
        fused_kernel,
        out_shape=out_shape,
        in_specs=[hbm, hbm] + [vm] * 5 + [hbm] * 4,
        out_specs=(hbm,) * 6 + (vm, vm),
        scratch_shapes=scratch,
        compiler_params=pltpu.CompilerParams(
            collective_id=0, has_side_effects=True, vmem_limit_bytes=63 * 2**20
        ),
    )(tok, cot, lens, jnp.asarray(high), jnp.asarray(low_part), norm_vectors, channel_vectors, fi, fo, mi, mo)


def update_kernel(*refs):
    to, tg, gfi, gfo, gmi, gmo, ng, cg = refs[:8]
    state = [refs[8 + 3 * k : 11 + 3 * k] for k in range(6)]
    out = refs[26:]
    out[0][...] = to[...].astype(F32)
    out[1][...] = tg[...].astype(F32)
    rates = (D**-0.5, FF**-0.5, D**-0.5, None, 0.3, 0.3)

    def step(k, at, gradient, rate):
        weight, mean, square = (r[at] for r in state[k])
        return adamw_step(weight, mean, square, gradient.astype(F32), rate)

    for k, g in ((0, gfi), (1, gfo)):
        for layer in range(2):
            new = step(k, layer, g[layer], rates[k])
            for i in range(3):
                out[2 + 3 * k + i][layer] = new[i]
    for layer in range(5):
        a, b, c = step(2, layer, gmi[layer], rates[2])
        out[8][layer] = a
        out[9][layer] = b
        if layer < 4:
            out[10][layer] = c
        else:
            out[11][...] = c
    for layer in range(2):
        rate = (max(2 * D // TOK_DEV, 1) ** -0.5, D**-0.5)[layer]
        new = step(3, layer, gmo[layer], rate)
        for i in range(3):
            out[12 + i][layer] = new[i]
    for k, g, n in ((4, ng, 10), (5, cg, 7)):
        new = step(k, slice(0, n), g[0:n, :], rates[k])
        for i in range(3):
            out[3 + 3 * k + i][...] = new[i]


def update_call(grads, *states):
    steps = 4
    r = SHARD // steps

    def stacked(layers, width):
        return pl.BlockSpec((layers, r, width), lambda i: (0, i, 0))

    def fixed(a, b):
        return pl.BlockSpec((a, b), lambda i: (0, 0))

    frames = pl.BlockSpec((ROWS // steps, D), lambda i: (i, 0))
    big = [stacked(2, 2048), stacked(2, 2048), stacked(5, 512), stacked(2, 512)]
    small = [fixed(10, D), fixed(7, 512)]
    in_specs = [frames, frames] + big + [fixed(16, D), fixed(8, 512)]
    out_specs = [frames, frames]
    out_shape = [jax.ShapeDtypeStruct((ROWS, D), F32)] * 2
    flat = list(grads)
    for k, three in enumerate(states):
        spec = (big + small)[k]
        for i, a in enumerate(three):
            flat.append(a)
            in_specs.append(spec)
            if k == 2 and i == 2:
                out_specs += [stacked(4, 512), pl.BlockSpec((r, 512), lambda i: (i, 0))]
                out_shape += [
                    jax.ShapeDtypeStruct((4, SHARD, 512), F32),
                    jax.ShapeDtypeStruct((SHARD, 512), F32),
                ]
            else:
                out_specs.append(spec)
                out_shape.append(jax.ShapeDtypeStruct(a.shape, F32))
    return pl.pallas_call(
        update_kernel,
        grid=(steps,),
        in_specs=in_specs,
        out_specs=out_specs,
        out_shape=out_shape,
        compiler_params=pltpu.CompilerParams(vmem_limit_bytes=63 * 2**20),
    )(*flat)


def fast_body(
    tokens_in, out_cotangent, utt_lengths,
    feed_in, feed_in_mean, feed_in_square,
    feed_out, feed_out_mean, feed_out_square,
    mixer_in, mixer_in_mean, mixer_in_square,
    mixer_out, mixer_out_mean, mixer_out_square,
    norm_vectors, norm_vectors_mean, norm_vectors_square,
    channel_vectors, channel_vectors_mean, channel_vectors_square,
):
    fo_t = jnp.swapaxes(feed_out, 1, 2)
    mo_t = jnp.swapaxes(mixer_out, 1, 2)
    tokens_out, tokens_grad, gfi, gfo, gmi, gmo, ngrad, cgrad = fused_call(
        tokens_in, out_cotangent, utt_lengths, norm_vectors, channel_vectors,
        feed_in, fo_t, mixer_in, mo_t,
    )

    def turned(v):
        return jnp.swapaxes(v, 1, 2)

    new = update_call(
        (tokens_out, tokens_grad, gfi, gfo, gmi, gmo, ngrad, cgrad),
        (feed_in, feed_in_mean, feed_in_square),
        (fo_t, turned(feed_out_mean), turned(feed_out_square)),
        (mixer_in, mixer_in_mean, mixer_in_square),
        (mo_t, turned(mixer_out_mean), turned(mixer_out_square)),
        (norm_vectors, norm_vectors_mean, norm_vectors_square),
        (channel_vectors, channel_vectors_mean, channel_vectors_square),
    )
    new = list(new)
    for k in (5, 6, 7, 12, 13, 14):
        new[k] = turned(new[k])
    return tuple(new)


def solution(mesh):
    fits = mesh.shape["dp"] == 16 and mesh.shape["mp"] == 2
    placed = (
        P("dp", None),
        P("dp", None),
        P("dp", None),
        P(None, "dp", "mp"),
        P(None, "dp", "mp"),
        P(None, "dp", "mp"),
        P(None, "mp", "dp"),
        P(None, "mp", "dp"),
        P(None, "mp", "dp"),
        P(None, "dp", "mp"),
        P(None, "dp", "mp"),
        P(None, "dp", "mp"),
        P(None, "mp", "dp"),
        P(None, "mp", "dp"),
        P(None, "mp", "dp"),
        P(),
        P(),
        P(),
        P(None, "mp"),
        P(None, "mp"),
        P(None, "mp"),
    )
    return jax.shard_map(
        fast_body if fits else body,
        mesh=mesh,
        in_specs=placed,
        out_specs=(
            P("dp", None),
            P("dp", None),
            P(None, "dp", "mp"),
            P(None, "dp", "mp"),
            P(None, "dp", "mp"),
            P(None, "mp", "dp"),
            P(None, "mp", "dp"),
            P(None, "mp", "dp"),
            P(None, "dp", "mp"),
            P(None, "dp", "mp"),
            P(None, "dp", "mp"),
            P("dp", "mp"),
            P(None, "mp", "dp"),
            P(None, "mp", "dp"),
            P(None, "mp", "dp"),
            P(),
            P(),
            P(),
            P(None, "mp"),
            P(None, "mp"),
            P(None, "mp"),
        ),
        check_vma=False,
    )
```

```python
import math

import jax
import jax.numpy as jnp
import numpy as np
from jax import lax
from jax.experimental import pallas as pl
from jax.experimental.pallas import tpu as pltpu
from jax.sharding import PartitionSpec as P

D = 1024
FF = 4096
HEAD_DIM = 128
KERNEL = 5
STEP_COUNT = 3
TOK_DEV = 256


EPS_NORM = 1e-05
EPS_ADAM = 1e-08
DECAY_WEIGHT = 0.01
BETA = 0.5
BIG_NEG = -1e30


def product(left_side, right_side):
    return jnp.dot(left_side, right_side, preferred_element_type=jnp.float32)


def weight_grad(inputs, gradients):
    return lax.dot_general(
        inputs, gradients, (((0,), (0,)), ((), ())), preferred_element_type=jnp.float32
    )


def input_grad(gradients, weight):
    return lax.dot_general(
        gradients, weight, (((1,), (1,)), ((), ())), preferred_element_type=jnp.float32
    )


def norm_forward(values, gain_row, shift_row):
    centre = values - jnp.mean(values, axis=-1, keepdims=True)
    inverse = lax.rsqrt(jnp.mean(centre * centre, axis=-1, keepdims=True) + EPS_NORM)
    scaled = centre * inverse
    return (scaled * gain_row + shift_row, scaled, inverse)


def norm_backward(grad_out, scaled, inverse, gain_row):
    grad_gain = jnp.sum(grad_out * scaled, axis=0)
    grad_shift = jnp.sum(grad_out, axis=0)
    grad_scaled = grad_out * gain_row
    grad_in = inverse * (
        grad_scaled
        - jnp.mean(grad_scaled, axis=-1, keepdims=True)
        - scaled * jnp.mean(grad_scaled * scaled, axis=-1, keepdims=True)
    )
    return (grad_in, grad_gain, grad_shift)


def rotate(values, cosine, sine_part):
    halfway = values.shape[-1] // 2
    front_half = values[..., :halfway]
    back_half = values[..., halfway:]
    return jnp.concatenate(
        [front_half * cosine - back_half * sine_part, front_half * sine_part + back_half * cosine],
        axis=-1,
    )


def unrotate(values, cosine, sine_part):
    halfway = values.shape[-1] // 2
    front_half = values[..., :halfway]
    back_half = values[..., halfway:]
    return jnp.concatenate(
        [front_half * cosine + back_half * sine_part, back_half * cosine - front_half * sine_part],
        axis=-1,
    )


def depthwise(gated_rows, kernel, group_ids):
    count_rows = gated_rows.shape[0]
    reach = KERNEL // 2
    padded = jnp.pad(gated_rows, ((reach, reach), (0, 0)))
    padded_ids = jnp.pad(group_ids, (reach, reach), constant_values=-1)
    summed = jnp.zeros_like(gated_rows)
    for offset in range(KERNEL):
        matched = (padded_ids[offset : offset + count_rows] == group_ids).astype(jnp.float32)
        summed = summed + kernel[offset] * padded[offset : offset + count_rows] * matched[:, None]
    return summed


def depthwise_back(grad_mixed, gated_rows, kernel, group_ids):
    count_rows = gated_rows.shape[0]
    reach = KERNEL // 2
    padded = jnp.pad(gated_rows, ((reach, reach), (0, 0)))
    padded_ids = jnp.pad(group_ids, (reach, reach), constant_values=-1)
    grad_padded = jnp.zeros_like(padded)
    kernel_rows = []
    for offset in range(KERNEL):
        matched = (padded_ids[offset : offset + count_rows] == group_ids).astype(jnp.float32)
        weighted = grad_mixed * matched[:, None]
        kernel_rows.append(jnp.sum(weighted * padded[offset : offset + count_rows], axis=0))
        grad_padded = grad_padded.at[offset : offset + count_rows].add(kernel[offset] * weighted)
    return (jnp.stack(kernel_rows), grad_padded[reach : reach + count_rows])


def rate_table():
    attention_fan = max(2 * D // TOK_DEV, 1)
    mixer_rates = jnp.array([attention_fan ** (-0.5), D ** (-0.5)], dtype=jnp.float32)[
        :, None, None
    ]
    return (D ** (-0.5), FF ** (-0.5), D ** (-0.5), mixer_rates, 0.3, 0.3)


def adamw_step(weight, mean_state, square_state, gradient, step_rate):
    mean_next = BETA * mean_state + (1.0 - BETA) * gradient
    square_next = BETA * square_state + (1.0 - BETA) * gradient * gradient
    correct = 1.0 - BETA**STEP_COUNT
    direction = mean_next / correct / (jnp.sqrt(square_next / correct) + EPS_ADAM)
    return (weight - step_rate * (direction + DECAY_WEIGHT * weight), mean_next, square_next)


def branch_total(partial_sum):
    return lax.psum(partial_sum.astype(jnp.bfloat16), "mp").astype(jnp.float32)


def input_total(partial_sum):
    return lax.psum(partial_sum.astype(jnp.bfloat16), "mp").astype(jnp.float32)


def body(
    tokens_in,
    out_cotangent,
    utt_lengths,
    feed_in,
    feed_in_mean,
    feed_in_square,
    feed_out,
    feed_out_mean,
    feed_out_square,
    mixer_in,
    mixer_in_mean,
    mixer_in_square,
    mixer_out,
    mixer_out_mean,
    mixer_out_square,
    norm_vectors,
    norm_vectors_mean,
    norm_vectors_square,
    channel_vectors,
    channel_vectors_mean,
    channel_vectors_square,
):
    count_rows = tokens_in.shape[0]
    local_width = mixer_in.shape[2]
    local_heads = local_width // HEAD_DIM
    heads_shape = (count_rows, local_heads, HEAD_DIM)
    score_scale = HEAD_DIM ** (-0.5)
    first_len = utt_lengths[0, 0]
    second = utt_lengths[0, 1]
    places = jnp.arange(count_rows, dtype=jnp.int32)
    in_first = (places < first_len).astype(jnp.int32)
    in_live = (places < first_len + second).astype(jnp.int32)
    group_ids = in_first + in_live
    positions = places - first_len * (1 - in_first) - second * (1 - in_live)
    live_rows = in_live.astype(jnp.float32)[:, None]
    halfway = HEAD_DIM // 2
    frequency = jnp.exp(
        jnp.arange(halfway, dtype=jnp.float32) * (-2.0 * math.log(10000.0) / HEAD_DIM)
    )
    angles = positions.astype(jnp.float32)[:, None] * frequency[None, :]
    cosine = jnp.cos(angles)[:, None, :]
    sine_part = jnp.sin(angles)[:, None, :]
    allowed = (group_ids[:, None] == group_ids[None, :])[None]
    kernel = channel_vectors[:KERNEL]
    batch_gain = channel_vectors[KERNEL]
    batch_shift = channel_vectors[KERNEL + 1]
    weight_in, weight_out, weight_mix, weight_back = (
        lax.all_gather(feed_in.astype(jnp.bfloat16), "dp", axis=1, tiled=True),
        lax.all_gather(feed_out.astype(jnp.bfloat16), "dp", axis=2, tiled=True),
        lax.all_gather(mixer_in.astype(jnp.bfloat16), "dp", axis=1, tiled=True),
        lax.all_gather(mixer_out.astype(jnp.bfloat16), "dp", axis=2, tiled=True),
    )

    def feed_forward(residual, norm_slot, feed_layer):
        normed, scaled, inverse = norm_forward(
            residual, norm_vectors[norm_slot], norm_vectors[5 + norm_slot]
        )
        normed_low = normed.astype(jnp.bfloat16)
        hidden = product(normed_low, weight_in[feed_layer])
        active = (hidden * jax.nn.sigmoid(hidden)).astype(jnp.bfloat16)
        branch = branch_total(product(active, weight_out[feed_layer]))
        return (residual + 0.5 * branch, (scaled, inverse, normed_low, hidden, active))

    section_zero = tokens_in.astype(jnp.float32)
    section_one, kept_first = feed_forward(section_zero, 0, 0)
    normed, scaled_att, inverse_att = norm_forward(section_one, norm_vectors[1], norm_vectors[6])
    normed_att = normed.astype(jnp.bfloat16)
    projected = jnp.einsum(
        "td,sdc->stc", normed_att, weight_mix[:3], preferred_element_type=jnp.float32
    )
    queries = (rotate(projected[0].reshape(heads_shape), cosine, sine_part) * score_scale).astype(
        jnp.bfloat16
    )
    key_rows = rotate(projected[1].reshape(heads_shape), cosine, sine_part).astype(jnp.bfloat16)
    value_rows = projected[2].reshape(heads_shape).astype(jnp.bfloat16)
    scores = jnp.where(
        allowed,
        jnp.einsum("qhd,khd->hqk", queries, key_rows, preferred_element_type=jnp.float32),
        BIG_NEG,
    )
    largest = jnp.max(scores, axis=-1, keepdims=True)
    exponent = jnp.exp(scores - largest)
    totals = jnp.sum(exponent, axis=-1, keepdims=True)
    softmax_rows = exponent / totals
    log_total = largest + jnp.log(totals)
    context = jnp.einsum(
        "hqk,khd->qhd",
        softmax_rows.astype(jnp.bfloat16),
        value_rows,
        preferred_element_type=jnp.float32,
    )
    context_low = context.reshape(count_rows, local_width).astype(jnp.bfloat16)
    section_two = section_one + branch_total(product(context_low, weight_back[0]))
    normed, scaled_conv, inverse_conv = norm_forward(section_two, norm_vectors[2], norm_vectors[7])
    normed_conv = normed.astype(jnp.bfloat16)
    conv_proj = jnp.einsum(
        "td,sdc->stc", normed_conv, weight_mix[3:], preferred_element_type=jnp.float32
    )
    gate_sig = jax.nn.sigmoid(conv_proj[1])
    gated_rows = conv_proj[0] * gate_sig
    mixed_rows = depthwise(gated_rows, kernel, group_ids)
    batch_stats = lax.psum(
        (
            jnp.sum(live_rows * mixed_rows, axis=0),
            jnp.sum(live_rows * mixed_rows * mixed_rows, axis=0),
            jnp.sum(live_rows),
        ),
        "dp",
    )
    count_live = batch_stats[2]
    mean_batch = batch_stats[0] / count_live
    inverse_batch = lax.rsqrt(batch_stats[1] / count_live - mean_batch * mean_batch + EPS_NORM)
    centred = mixed_rows - mean_batch
    batch_out = centred * inverse_batch * batch_gain + batch_shift
    batch_sig = jax.nn.sigmoid(batch_out)
    active_conv = (batch_out * batch_sig).astype(jnp.bfloat16)
    section_three = section_two + branch_total(product(active_conv, weight_back[1]))
    section_four, kept_second = feed_forward(section_three, 3, 1)
    tokens_out, scaled_last, inverse_last = norm_forward(
        section_four, norm_vectors[4], norm_vectors[9]
    )

    def feed_backward(grad_residual, kept, norm_slot, feed_layer):
        scaled, inverse, normed_low, hidden, active = kept
        grad_branch = (0.5 * grad_residual).astype(jnp.bfloat16)
        grad_down = weight_grad(active, grad_branch)
        hidden_sig = jax.nn.sigmoid(hidden)
        grad_hidden = (
            input_grad(grad_branch, weight_out[feed_layer])
            * hidden_sig
            * (1.0 + hidden * (1.0 - hidden_sig))
        ).astype(jnp.bfloat16)
        grad_up = weight_grad(normed_low, grad_hidden)
        grad_normed = input_total(input_grad(grad_hidden, weight_in[feed_layer]))
        grad_in, grad_gain, grad_shift = norm_backward(
            grad_normed, scaled, inverse, norm_vectors[norm_slot]
        )
        return (grad_residual + grad_in, grad_up, grad_down, grad_gain, grad_shift)

    grad_residual, gain_last, shift_last = norm_backward(
        out_cotangent.astype(jnp.float32), scaled_last, inverse_last, norm_vectors[4]
    )
    grad_residual, up_second, down_second, gain_three, shift_three = feed_backward(
        grad_residual, kept_second, 3, 1
    )
    grad_branch = grad_residual.astype(jnp.bfloat16)
    grad_conv_down = weight_grad(active_conv, grad_branch)
    grad_batch = (
        input_grad(grad_branch, weight_back[1]) * batch_sig * (1.0 + batch_out * (1.0 - batch_sig))
    )
    batch_sums = lax.psum(
        (jnp.sum(grad_batch, axis=0), jnp.sum(grad_batch * centred, axis=0)), "dp"
    )
    grad_var = -0.5 * inverse_batch**3 * batch_gain * batch_sums[1]
    grad_mean = -inverse_batch * batch_gain * batch_sums[0] - 2.0 * mean_batch * grad_var
    grad_mixed = (
        grad_batch * batch_gain * inverse_batch
        + live_rows * (grad_mean + 2.0 * mixed_rows * grad_var) / count_live
    )
    kernel_grads, grad_gated = depthwise_back(grad_mixed, gated_rows, kernel, group_ids)
    grad_conv_up = jnp.stack(
        [grad_gated * gate_sig, grad_gated * conv_proj[0] * gate_sig * (1.0 - gate_sig)]
    ).astype(jnp.bfloat16)
    grad_conv_in = jnp.einsum(
        "td,stc->sdc", normed_conv, grad_conv_up, preferred_element_type=jnp.float32
    )
    grad_normed = input_total(
        jnp.einsum("stc,sdc->td", grad_conv_up, weight_mix[3:], preferred_element_type=jnp.float32)
    )
    grad_in, gain_two, shift_two = norm_backward(
        grad_normed, scaled_conv, inverse_conv, norm_vectors[2]
    )
    grad_residual = grad_residual + grad_in
    grad_branch = grad_residual.astype(jnp.bfloat16)
    grad_att_down = weight_grad(context_low, grad_branch)
    grad_context = input_grad(grad_branch, weight_back[0]).astype(jnp.bfloat16).reshape(heads_shape)
    scores_again = jnp.where(
        allowed,
        jnp.einsum("qhd,khd->hqk", queries, key_rows, preferred_element_type=jnp.float32),
        BIG_NEG,
    )
    softmax_again = jnp.exp(scores_again - log_total)
    grad_softmax = jnp.einsum(
        "qhd,khd->hqk", grad_context, value_rows, preferred_element_type=jnp.float32
    )
    grad_values = jnp.einsum(
        "hqk,qhd->khd",
        softmax_again.astype(jnp.bfloat16),
        grad_context,
        preferred_element_type=jnp.float32,
    )
    grad_scores = (
        softmax_again
        * (grad_softmax - jnp.sum(softmax_again * grad_softmax, axis=-1, keepdims=True))
    ).astype(jnp.bfloat16)
    grad_queries = unrotate(
        jnp.einsum("hqk,khd->qhd", grad_scores, key_rows, preferred_element_type=jnp.float32)
        * score_scale,
        cosine,
        sine_part,
    )
    grad_keys = unrotate(
        jnp.einsum("hqk,qhd->khd", grad_scores, queries, preferred_element_type=jnp.float32),
        cosine,
        sine_part,
    )
    grad_att_up = (
        jnp.stack([grad_queries, grad_keys, grad_values])
        .reshape(3, count_rows, local_width)
        .astype(jnp.bfloat16)
    )
    grad_att_in = jnp.einsum(
        "td,stc->sdc", normed_att, grad_att_up, preferred_element_type=jnp.float32
    )
    grad_normed = input_total(
        jnp.einsum("stc,sdc->td", grad_att_up, weight_mix[:3], preferred_element_type=jnp.float32)
    )
    grad_in, gain_one, shift_one = norm_backward(
        grad_normed, scaled_att, inverse_att, norm_vectors[1]
    )
    grad_residual = grad_residual + grad_in
    grad_residual, up_first, down_first, gain_zero, shift_zero = feed_backward(
        grad_residual, kept_first, 0, 0
    )
    feed_in_grad, feed_out_grad, mixer_in_grad, mixer_out_grad = (
        lax.psum_scatter(jnp.stack([up_first, up_second]), "dp", scatter_dimension=1, tiled=True),
        lax.psum_scatter(
            jnp.stack([down_first, down_second]), "dp", scatter_dimension=2, tiled=True
        ),
        lax.psum_scatter(
            jnp.concatenate([grad_att_in, grad_conv_in], axis=0),
            "dp",
            scatter_dimension=1,
            tiled=True,
        ),
        lax.psum_scatter(
            jnp.stack([grad_att_down, grad_conv_down]), "dp", scatter_dimension=2, tiled=True
        ),
    )
    norm_grads = jnp.stack(
        [
            gain_zero,
            gain_one,
            gain_two,
            gain_three,
            gain_last,
            shift_zero,
            shift_one,
            shift_two,
            shift_three,
            shift_last,
        ]
    )
    norm_total, kernel_total = lax.psum((norm_grads, kernel_grads), "dp")
    channel_grads = jnp.concatenate(
        [kernel_total, (inverse_batch * batch_sums[1])[None], batch_sums[0][None]], axis=0
    )
    rate_list = rate_table()
    feed_in_next, feed_in_mean_next, feed_in_square_next = adamw_step(
        feed_in, feed_in_mean, feed_in_square, feed_in_grad, rate_list[0]
    )
    feed_out_next, feed_out_mean_next, feed_out_square_next = adamw_step(
        feed_out, feed_out_mean, feed_out_square, feed_out_grad, rate_list[1]
    )
    mixer_in_next, mixer_in_mean_next, mixer_in_square_next = adamw_step(
        mixer_in, mixer_in_mean, mixer_in_square, mixer_in_grad, rate_list[2]
    )
    mixer_out_next, mixer_out_mean_next, mixer_out_square_next = adamw_step(
        mixer_out, mixer_out_mean, mixer_out_square, mixer_out_grad, rate_list[3]
    )
    norm_vectors_next, norm_vectors_mean_next, norm_vectors_square_next = adamw_step(
        norm_vectors, norm_vectors_mean, norm_vectors_square, norm_total, rate_list[4]
    )
    channel_vectors_next, channel_vectors_mean_next, channel_vectors_square_next = adamw_step(
        channel_vectors, channel_vectors_mean, channel_vectors_square, channel_grads, rate_list[5]
    )
    return (
        tokens_out,
        grad_residual,
        feed_in_next,
        feed_in_mean_next,
        feed_in_square_next,
        feed_out_next,
        feed_out_mean_next,
        feed_out_square_next,
        mixer_in_next,
        mixer_in_mean_next,
        mixer_in_square_next[:4],
        mixer_in_square_next[4],
        mixer_out_next,
        mixer_out_mean_next,
        mixer_out_square_next,
        norm_vectors_next,
        norm_vectors_mean_next,
        norm_vectors_square_next,
        channel_vectors_next,
        channel_vectors_mean_next,
        channel_vectors_square_next,
    )


MESH = pl.DeviceIdType.MESH
F32 = jnp.float32
BF16 = jnp.bfloat16
ROWS = 256
HALF = 128
QUAD = 64
OCT = 32
SHARD = 64
G_IN0, G_OUT0, G_ATT, G_CONV, G_IN1, G_OUT1 = range(6)


def dot_nn(a, b):
    return lax.dot_general(a, b, (((1,), (0,)), ((), ())), preferred_element_type=F32)


def dot_nt(a, b):
    return lax.dot_general(a, b, (((1,), (1,)), ((), ())), preferred_element_type=F32)


def dot_tn(a, b):
    return lax.dot_general(a, b, (((0,), (0,)), ((), ())), preferred_element_type=F32)


def sigm(v):
    return 1.0 / (1.0 + jnp.exp(-v))


def fused_kernel(
    tok, cot, lens, rot_hi, rot_lo, nv, cv, fi_h, fo_h, mi_h, mo_h,
    tout, tgrad, gfi, gfo, gmi, gmo, ngrad, cgrad,
    fi_f, fo_f, mi_f, mo_f, fi_b, fo_b, mi_b, mo_b,
    w0, w1, w2, w3, w4, w5, xg0, xg1, xg2, xg3, xb0, xb1,
    fh0, fh1, fs0, fs1, hb, qr, kr, vr, ctx, dqkv, pf,
    cu, sg, glu, zc, dd, cw, du, gid, live, rc_t, rs_t, lb,
    xh, inv, res, si, sd, hx, hy, sx, sy, rx, ry, part,
    gs0, gs1, gs2, gs3, gs4, gs5, gi0, gi1, gi2, gi3, gi4, gi5,
    ac0, ac1, ac2, ac3, ac4, ac5, stats, tapm, ngm, nsib, nx, ny, nz, cgm, tstage, cotb,
    ags, agr, rss, rsr, was, war, zs, zr, grs, grr, gas, gar, lss, lsr,
    bns, bnr, nss, nsr, cgs, cgr, outs, outr, cts, ctr, lds,
):
    w = (w0, w1, w2, w3, w4, w5)
    gst = (gs0, gs1, gs2, gs3, gs4, gs5)
    gin = (gi0, gi1, gi2, gi3, gi4, gi5)
    acc = (ac0, ac1, ac2, ac3, ac4, ac5)
    dp = lax.axis_index("dp")
    m = lax.axis_index("mp")
    x = dp % 2
    y = (dp // 2) % 2
    z = dp // 4
    p = dp % 4
    base = z * 4
    px = p + 1 - 2 * x
    py = p + 2 - 4 * y
    pd = 3 - p
    sib = (dp, 1 - m)
    xn = (base + px, m)
    yn = (base + py, m)
    dn = (base + pd, m)
    plane = ((px, xn), (py, yn), (pd, dn))
    inner = (z + 1) // 2 % 2
    others = tuple((z + k) % 4 for k in (1, 2, 3))

    def zdev(zz):
        return (zz * 4 + p, m)

    def remote(src, dst, ssem, rsem, dev):
        return pltpu.make_async_remote_copy(
            src_ref=src, dst_ref=dst, send_sem=ssem, recv_sem=rsem, device_id=dev, device_id_type=MESH
        )

    def rows(start, size):
        return pl.ds(pl.multiple_of(start, size), size)

    def block(b):
        return rows(b * ROWS, ROWS)

    pending = []

    def go_send(copy):
        copy.start()
        pending.append(copy)

    shards = {
        G_IN0: ((fi_h, fi_f, fi_b, slice(0, 1)),),
        G_OUT0: ((fo_h, fo_f, fo_b, slice(0, 1)),),
        G_ATT: ((mi_h, mi_f, mi_b, slice(0, 3)), (mo_h, mo_f, mo_b, slice(0, 1))),
        G_CONV: ((mi_h, mi_f, mi_b, slice(3, 5)), (mo_h, mo_f, mo_b, slice(1, 2))),
        G_IN1: ((fi_h, fi_f, fi_b, slice(1, 2)),),
        G_OUT1: ((fo_h, fo_f, fo_b, slice(1, 2)),),
    }

    def shard_copies(g):
        return [
            pltpu.make_async_copy(src.at[r], dst.at[r], lds.at[g, k])
            for k, (src, dst, _, r) in enumerate(shards[g])
        ]

    for g in range(6):
        for copy in shard_copies(g):
            copy.start()

    def round_shard(g):
        for copy in shard_copies(g):
            copy.wait()
        for _, src, dst, r in shards[g]:
            dst[r] = src[r].astype(BF16)

    barrier = pltpu.get_barrier_semaphore()
    greet = (sib, xn, yn, dn) + tuple(zdev(k) for k in others)
    greet += tuple((base + k, 1 - m) for k in (px, py, pd))
    for dev in greet:
        pl.semaphore_signal(barrier, inc=1, device_id=dev, device_id_type=MESH)
    pl.semaphore_wait(barrier, len(greet))

    def wview(g, start, size):
        r = pl.ds(pl.multiple_of(start, SHARD), size)
        return w[g].at[:, r] if g in (G_ATT, G_CONV) else w[g].at[r]

    def columns(i, wd):
        return pl.ds(pl.multiple_of(i * wd, 128), wd)

    def wpieces(g, peer, owner):
        r = pl.ds(pl.multiple_of(z * ROWS + owner * SHARD, SHARD), SHARD)
        if g == G_ATT:
            return (
                (mi_b.at[0:3, :, columns(peer, 128)], w[g].at[0:3, r]),
                (mo_b.at[0, :, columns(peer, 128)], w[g].at[3, r]),
            )
        if g == G_CONV:
            return (
                (mi_b.at[3:5, :, columns(peer, 128)], w[g].at[0:2, r]),
                (mo_b.at[1, :, columns(peer, 128)], w[g].at[2, r]),
            )
        src = fi_b if g in (G_IN0, G_IN1) else fo_b
        layer = 0 if g in (G_IN0, G_OUT0) else 1
        return ((src.at[layer, :, columns(peer, 512)], w[g].at[r]),)

    def plane_start(g):
        round_shard(g)
        for r, (peer, dev) in enumerate(plane):
            for k, (src, dst) in enumerate(wpieces(g, peer, p)):
                go_send(remote(src, dst, was.at[g, r, k], war.at[g, r, k], dev))
        for k, (src, dst) in enumerate(wpieces(g, p, p)):
            pltpu.make_async_copy(src, dst, was.at[g, 3, k]).start()

    def plane_wait(g):
        for r, (peer, dev) in enumerate(plane):
            for k, (_, dst) in enumerate(wpieces(g, peer, peer)):
                remote(dst, dst, was.at[g, r, k], war.at[g, r, k], dev).wait_recv()
        for k, (src, dst) in enumerate(wpieces(g, p, p)):
            pltpu.make_async_copy(src, dst, was.at[g, 3, k]).wait()

    targets = {0: (2, 1), 1: (3, 0, 2), 2: (0, 3, 1), 3: (1, 2)}
    far = {1: (3, 0), 2: (0, 3)}

    def zcopy(g, owner, k, to):
        part_w = wview(g, owner * ROWS, ROWS)
        return remote(part_w, part_w, zs.at[g, k], zr.at[g, owner], zdev(to))

    def zpiece(g, owner, k, to, peer):
        v = wview(g, owner * ROWS + peer * SHARD, SHARD)
        return remote(v, v, zs.at[g, k], zr.at[g, owner], zdev(to))

    def line_pieces(g, peer):
        for zz, tos in targets.items():

            @pl.when(z == zz)
            def _():
                for k, to in enumerate(tos):
                    zpiece(g, zz, k, to, peer).start()

    def line_start_own(g):
        for k, (src, dst) in enumerate(wpieces(g, p, p)):
            pltpu.make_async_copy(src, dst, was.at[g, 3, k]).wait()
        line_pieces(g, p)

    def line_start_rest(g):
        for r, (peer, dev) in enumerate(plane):
            for k, (_, dst) in enumerate(wpieces(g, peer, peer)):
                remote(dst, dst, was.at[g, r, k], war.at[g, r, k], dev).wait_recv()
            line_pieces(g, peer)

    def line_start(g):
        plane_wait(g)
        for zz, tos in targets.items():

            @pl.when(z == zz)
            def _():
                for k, to in enumerate(tos):
                    zcopy(g, zz, k, to).start()

    def line_pass(g):
        for zz, (owner, to) in far.items():

            @pl.when(z == zz)
            def _():
                zcopy(g, owner, 3, to).wait_recv()
                zcopy(g, owner, 3, to).start()

    def line_ready(g):
        for zz in range(4):

            @pl.when(z == zz)
            def _():
                for owner in range(4):
                    if owner != zz and (zz not in far or far[zz][0] != owner):
                        zcopy(g, owner, 0, zz).wait_recv()

    def line_done(g):
        for zz, tos in targets.items():

            @pl.when(z == zz)
            def _():
                for k, to in enumerate(tos):
                    zcopy(g, zz, k, to).wait_send()
                if zz in far:
                    zcopy(g, far[zz][0], 3, far[zz][1]).wait_send()

    def pieces(s):
        return lambda b, c, off, size: pl.ds(
            pl.multiple_of(s * 2 * ROWS + b * HALF + c * QUAD + off, OCT), size
        )

    def blocks_of_chips(b, c, off, size):
        return pl.ds(pl.multiple_of(place_of(b) * ROWS + c * HALF + off, QUAD), size)

    def place_of(b):
        return b % 2 * 2 + b // 2

    def mine(s):
        return pieces(s)(p, m, 0, QUAD)

    def settle(sends):
        for k in sends:
            k.wait_send()
        sends.clear()

    def gather(xg, where, half, sem, near, far_piece, name, sends):
        quad = half // 2

        def c(i, b, core, off, size, dev):
            r = xg.at[where(b, core, off, size)]
            return remote(r, r, ags.at[sem, i], agr.at[sem, i], dev)

        def start(*a):
            k = c(*a)
            k.start()
            sends.append(k)

        n = 1 - m
        settle(sends)
        start(0, p, m, 0, half, sib)
        start(1, p, m, 0, quad, xn)
        start(3, p, m, quad, quad, yn)
        start(2, p, m, quad, quad, xn)
        start(4, p, m, 0, quad, yn)
        yield name + ".0"
        c(1, px, m, 0, quad, xn).wait_recv()
        start(5, px, m, 0, quad, yn)
        c(3, py, m, quad, quad, yn).wait_recv()
        start(6, py, m, quad, quad, xn)
        yield name + ".1"
        c(2, px, m, quad, quad, xn).wait_recv()
        start(7, px, m, 0, half, sib)
        c(4, py, m, 0, quad, yn).wait_recv()
        start(8, py, m, 0, half, sib)
        yield name + ".1b"
        c(0, p, n, 0, half, sib).wait_recv()
        c(7, px, n, 0, half, sib).wait_recv()
        near()
        yield name + ".2"
        c(5, pd, m, 0, quad, yn).wait_recv()
        start(9, pd, m, 0, quad, sib)
        c(6, pd, m, quad, quad, xn).wait_recv()
        start(10, pd, m, quad, quad, sib)
        yield name + ".3"
        c(8, py, n, 0, half, sib).wait_recv()
        c(9, pd, n, 0, quad, sib).wait_recv()
        c(10, pd, n, quad, quad, sib).wait_recv()
        far_piece()

    def scatter(s, compute, name, sends):
        def csib(i):
            src = part.at[s, i % 2, held(i, 1 - m)]
            return remote(src, si.at[s, i], rss.at[s, i], rsr.at[s, i], sib)

        def start(k):
            k.start()
            sends.append(k)

        def held(i, core, off=0, size=QUAD):
            chip_x = x if i > 1 else 1 - x
            return pl.ds(pl.multiple_of(chip_x * HALF + core * QUAD + off, OCT), size)

        def mine_of(i, off=0, size=QUAD):
            return part[s, i % 2, held(i, m, off, size), :].astype(F32)

        a = slice(0, OCT)
        bb = slice(OCT, QUAD)
        chx = remote(sd.at[s, a], hx.at[s], rss.at[s, 4], rsr.at[s, 4], xn)
        chy = remote(sd.at[s, bb], hy.at[s], rss.at[s, 5], rsr.at[s, 5], yn)
        cxa = remote(sx.at[s, a], rx.at[s, a], rss.at[s, 6], rsr.at[s, 6], xn)
        cxb = remote(sx.at[s, bb], rx.at[s, bb], rss.at[s, 7], rsr.at[s, 7], xn)
        cyb = remote(sy.at[s, bb], ry.at[s, bb], rss.at[s, 8], rsr.at[s, 8], yn)
        cya = remote(sy.at[s, a], ry.at[s, a], rss.at[s, 9], rsr.at[s, 9], yn)
        settle(sends)
        part[s, 0] = compute(1 - y).astype(BF16)
        start(csib(0))
        start(csib(2))
        part[s, 1] = compute(y).astype(BF16)
        start(csib(1))
        start(csib(3))
        yield name + ".0"
        csib(0).wait_recv()
        sd[s] = (mine_of(0) + si[s, 0].astype(F32)).astype(BF16)
        start(chx)
        start(chy)
        csib(1).wait_recv()
        sx[s, a, :] = (mine_of(1, 0, OCT) + si[s, 1, a, :].astype(F32)).astype(BF16)
        start(cxa)
        csib(2).wait_recv()
        sy[s, bb, :] = (mine_of(2, OCT, OCT) + si[s, 2, bb, :].astype(F32)).astype(BF16)
        start(cyb)
        yield name + ".1"
        chy.wait_recv()
        sx[s, bb, :] = (
            mine_of(1, OCT, OCT) + si[s, 1, bb, :].astype(F32) + hy[s].astype(F32)
        ).astype(BF16)
        start(cxb)
        chx.wait_recv()
        sy[s, a, :] = (
            mine_of(2, 0, OCT) + si[s, 2, a, :].astype(F32) + hx[s].astype(F32)
        ).astype(BF16)
        start(cya)
        yield name + ".2"
        csib(3).wait_recv()
        cxa.wait_recv()
        cyb.wait_recv()
        cxb.wait_recv()
        cya.wait_recv()
        return mine_of(3) + si[s, 3].astype(F32) + rx[s].astype(F32) + ry[s].astype(F32)

    def hats(v):
        centre = v - jnp.mean(v, axis=-1, keepdims=True)
        scale = lax.rsqrt(jnp.mean(centre * centre, axis=-1, keepdims=True) + EPS_NORM)
        return centre * scale, scale

    def norm(v, i, s):
        hat, scale = hats(v)
        xh[i, s] = hat
        inv[i, s] = jnp.broadcast_to(scale, (QUAD, 128))
        return hat * nv[i : i + 1, :] + nv[5 + i : 6 + i, :]

    def norm_back(g, i, s):
        hat = xh[i, s]
        scale = inv[i, s, :, 0:1]
        gains = jnp.sum(g * hat, axis=0, keepdims=True)
        shifts = jnp.sum(g, axis=0, keepdims=True)
        if s == 0:
            ngm[i : i + 1, :] = gains
            ngm[5 + i : 6 + i, :] = shifts
        else:
            ngm[i : i + 1, :] = ngm[i : i + 1, :] + gains
            ngm[5 + i : 6 + i, :] = ngm[5 + i : 6 + i, :] + shifts
        e = g * nv[i : i + 1, :]
        return scale * (
            e
            - jnp.mean(e, axis=-1, keepdims=True)
            - hat * jnp.mean(e * hat, axis=-1, keepdims=True)
        )

    outer = 1 - inner
    c0 = 3 * (1 - z // 2)
    c1 = 2 - z // 2
    c2 = z + 1 - 2 * (z % 2)
    order = (c0, c1, c2, z)

    def grad_chunk(g, k):
        zz = order[k]
        cols = pl.ds(pl.multiple_of(zz * ROWS, ROWS), ROWS)
        if g == G_IN0:
            v = dot_tn(xg0[:, cols], hb[...])
        elif g == G_OUT0:
            v = dot_tn(xb1[:, cols], fs0[...])
        elif g == G_IN1:
            v = dot_tn(xg3[:, cols], hb[...])
        elif g == G_OUT1:
            v = dot_tn(xb0[:, cols], fs1[...])
        if g == G_ATT:
            v = dot_tn(xg1[:, cols], dqkv[...]).astype(BF16)
            for k in range(3):
                gst[g][zz, k] = v[:, k * 128 : (k + 1) * 128]
            gst[g][zz, 3] = dot_tn(xb0[:, cols], ctx[...]).astype(BF16)
        elif g == G_CONV:
            v = dot_tn(xg2[:, cols], du[...]).astype(BF16)
            for k in range(2):
                gst[g][zz, k] = v[:, k * 128 : (k + 1) * 128]
            gst[g][zz, 2] = dot_tn(xb1[:, cols], cw[...]).astype(BF16)
        else:
            gst[g][zz] = v.astype(BF16)

    neighbour = 1 + z // 2

    def acc_copy(g):
        return remote(gst[g].at[c0], acc[g], grs.at[g, 0], grr.at[g, 3], zdev(neighbour))

    def slot_copy(g, k):
        zz = order[k]
        if k == 0:
            slot = 1
        elif k == 1:
            slot = 1 + outer
        else:
            slot = 0
        return remote(gst[g].at[zz], gin[g].at[slot], grs.at[g, k], grr.at[g, slot], zdev(zz))

    def grad_send(g, k):
        if k == 0:

            @pl.when(outer == 1)
            def _():
                acc_copy(g).start()
        elif k < 3:
            slot_copy(g, k).start()

    def grad_acc(g):
        @pl.when(inner == 1)
        def _():
            acc_copy(g).wait_recv()
            gst[g][c0] = (gst[g][c0].astype(F32) + acc[g][...].astype(F32)).astype(BF16)
            slot_copy(g, 0).start()

    def gpieces(g, peer, owner):
        r = pl.ds(pl.multiple_of(peer * SHARD, SHARD), SHARD)
        if g == G_ATT:
            return (
                (gst[g].at[z, 0:3, r], gmi.at[0:3, :, columns(owner, 128)]),
                (gst[g].at[z, 3, r], gmo.at[0, :, columns(owner, 128)]),
            )
        if g == G_CONV:
            return (
                (gst[g].at[z, 0:2, r], gmi.at[3:5, :, columns(owner, 128)]),
                (gst[g].at[z, 2, r], gmo.at[1, :, columns(owner, 128)]),
            )
        dst = gfi if g in (G_IN0, G_IN1) else gfo
        layer = 0 if g in (G_IN0, G_OUT0) else 1
        return ((gst[g].at[z, r], dst.at[layer, :, columns(owner, 512)]),)

    def gplane(g):
        return [
            remote(src, dst, gas.at[g, r, k], gar.at[g, r, k], dev)
            for r, (peer, dev) in enumerate(plane)
            for k, (src, dst) in enumerate(gpieces(g, peer, p))
        ] + [
            pltpu.make_async_copy(src, dst, gas.at[g, 3, k])
            for k, (src, dst) in enumerate(gpieces(g, p, p))
        ]

    def slot_wait(g, slot):
        remote(gin[g].at[slot], gin[g].at[slot], grs.at[g, 1], grr.at[g, slot], sib).wait_recv()

    def grad_final(g):
        slot_wait(g, 0)
        slot_wait(g, 1)
        t = gst[g][z].astype(F32) + gin[g][0].astype(F32) + gin[g][1].astype(F32)
        keep_t = t

        @pl.when(outer == 1)
        def _():
            gst[g][z] = keep_t.astype(BF16)

        @pl.when(inner == 1)
        def _():
            slot_wait(g, 2)
            gst[g][z] = (keep_t + gin[g][2].astype(F32)).astype(BF16)

        for copy in gplane(g):
            copy.start()

    def grad_done(g):
        for r, (peer, dev) in enumerate(plane):
            for k, (_, dst) in enumerate(gpieces(g, peer, peer)):
                remote(dst, dst, gas.at[g, r, k], gar.at[g, r, k], dev).wait_recv()
        for i, copy in enumerate(gplane(g)):
            if i < 3 * len(gpieces(g, p, p)):
                copy.wait_send()
            else:
                copy.wait()

        @pl.when(outer == 1)
        def _():
            acc_copy(g).wait_send()

        @pl.when(inner == 1)
        def _():
            slot_copy(g, 0).wait_send()

        slot_copy(g, 1).wait_send()
        slot_copy(g, 2).wait_send()

    def line_share(buf, sem_s, sem_r, start):
        for k in range(3):
            to = others[k]
            if start:
                remote(buf.at[z], buf.at[z], sem_s.at[k], sem_r.at[2 - k], zdev(to)).start()
            else:
                frm = others[2 - k]
                remote(buf.at[z], buf.at[z], sem_s.at[k], sem_r.at[2 - k], zdev(to)).wait_send()
                remote(buf.at[frm], buf.at[frm], sem_s.at[k], sem_r.at[2 - k], zdev(frm)).wait_recv()

    stats[...] = jnp.zeros_like(stats)
    tapm[...] = jnp.zeros_like(tapm)
    ngm[10:16, :] = jnp.zeros((6, D), F32)
    lb[p, 0:1, :] = jnp.broadcast_to(lens[0:1, 0:1].astype(F32), (1, ROWS))
    lb[p, 1:2, :] = jnp.broadcast_to(lens[0:1, 1:2].astype(F32), (1, ROWS))
    lb[p, 2:8, :] = jnp.zeros((6, ROWS), F32)
    plane_start(G_IN0)
    for r in range(3):
        peer, dev = plane[r]
        remote(lb.at[p], lb.at[p], lss.at[r], lsr.at[r], dev).start()
    load = pltpu.make_async_copy(
        tok.at[pl.ds(pl.multiple_of(m * HALF, HALF), HALF)],
        xg0.at[blocks_of_chips(p, m, 0, HALF)],
        cts.at[1],
    )
    load.start()
    load.wait()

    def nothing():
        return None

    def either(here, a, b):
        @pl.when(here)
        def _():
            a()

        @pl.when(jnp.logical_not(here))
        def _():
            b()

    def cot_rows(owner_x):
        return cot.at[pl.ds(pl.multiple_of(owner_x * HALF + m * QUAD, QUAD), QUAD)]

    def cot_away():
        return remote(cot_rows(1 - x), cotb.at[x], cts.at[0], ctr.at[0], xn)

    def cot_local():
        return pltpu.make_async_copy(cot_rows(x), cotb.at[x], ctr.at[1])

    def cot_start():
        cot_away().start()
        cot_local().start()

    def cot_wait():
        cot_away().wait_send()
        remote(cotb.at[1 - x], cotb.at[1 - x], cts.at[0], ctr.at[0], xn).wait_recv()
        cot_local().wait()

    def tables():
        for r in range(3):
            peer, dev = plane[r]
            remote(lb.at[p], lb.at[p], lss.at[r], lsr.at[r], dev).wait_send()
            remote(lb.at[peer], lb.at[peer], lss.at[r], lsr.at[r], dev).wait_recv()
        place = lax.broadcasted_iota(jnp.int32, (ROWS, ROWS), 0).astype(F32)
        lane = lax.broadcasted_iota(jnp.int32, (ROWS, ROWS), 1).astype(F32)
        for b in range(4):
            l0 = lb[b % 2 * 2 + b // 2, 0:1, :]
            l1 = lb[b % 2 * 2 + b // 2, 1:2, :]
            first_in = jnp.where(place < l0, 1.0, 0.0)
            live_in = jnp.where(place < l0 + l1, 1.0, 0.0)
            at = place - l0 * (1.0 - first_in) - l1 * (1.0 - live_in)
            r = slice(b * ROWS, (b + 1) * ROWS)
            gid[r, :] = 3.0 * b + first_in[:, :128] + live_in[:, :128]
            live[r, :] = live_in[:, :128]
            hot = jnp.where(at == lane, 1.0, 0.0).astype(BF16)
            t = dot_nn(hot, rot_hi[...]) + dot_nn(hot, rot_lo[...])
            rc_t[r, :] = t[:, :128]
            rs_t[r, :] = t[:, 128:]

    first_sends = []
    opening = gather(xg0, blocks_of_chips, HALF, 2, nothing, nothing, "G0", first_sends)
    line_start_own(G_IN0)
    next(opening)
    line_start_rest(G_IN0)
    next(opening)
    plane_start(G_OUT0)
    next(opening)
    next(opening)
    tables()
    next(opening)
    line_pass(G_IN0)
    line_start(G_OUT0)
    for _ in opening:
        pass
    settle(first_sends)
    for g in (G_ATT, G_CONV, G_IN1, G_OUT1):
        plane_start(g)
    cot_start()
    for s in range(2):
        first = xg0[mine(s), :].astype(F32)
        res[s] = first
        norm(first, 0, s)

    @pl.loop(0, 8)
    def _(i):
        r = rows(i * HALF, HALF)
        hat, _ = hats(xg0[r, :].astype(F32))
        xg0[r, :] = (hat * nv[0:1, :] + nv[5:6, :]).astype(BF16)

    def block_rows(s, q):
        return pl.ds(pl.multiple_of((2 * s + q) * ROWS, ROWS), ROWS)

    def ff_hidden(s, xg, g, fh, fs):
        def f(q):
            r = block_rows(s, q)
            h = dot_nn(xg[r, :], w[g][...])
            fh[r, :] = h
            fs[r, :] = (h * sigm(h)).astype(BF16)

        return f

    def wide(g, first, last):
        return jnp.concatenate([w[g][k] for k in range(first, last)], axis=1)

    def part_nt(s, lhs, weight):
        def f(q):
            return dot_nt(lhs[block_rows(s, q), :], weight())

        return f

    def whole(g):
        return lambda: w[g][...]

    def turn(v, r):
        return v * rc_t[r, :] + pltpu.roll(v, 64, 1) * rs_t[r, :]

    def turn_back(v, r):
        return v * rc_t[r, :] - pltpu.roll(v, 64, 1) * rs_t[r, :]

    lane_row = lax.broadcasted_iota(jnp.int32, (1, ROWS), 1).astype(F32)

    def attend(s):
        def f(q):
            r = block_rows(s, q)
            b = 2 * q + s
            t = dot_nn(xg1[r, :], wide(G_ATT, 0, 3))
            qs = (turn(t[:, 0:128], r) * (HEAD_DIM**-0.5)).astype(BF16)
            k = turn(t[:, 128:256], r).astype(BF16)
            v = t[:, 256:384].astype(BF16)
            qr[r, :] = qs
            kr[r, :] = k
            vr[r, :] = v
            sc = dot_nt(qs, k)
            l0 = lb[b, 0:1, :]
            l1 = lb[b, 1:2, :]
            gk = (
                3.0 * (2 * s + q).astype(F32)
                + jnp.where(lane_row < l0, 1.0, 0.0)
                + jnp.where(lane_row < l0 + l1, 1.0, 0.0)
            )
            gq = gid[r, :]
            gq = jnp.concatenate([gq, gq], axis=1)
            sc = jnp.where(gq == gk, sc, BIG_NEG)
            e = jnp.exp(sc - jnp.max(sc, axis=-1, keepdims=True))
            pr = e / jnp.sum(e, axis=-1, keepdims=True)
            pf[r, :] = pr
            ctx[r, :] = dot_nn(pr.astype(BF16), v).astype(BF16)

        return f

    def attend_back(s):
        def f(q):
            r = block_rows(s, q)
            dc = dot_nn(xb0[r, :], w[G_ATT][3]).astype(BF16)
            pr = pf[r, :]
            k = kr[r, :]
            dp_ = dot_nt(dc, vr[r, :])
            dqkv[r, 256:384] = dot_tn(pr.astype(BF16), dc).astype(BF16)
            sb = (pr * (dp_ - jnp.sum(pr * dp_, axis=-1, keepdims=True))).astype(BF16)
            dqkv[r, 0:128] = turn_back(dot_nn(sb, k) * (HEAD_DIM**-0.5), r).astype(BF16)
            dqkv[r, 128:256] = turn_back(dot_tn(sb, qr[r, :]), r).astype(BF16)

        return f

    chan = pl.ds(pl.multiple_of(p * 128, 128), 128)
    taps = [cv[j : j + 1, chan] for j in range(KERNEL)]
    gain = cv[KERNEL : KERNEL + 1, chan]
    shift = cv[KERNEL + 1 : KERNEL + 2, chan]
    count = 2 * ROWS
    bn = {}

    def conv_in(s):
        def f(q):
            r = block_rows(s, q)
            t = dot_nn(xg2[r, :], wide(G_CONV, 0, 2))
            sig = sigm(t[:, 128:256])
            cu[r, :] = t[:, 0:128]
            sg[r, :] = sig
            glu[r, :] = t[:, 0:128] * sig

        return f

    def span(s):
        return slice(s * count, (s + 1) * count)

    def same(s, j):
        ids = gid[span(s), :]
        return jnp.where(pltpu.roll(ids, (2 - j) % count, 0) == ids, 1.0, 0.0)

    def add_row(ref, z_, row, value, s):
        at = slice(row, row + 1)
        ref[z_, at, :] = value if s == 0 else ref[z_, at, :] + value

    def mix(s):
        g_all = glu[span(s), :]
        mixed = taps[2] * g_all
        for j in (0, 1, 3, 4):
            mixed = mixed + taps[j] * pltpu.roll(g_all, (2 - j) % count, 0) * same(s, j)
        zc[span(s), :] = mixed
        lv = live[span(s), :]
        add_row(stats.at[0], z, 0, jnp.sum(lv * mixed, axis=0, keepdims=True), s)
        add_row(stats.at[0], z, 1, jnp.sum(lv * mixed * mixed, axis=0, keepdims=True), s)
        add_row(stats.at[0], z, 2, jnp.sum(lv, axis=0, keepdims=True), s)

    def bn_forward():
        line_share(stats.at[0], bns.at[0], bnr.at[0], True)
        line_pass(G_IN1)
        line_start(G_OUT1)
        line_share(stats.at[0], bns.at[0], bnr.at[0], False)
        tot = stats[0, 0] + stats[0, 1] + stats[0, 2] + stats[0, 3]
        bn["n"] = tot[2:3, :]
        bn["mean"] = tot[0:1, :] / bn["n"]
        bn["inv"] = lax.rsqrt(tot[1:2, :] / bn["n"] - bn["mean"] * bn["mean"] + EPS_NORM)

    def conv_out(s):
        def f(q):
            r = block_rows(s, q)
            v = (zc[r, :] - bn["mean"]) * bn["inv"] * gain + shift
            cw[r, :] = (v * sigm(v)).astype(BF16)
            return dot_nt(cw[r, :], w[G_CONV][2])

        return f

    def conv_back(s):
        def f(q):
            r = block_rows(s, q)
            v = (zc[r, :] - bn["mean"]) * bn["inv"] * gain + shift
            sig = sigm(v)
            dd[r, :] = dot_nn(xb1[r, :], w[G_CONV][2]) * sig * (1.0 + v * (1.0 - sig))

        return f

    def batch_sums(s):
        d_all = dd[span(s), :]
        add_row(stats.at[1], z, 0, jnp.sum(d_all, axis=0, keepdims=True), s)
        centred = zc[span(s), :] - bn["mean"]
        add_row(stats.at[1], z, 1, jnp.sum(d_all * centred, axis=0, keepdims=True), s)

    def bn_backward():
        line_share(stats.at[1], bns.at[1], bnr.at[1], True)
        for k in range(4):
            grad_chunk(G_IN1, k)
        line_share(stats.at[1], bns.at[1], bnr.at[1], False)
        tot = stats[1, 0] + stats[1, 1] + stats[1, 2] + stats[1, 3]
        i = bn["inv"]
        bn["s1"] = tot[0:1, :]
        bn["s2"] = tot[1:2, :]
        bn["dv"] = -0.5 * i * i * i * gain * bn["s2"]
        bn["dm"] = -i * gain * bn["s1"] - 2.0 * bn["mean"] * bn["dv"]

    def unmix(s):
        r = span(s)
        dz = dd[r, :] * (gain * bn["inv"]) + live[r, :] * (
            (bn["dm"] + 2.0 * zc[r, :] * bn["dv"]) / bn["n"]
        )
        g_all = glu[r, :]
        back = jnp.zeros_like(dz)
        for j in range(KERNEL):
            if j == 2:
                weighted = dz
                moved = g_all
            else:
                weighted = dz * same(s, j)
                moved = pltpu.roll(g_all, (2 - j) % count, 0)
            add_row(tapm, z, j, jnp.sum(weighted * moved, axis=0, keepdims=True), s)
            weighted = taps[j] * weighted
            if j != 2:
                weighted = pltpu.roll(weighted, (j - 2) % count, 0)
            back = back + weighted
        s_all = sg[r, :]
        du[r, 0:128] = (back * s_all).astype(BF16)
        du[r, 128:256] = (back * cu[r, :] * s_all * (1.0 - s_all)).astype(BF16)

    def ff_back(s, xb, g, fh):
        def f(q):
            r = block_rows(s, q)
            h = fh[r, :]
            sig = sigm(h)
            d = dot_nn(xb[r, :], w[g][...])
            hb[r, :] = (d * sig * (1.0 + h * (1.0 - sig))).astype(BF16)

        return f

    def out_rows(out, owner_x, core):
        return out.at[pl.ds(pl.multiple_of(owner_x * HALF + core * QUAD, QUAD), QUAD)]

    def give_out(i, s, out):
        there = out_rows(out, x, m)
        src = tstage.at[i, s]
        r_sem = outr.at[i, x, m]

        def a():
            pltpu.make_async_copy(src, there, r_sem).start()
            remote(src, there, outs.at[i, s, 0], r_sem, sib).start()

        def b():
            remote(src, there, outs.at[i, s, 0], r_sem, xn).start()
            remote(src, there, outs.at[i, s, 1], r_sem, (base + px, 1 - m)).start()

        either(x == s, a, b)

    def out_wait(i, out):
        there = out_rows(out, x, m)
        for s in range(2):
            src = tstage.at[i, s]
            remote(src, there, outs.at[i, s, 0], outr.at[i, x, m], xn).wait_send()

            @pl.when(x != s)
            def _():
                remote(src, there, outs.at[i, s, 1], outr.at[i, x, m], xn).wait_send()

        for cx in range(2):
            for cm in range(2):
                here = out.at[cx * HALF + cm * QUAD : cx * HALF + (cm + 1) * QUAD]
                remote(here, here, outs.at[i, 0, 0], outr.at[i, cx, cm], sib).wait_recv()

    def stream(s):
        g_sends = []
        r_sends = []
        at = mine(s)

        def take(xg, compute, name, ready=None):
            def near():
                if ready is not None and s == 0:
                    line_ready(ready)
                compute(y)

            return gather(xg, pieces(s), QUAD, s, near, lambda: compute(1 - y), name, g_sends)

        def give(compute, name):
            return scatter(s, compute, name, r_sends)

        hidden = ff_hidden(s, xg0, G_IN0, fh0, fs0)
        hidden(0)
        hidden(1)
        yield "W"
        t = yield from give(part_nt(s, fs0, whole(G_OUT0)), "R0")
        v = res[s] + 0.5 * t
        res[s] = v
        xg1[at, :] = norm(v, 1, s).astype(BF16)
        yield from take(xg1, attend(s), "G1", G_ATT)
        t = yield from give(part_nt(s, ctx, lambda: w[G_ATT][3]), "R1")
        v = res[s] + t
        res[s] = v
        xg2[at, :] = norm(v, 2, s).astype(BF16)
        yield from take(xg2, conv_in(s), "G2", G_CONV)
        mix(s)
        yield "BN1"
        t = yield from give(conv_out(s), "R2")
        v = res[s] + t
        res[s] = v
        xg3[at, :] = norm(v, 3, s).astype(BF16)
        yield from take(xg3, ff_hidden(s, xg3, G_IN1, fh1, fs1), "G3", G_IN1)
        if s == 0:
            line_ready(G_OUT1)
        t = yield from give(part_nt(s, fs1, whole(G_OUT1)), "R3")
        tstage[0, s] = norm(res[s] + 0.5 * t, 4, s).astype(BF16)
        if s == 0:
            cot_wait()
        v = norm_back(cotb[s].astype(F32), 4, s)
        res[s] = v
        xb0[at, :] = (0.5 * v).astype(BF16)
        yield from take(xb0, ff_back(s, xb0, G_OUT1, fh1), "H3")
        t = yield from give(part_nt(s, hb, whole(G_IN1)), "Q3")
        v = res[s] + norm_back(t, 3, s)
        res[s] = v
        xb1[at, :] = v.astype(BF16)
        yield from take(xb1, conv_back(s), "H2")
        batch_sums(s)
        yield "BN2"
        unmix(s)
        yield "TAPS"
        t = yield from give(part_nt(s, du, lambda: wide(G_CONV, 0, 2)), "Q2")
        v = res[s] + norm_back(t, 2, s)
        res[s] = v
        xb0[at, :] = v.astype(BF16)
        yield from take(xb0, attend_back(s), "H1")
        t = yield from give(part_nt(s, dqkv, lambda: wide(G_ATT, 0, 3)), "Q1")
        v = res[s] + norm_back(t, 1, s)
        res[s] = v
        xb1[at, :] = (0.5 * v).astype(BF16)
        yield from take(xb1, ff_back(s, xb1, G_OUT0, fh0), "H0")
        yield "TAIL"
        t = yield from give(part_nt(s, hb, whole(G_IN0)), "Q0")
        tstage[1, s] = (res[s] + norm_back(t, 0, s)).astype(BF16)
        give_out(1, s, tgrad)
        settle(g_sends)
        settle(r_sends)

    queue = []

    def chunks(g, send):
        def one(k):
            def f():
                grad_chunk(g, k)
                if send:
                    grad_send(g, k)

            return f

        return [one(k) for k in range(4)]

    def first_feed():
        line_pass(G_OUT0)
        line_start(G_ATT)
        line_ready(G_OUT0)

    def tap_share():
        line_share(tapm, bns.at[2], bnr.at[2], True)
        for k in range(3):
            grad_send(G_IN1, k)

    def tail():
        for f in chunks(G_OUT0, True) + chunks(G_IN0, True):
            f()
        for s in range(2):
            give_out(0, s, tout)

    def passing(g, following):
        def f():
            line_pass(g)
            if following is not None:
                line_start(following)

        return f

    meet = {
        "W": first_feed, "BN1": bn_forward, "BN2": bn_backward, "TAPS": tap_share, "TAIL": tail,
    }
    after = {
        "R0.2": [passing(G_ATT, G_CONV)],
        "R1.1": [passing(G_CONV, G_IN1)],
        "G3.0": [passing(G_OUT1, None)],
        "Q3.0": chunks(G_OUT1, True),
        "H2.0": [lambda: grad_acc(G_OUT1)],
        "Q2.0": chunks(G_CONV, True),
        "Q2.2": [lambda: grad_acc(G_IN1)],
        "H1.1": [lambda: grad_final(G_OUT1)],
        "H1.2": [lambda: grad_acc(G_CONV)],
        "Q1.0": chunks(G_ATT, True),
        "Q1.2": [lambda: grad_final(G_IN1)],
        "H0.1": [lambda: grad_acc(G_ATT)],
        "H0.2": [lambda: grad_final(G_CONV)],
        "Q0.1": [lambda: grad_acc(G_OUT0)],
    }
    line_ready(G_IN0)
    streams = [stream(0), stream(1)]
    state = ["", ""]
    while streams[1] is not None:
        for s in range(2):
            if streams[s] is None:
                continue
            try:
                state[s] = next(streams[s])
            except StopIteration:
                streams[s] = None
                continue
            if s == 1:
                queue.extend(after.get(state[s], []))
            if queue:
                queue.pop(0)()
            if s == 1 and state[s] in meet:
                while queue:
                    queue.pop(0)()
                meet[state[s]]()
    while queue:
        queue.pop(0)()
    grad_final(G_ATT)
    grad_acc(G_IN0)

    def swap(src, dst, k, dev):
        copy = remote(src, dst, nss.at[k], nsr.at[k], dev)
        copy.start()
        copy.wait()

    swap(ngm, nsib, 0, sib)
    ngm[...] = ngm[...] + nsib[...]
    swap(ngm, nx, 1, xn)
    ngm[...] = ngm[...] + nx[...]
    swap(ngm, ny, 2, yn)
    nz[z] = ngm[...] + ny[...]
    line_share(nz, nss.at[pl.ds(3, 3)], nsr.at[pl.ds(3, 3)], True)
    line_share(tapm, bns.at[2], bnr.at[2], False)
    cgm[...] = tapm[0] + tapm[1] + tapm[2] + tapm[3]
    cgm[5:6, :] = bn["inv"] * bn["s2"]
    cgm[6:7, :] = bn["s1"]
    cgrad[:, chan] = cgm[...]
    for r in range(3):
        remote(cgm, cgrad.at[:, chan], cgs.at[r], cgr.at[r], plane[r][1]).start()
    grad_final(G_OUT0)
    line_share(nz, nss.at[pl.ds(3, 3)], nsr.at[pl.ds(3, 3)], False)
    ngrad[...] = nz[0] + nz[1] + nz[2] + nz[3]
    for r in range(3):
        peer, dev = plane[r]
        there = cgrad.at[:, pl.ds(pl.multiple_of(peer * 128, 128), 128)]
        remote(there, there, cgs.at[r], cgr.at[r], dev).wait_recv()
        remote(cgm, cgrad.at[:, chan], cgs.at[r], cgr.at[r], dev).wait_send()
    grad_final(G_IN0)
    out_wait(0, tout)
    out_wait(1, tgrad)
    for copy in pending:
        copy.wait_send()
    for g in range(6):
        line_done(g)
        grad_done(g)


def group_shape(g, rows):
    if g == G_ATT:
        return (4, rows, 128)
    if g == G_CONV:
        return (3, rows, 128)
    return (rows, 512)


def rotation_tables():
    half = HEAD_DIM // 2
    frequency = np.exp(np.arange(half, dtype=np.float32) * np.float32(-2.0 * math.log(10000.0) / HEAD_DIM))
    angles = np.arange(ROWS, dtype=np.float32)[:, None] * frequency.astype(np.float32)[None, :]
    c = np.cos(angles.astype(np.float64))
    s = np.sin(angles.astype(np.float64))
    table = np.concatenate([c, c, -s, s], axis=1).astype(np.float32)
    high = table.astype(BF16)
    low_part = (table - high.astype(np.float32)).astype(BF16)
    return high, low_part


def fused_call(tok, cot, lens, norm_vectors, channel_vectors, fi, fo, mi, mo):
    high, low_part = rotation_tables()
    vm = pl.BlockSpec(memory_space=pltpu.VMEM)
    hbm = pl.BlockSpec(memory_space=pl.ANY)

    def v(shape, dtype):
        return pltpu.VMEM(shape, dtype)

    t16 = (4 * ROWS, D)
    h16 = (4 * ROWS, 512)
    c16 = (4 * ROWS, 128)
    shapes = ((2, SHARD, 2048), (2, SHARD, 2048), (5, SHARD, 512), (2, SHARD, 512))
    scratch = [v(k, F32) for k in shapes] + [v(k, BF16) for k in shapes]
    scratch += [v(group_shape(g, D), BF16) for g in range(6)]
    scratch += [v(t16, BF16)] * 6
    scratch += [v(h16, F32)] * 2 + [v(h16, BF16)] * 3
    scratch += [v(c16, BF16)] * 4 + [v((4 * ROWS, 384), BF16), v((4 * ROWS, ROWS), F32)]
    scratch += [v(c16, F32)] * 5 + [v(c16, BF16), v((4 * ROWS, 256), BF16)]
    scratch += [v(c16, F32)] * 4 + [v((4, 8, ROWS), F32)]
    scratch += [v((5, 2, QUAD, D), F32), v((5, 2, QUAD, 128), F32), v((2, QUAD, D), F32)]
    scratch += [v((2, 4, QUAD, D), BF16)] + [v((2, QUAD, D), BF16)] + [v((2, OCT, D), BF16)] * 2
    scratch += [v((2, QUAD, D), BF16)] * 4 + [v((2, 2, ROWS, D), BF16)]
    scratch += [v((4,) + group_shape(g, ROWS), BF16) for g in range(6)]
    scratch += [v((3,) + group_shape(g, ROWS), BF16) for g in range(6)]
    scratch += [v(group_shape(g, ROWS), BF16) for g in range(6)]
    scratch += [v((2, 4, 8, 128), F32), v((4, 8, 128), F32)]
    scratch += [v((16, D), F32)] * 4 + [v((4, 16, D), F32), v((8, 128), F32), v((2, 2, QUAD, D), BF16)]
    scratch += [v((2, QUAD, D), BF16)]
    dma = pltpu.SemaphoreType.DMA
    sems = [(3, 11), (3, 11), (2, 10), (2, 10), (6, 4, 2), (6, 4, 2), (6, 4), (6, 4), (6, 4), (6, 4)]
    sems += [(6, 4, 2), (6, 4, 2), (3,), (3,), (3, 3), (3, 3), (6,), (6,), (3,), (3,), (2, 2, 2), (2, 2, 2), (2,), (2,), (6, 2)]
    scratch += [dma(k) for k in sems]
    out_shape = (
        jax.ShapeDtypeStruct((ROWS, D), BF16),
        jax.ShapeDtypeStruct((ROWS, D), BF16),
        jax.ShapeDtypeStruct((2, SHARD, 2048), BF16),
        jax.ShapeDtypeStruct((2, SHARD, 2048), BF16),
        jax.ShapeDtypeStruct((5, SHARD, 512), BF16),
        jax.ShapeDtypeStruct((2, SHARD, 512), BF16),
        jax.ShapeDtypeStruct((16, D), F32),
        jax.ShapeDtypeStruct((8, 512), F32),
    )
    return pl.pallas_call(
        fused_kernel,
        out_shape=out_shape,
        in_specs=[hbm, hbm] + [vm] * 5 + [hbm] * 4,
        out_specs=(hbm,) * 6 + (vm, vm),
        scratch_shapes=scratch,
        compiler_params=pltpu.CompilerParams(
            collective_id=0, has_side_effects=True, vmem_limit_bytes=63 * 2**20
        ),
    )(tok, cot, lens, jnp.asarray(high), jnp.asarray(low_part), norm_vectors, channel_vectors, fi, fo, mi, mo)


def update_kernel(*refs):
    to, tg, gfi, gfo, gmi, gmo, ng, cg = refs[:8]
    state = [refs[8 + 3 * k : 11 + 3 * k] for k in range(6)]
    out = refs[26:]
    out[0][...] = to[...].astype(F32)
    out[1][...] = tg[...].astype(F32)
    rates = (D**-0.5, FF**-0.5, D**-0.5, None, 0.3, 0.3)

    def step(k, at, gradient, rate):
        weight, mean, square = (r[at] for r in state[k])
        return adamw_step(weight, mean, square, gradient.astype(F32), rate)

    for k, g in ((0, gfi), (1, gfo)):
        for layer in range(2):
            new = step(k, layer, g[layer], rates[k])
            for i in range(3):
                out[2 + 3 * k + i][layer] = new[i]
    for layer in range(5):
        a, b, c = step(2, layer, gmi[layer], rates[2])
        out[8][layer] = a
        out[9][layer] = b
        if layer < 4:
            out[10][layer] = c
        else:
            out[11][...] = c
    for layer in range(2):
        rate = (max(2 * D // TOK_DEV, 1) ** -0.5, D**-0.5)[layer]
        new = step(3, layer, gmo[layer], rate)
        for i in range(3):
            out[12 + i][layer] = new[i]
    for k, g, n in ((4, ng, 10), (5, cg, 7)):
        new = step(k, slice(0, n), g[0:n, :], rates[k])
        for i in range(3):
            out[3 + 3 * k + i][...] = new[i]


def update_call(grads, *states):
    steps = 4
    r = SHARD // steps

    def stacked(layers, width):
        return pl.BlockSpec((layers, r, width), lambda i: (0, i, 0))

    def fixed(a, b):
        return pl.BlockSpec((a, b), lambda i: (0, 0))

    frames = pl.BlockSpec((ROWS // steps, D), lambda i: (i, 0))
    big = [stacked(2, 2048), stacked(2, 2048), stacked(5, 512), stacked(2, 512)]
    small = [fixed(10, D), fixed(7, 512)]
    in_specs = [frames, frames] + big + [fixed(16, D), fixed(8, 512)]
    out_specs = [frames, frames]
    out_shape = [jax.ShapeDtypeStruct((ROWS, D), F32)] * 2
    flat = list(grads)
    for k, three in enumerate(states):
        spec = (big + small)[k]
        for i, a in enumerate(three):
            flat.append(a)
            in_specs.append(spec)
            if k == 2 and i == 2:
                out_specs += [stacked(4, 512), pl.BlockSpec((r, 512), lambda i: (i, 0))]
                out_shape += [
                    jax.ShapeDtypeStruct((4, SHARD, 512), F32),
                    jax.ShapeDtypeStruct((SHARD, 512), F32),
                ]
            else:
                out_specs.append(spec)
                out_shape.append(jax.ShapeDtypeStruct(a.shape, F32))
    return pl.pallas_call(
        update_kernel,
        grid=(steps,),
        in_specs=in_specs,
        out_specs=out_specs,
        out_shape=out_shape,
        compiler_params=pltpu.CompilerParams(vmem_limit_bytes=63 * 2**20),
    )(*flat)


def fast_body(
    tokens_in, out_cotangent, utt_lengths,
    feed_in, feed_in_mean, feed_in_square,
    feed_out, feed_out_mean, feed_out_square,
    mixer_in, mixer_in_mean, mixer_in_square,
    mixer_out, mixer_out_mean, mixer_out_square,
    norm_vectors, norm_vectors_mean, norm_vectors_square,
    channel_vectors, channel_vectors_mean, channel_vectors_square,
):
    fo_t = jnp.swapaxes(feed_out, 1, 2)
    mo_t = jnp.swapaxes(mixer_out, 1, 2)
    tokens_out, tokens_grad, gfi, gfo, gmi, gmo, ngrad, cgrad = fused_call(
        tokens_in, out_cotangent, utt_lengths, norm_vectors, channel_vectors,
        feed_in, fo_t, mixer_in, mo_t,
    )

    def turned(v):
        return jnp.swapaxes(v, 1, 2)

    new = update_call(
        (tokens_out, tokens_grad, gfi, gfo, gmi, gmo, ngrad, cgrad),
        (feed_in, feed_in_mean, feed_in_square),
        (fo_t, turned(feed_out_mean), turned(feed_out_square)),
        (mixer_in, mixer_in_mean, mixer_in_square),
        (mo_t, turned(mixer_out_mean), turned(mixer_out_square)),
        (norm_vectors, norm_vectors_mean, norm_vectors_square),
        (channel_vectors, channel_vectors_mean, channel_vectors_square),
    )
    new = list(new)
    for k in (5, 6, 7, 12, 13, 14):
        new[k] = turned(new[k])
    return tuple(new)


def solution(mesh):
    fits = mesh.shape["dp"] == 16 and mesh.shape["mp"] == 2
    placed = (
        P("dp", None),
        P("dp", None),
        P("dp", None),
        P(None, "dp", "mp"),
        P(None, "dp", "mp"),
        P(None, "dp", "mp"),
        P(None, "mp", "dp"),
        P(None, "mp", "dp"),
        P(None, "mp", "dp"),
        P(None, "dp", "mp"),
        P(None, "dp", "mp"),
        P(None, "dp", "mp"),
        P(None, "mp", "dp"),
        P(None, "mp", "dp"),
        P(None, "mp", "dp"),
        P(),
        P(),
        P(),
        P(None, "mp"),
        P(None, "mp"),
        P(None, "mp"),
    )
    return jax.shard_map(
        fast_body if fits else body,
        mesh=mesh,
        in_specs=placed,
        out_specs=(
            P("dp", None),
            P("dp", None),
            P(None, "dp", "mp"),
            P(None, "dp", "mp"),
            P(None, "dp", "mp"),
            P(None, "mp", "dp"),
            P(None, "mp", "dp"),
            P(None, "mp", "dp"),
            P(None, "dp", "mp"),
            P(None, "dp", "mp"),
            P(None, "dp", "mp"),
            P("dp", "mp"),
            P(None, "mp", "dp"),
            P(None, "mp", "dp"),
            P(None, "mp", "dp"),
            P(),
            P(),
            P(),
            P(None, "mp"),
            P(None, "mp"),
            P(None, "mp"),
        ),
        check_vma=False,
    )
```

```python
import math

import jax
import jax.numpy as jnp
import numpy as np
from jax import lax
from jax.experimental import pallas as pl
from jax.experimental.pallas import tpu as pltpu
from jax.sharding import PartitionSpec as P

D = 1024
FF = 4096
HEAD_DIM = 128
KERNEL = 5
STEP_COUNT = 3
TOK_DEV = 256


EPS_NORM = 1e-05
EPS_ADAM = 1e-08
DECAY_WEIGHT = 0.01
BETA = 0.5
BIG_NEG = -1e30


def product(left_side, right_side):
    return jnp.dot(left_side, right_side, preferred_element_type=jnp.float32)


def weight_grad(inputs, gradients):
    return lax.dot_general(
        inputs, gradients, (((0,), (0,)), ((), ())), preferred_element_type=jnp.float32
    )


def input_grad(gradients, weight):
    return lax.dot_general(
        gradients, weight, (((1,), (1,)), ((), ())), preferred_element_type=jnp.float32
    )


def norm_forward(values, gain_row, shift_row):
    centre = values - jnp.mean(values, axis=-1, keepdims=True)
    inverse = lax.rsqrt(jnp.mean(centre * centre, axis=-1, keepdims=True) + EPS_NORM)
    scaled = centre * inverse
    return (scaled * gain_row + shift_row, scaled, inverse)


def norm_backward(grad_out, scaled, inverse, gain_row):
    grad_gain = jnp.sum(grad_out * scaled, axis=0)
    grad_shift = jnp.sum(grad_out, axis=0)
    grad_scaled = grad_out * gain_row
    grad_in = inverse * (
        grad_scaled
        - jnp.mean(grad_scaled, axis=-1, keepdims=True)
        - scaled * jnp.mean(grad_scaled * scaled, axis=-1, keepdims=True)
    )
    return (grad_in, grad_gain, grad_shift)


def rotate(values, cosine, sine_part):
    halfway = values.shape[-1] // 2
    front_half = values[..., :halfway]
    back_half = values[..., halfway:]
    return jnp.concatenate(
        [front_half * cosine - back_half * sine_part, front_half * sine_part + back_half * cosine],
        axis=-1,
    )


def unrotate(values, cosine, sine_part):
    halfway = values.shape[-1] // 2
    front_half = values[..., :halfway]
    back_half = values[..., halfway:]
    return jnp.concatenate(
        [front_half * cosine + back_half * sine_part, back_half * cosine - front_half * sine_part],
        axis=-1,
    )


def depthwise(gated_rows, kernel, group_ids):
    count_rows = gated_rows.shape[0]
    reach = KERNEL // 2
    padded = jnp.pad(gated_rows, ((reach, reach), (0, 0)))
    padded_ids = jnp.pad(group_ids, (reach, reach), constant_values=-1)
    summed = jnp.zeros_like(gated_rows)
    for offset in range(KERNEL):
        matched = (padded_ids[offset : offset + count_rows] == group_ids).astype(jnp.float32)
        summed = summed + kernel[offset] * padded[offset : offset + count_rows] * matched[:, None]
    return summed


def depthwise_back(grad_mixed, gated_rows, kernel, group_ids):
    count_rows = gated_rows.shape[0]
    reach = KERNEL // 2
    padded = jnp.pad(gated_rows, ((reach, reach), (0, 0)))
    padded_ids = jnp.pad(group_ids, (reach, reach), constant_values=-1)
    grad_padded = jnp.zeros_like(padded)
    kernel_rows = []
    for offset in range(KERNEL):
        matched = (padded_ids[offset : offset + count_rows] == group_ids).astype(jnp.float32)
        weighted = grad_mixed * matched[:, None]
        kernel_rows.append(jnp.sum(weighted * padded[offset : offset + count_rows], axis=0))
        grad_padded = grad_padded.at[offset : offset + count_rows].add(kernel[offset] * weighted)
    return (jnp.stack(kernel_rows), grad_padded[reach : reach + count_rows])


def rate_table():
    attention_fan = max(2 * D // TOK_DEV, 1)
    mixer_rates = jnp.array([attention_fan ** (-0.5), D ** (-0.5)], dtype=jnp.float32)[
        :, None, None
    ]
    return (D ** (-0.5), FF ** (-0.5), D ** (-0.5), mixer_rates, 0.3, 0.3)


def adamw_step(weight, mean_state, square_state, gradient, step_rate):
    mean_next = BETA * mean_state + (1.0 - BETA) * gradient
    square_next = BETA * square_state + (1.0 - BETA) * gradient * gradient
    correct = 1.0 - BETA**STEP_COUNT
    direction = mean_next / correct / (jnp.sqrt(square_next / correct) + EPS_ADAM)
    return (weight - step_rate * (direction + DECAY_WEIGHT * weight), mean_next, square_next)


def branch_total(partial_sum):
    return lax.psum(partial_sum.astype(jnp.bfloat16), "mp").astype(jnp.float32)


def input_total(partial_sum):
    return lax.psum(partial_sum.astype(jnp.bfloat16), "mp").astype(jnp.float32)


def body(
    tokens_in,
    out_cotangent,
    utt_lengths,
    feed_in,
    feed_in_mean,
    feed_in_square,
    feed_out,
    feed_out_mean,
    feed_out_square,
    mixer_in,
    mixer_in_mean,
    mixer_in_square,
    mixer_out,
    mixer_out_mean,
    mixer_out_square,
    norm_vectors,
    norm_vectors_mean,
    norm_vectors_square,
    channel_vectors,
    channel_vectors_mean,
    channel_vectors_square,
):
    count_rows = tokens_in.shape[0]
    local_width = mixer_in.shape[2]
    local_heads = local_width // HEAD_DIM
    heads_shape = (count_rows, local_heads, HEAD_DIM)
    score_scale = HEAD_DIM ** (-0.5)
    first_len = utt_lengths[0, 0]
    second = utt_lengths[0, 1]
    places = jnp.arange(count_rows, dtype=jnp.int32)
    in_first = (places < first_len).astype(jnp.int32)
    in_live = (places < first_len + second).astype(jnp.int32)
    group_ids = in_first + in_live
    positions = places - first_len * (1 - in_first) - second * (1 - in_live)
    live_rows = in_live.astype(jnp.float32)[:, None]
    halfway = HEAD_DIM // 2
    frequency = jnp.exp(
        jnp.arange(halfway, dtype=jnp.float32) * (-2.0 * math.log(10000.0) / HEAD_DIM)
    )
    angles = positions.astype(jnp.float32)[:, None] * frequency[None, :]
    cosine = jnp.cos(angles)[:, None, :]
    sine_part = jnp.sin(angles)[:, None, :]
    allowed = (group_ids[:, None] == group_ids[None, :])[None]
    kernel = channel_vectors[:KERNEL]
    batch_gain = channel_vectors[KERNEL]
    batch_shift = channel_vectors[KERNEL + 1]
    weight_in, weight_out, weight_mix, weight_back = (
        lax.all_gather(feed_in.astype(jnp.bfloat16), "dp", axis=1, tiled=True),
        lax.all_gather(feed_out.astype(jnp.bfloat16), "dp", axis=2, tiled=True),
        lax.all_gather(mixer_in.astype(jnp.bfloat16), "dp", axis=1, tiled=True),
        lax.all_gather(mixer_out.astype(jnp.bfloat16), "dp", axis=2, tiled=True),
    )

    def feed_forward(residual, norm_slot, feed_layer):
        normed, scaled, inverse = norm_forward(
            residual, norm_vectors[norm_slot], norm_vectors[5 + norm_slot]
        )
        normed_low = normed.astype(jnp.bfloat16)
        hidden = product(normed_low, weight_in[feed_layer])
        active = (hidden * jax.nn.sigmoid(hidden)).astype(jnp.bfloat16)
        branch = branch_total(product(active, weight_out[feed_layer]))
        return (residual + 0.5 * branch, (scaled, inverse, normed_low, hidden, active))

    section_zero = tokens_in.astype(jnp.float32)
    section_one, kept_first = feed_forward(section_zero, 0, 0)
    normed, scaled_att, inverse_att = norm_forward(section_one, norm_vectors[1], norm_vectors[6])
    normed_att = normed.astype(jnp.bfloat16)
    projected = jnp.einsum(
        "td,sdc->stc", normed_att, weight_mix[:3], preferred_element_type=jnp.float32
    )
    queries = (rotate(projected[0].reshape(heads_shape), cosine, sine_part) * score_scale).astype(
        jnp.bfloat16
    )
    key_rows = rotate(projected[1].reshape(heads_shape), cosine, sine_part).astype(jnp.bfloat16)
    value_rows = projected[2].reshape(heads_shape).astype(jnp.bfloat16)
    scores = jnp.where(
        allowed,
        jnp.einsum("qhd,khd->hqk", queries, key_rows, preferred_element_type=jnp.float32),
        BIG_NEG,
    )
    largest = jnp.max(scores, axis=-1, keepdims=True)
    exponent = jnp.exp(scores - largest)
    totals = jnp.sum(exponent, axis=-1, keepdims=True)
    softmax_rows = exponent / totals
    log_total = largest + jnp.log(totals)
    context = jnp.einsum(
        "hqk,khd->qhd",
        softmax_rows.astype(jnp.bfloat16),
        value_rows,
        preferred_element_type=jnp.float32,
    )
    context_low = context.reshape(count_rows, local_width).astype(jnp.bfloat16)
    section_two = section_one + branch_total(product(context_low, weight_back[0]))
    normed, scaled_conv, inverse_conv = norm_forward(section_two, norm_vectors[2], norm_vectors[7])
    normed_conv = normed.astype(jnp.bfloat16)
    conv_proj = jnp.einsum(
        "td,sdc->stc", normed_conv, weight_mix[3:], preferred_element_type=jnp.float32
    )
    gate_sig = jax.nn.sigmoid(conv_proj[1])
    gated_rows = conv_proj[0] * gate_sig
    mixed_rows = depthwise(gated_rows, kernel, group_ids)
    batch_stats = lax.psum(
        (
            jnp.sum(live_rows * mixed_rows, axis=0),
            jnp.sum(live_rows * mixed_rows * mixed_rows, axis=0),
            jnp.sum(live_rows),
        ),
        "dp",
    )
    count_live = batch_stats[2]
    mean_batch = batch_stats[0] / count_live
    inverse_batch = lax.rsqrt(batch_stats[1] / count_live - mean_batch * mean_batch + EPS_NORM)
    centred = mixed_rows - mean_batch
    batch_out = centred * inverse_batch * batch_gain + batch_shift
    batch_sig = jax.nn.sigmoid(batch_out)
    active_conv = (batch_out * batch_sig).astype(jnp.bfloat16)
    section_three = section_two + branch_total(product(active_conv, weight_back[1]))
    section_four, kept_second = feed_forward(section_three, 3, 1)
    tokens_out, scaled_last, inverse_last = norm_forward(
        section_four, norm_vectors[4], norm_vectors[9]
    )

    def feed_backward(grad_residual, kept, norm_slot, feed_layer):
        scaled, inverse, normed_low, hidden, active = kept
        grad_branch = (0.5 * grad_residual).astype(jnp.bfloat16)
        grad_down = weight_grad(active, grad_branch)
        hidden_sig = jax.nn.sigmoid(hidden)
        grad_hidden = (
            input_grad(grad_branch, weight_out[feed_layer])
            * hidden_sig
            * (1.0 + hidden * (1.0 - hidden_sig))
        ).astype(jnp.bfloat16)
        grad_up = weight_grad(normed_low, grad_hidden)
        grad_normed = input_total(input_grad(grad_hidden, weight_in[feed_layer]))
        grad_in, grad_gain, grad_shift = norm_backward(
            grad_normed, scaled, inverse, norm_vectors[norm_slot]
        )
        return (grad_residual + grad_in, grad_up, grad_down, grad_gain, grad_shift)

    grad_residual, gain_last, shift_last = norm_backward(
        out_cotangent.astype(jnp.float32), scaled_last, inverse_last, norm_vectors[4]
    )
    grad_residual, up_second, down_second, gain_three, shift_three = feed_backward(
        grad_residual, kept_second, 3, 1
    )
    grad_branch = grad_residual.astype(jnp.bfloat16)
    grad_conv_down = weight_grad(active_conv, grad_branch)
    grad_batch = (
        input_grad(grad_branch, weight_back[1]) * batch_sig * (1.0 + batch_out * (1.0 - batch_sig))
    )
    batch_sums = lax.psum(
        (jnp.sum(grad_batch, axis=0), jnp.sum(grad_batch * centred, axis=0)), "dp"
    )
    grad_var = -0.5 * inverse_batch**3 * batch_gain * batch_sums[1]
    grad_mean = -inverse_batch * batch_gain * batch_sums[0] - 2.0 * mean_batch * grad_var
    grad_mixed = (
        grad_batch * batch_gain * inverse_batch
        + live_rows * (grad_mean + 2.0 * mixed_rows * grad_var) / count_live
    )
    kernel_grads, grad_gated = depthwise_back(grad_mixed, gated_rows, kernel, group_ids)
    grad_conv_up = jnp.stack(
        [grad_gated * gate_sig, grad_gated * conv_proj[0] * gate_sig * (1.0 - gate_sig)]
    ).astype(jnp.bfloat16)
    grad_conv_in = jnp.einsum(
        "td,stc->sdc", normed_conv, grad_conv_up, preferred_element_type=jnp.float32
    )
    grad_normed = input_total(
        jnp.einsum("stc,sdc->td", grad_conv_up, weight_mix[3:], preferred_element_type=jnp.float32)
    )
    grad_in, gain_two, shift_two = norm_backward(
        grad_normed, scaled_conv, inverse_conv, norm_vectors[2]
    )
    grad_residual = grad_residual + grad_in
    grad_branch = grad_residual.astype(jnp.bfloat16)
    grad_att_down = weight_grad(context_low, grad_branch)
    grad_context = input_grad(grad_branch, weight_back[0]).astype(jnp.bfloat16).reshape(heads_shape)
    scores_again = jnp.where(
        allowed,
        jnp.einsum("qhd,khd->hqk", queries, key_rows, preferred_element_type=jnp.float32),
        BIG_NEG,
    )
    softmax_again = jnp.exp(scores_again - log_total)
    grad_softmax = jnp.einsum(
        "qhd,khd->hqk", grad_context, value_rows, preferred_element_type=jnp.float32
    )
    grad_values = jnp.einsum(
        "hqk,qhd->khd",
        softmax_again.astype(jnp.bfloat16),
        grad_context,
        preferred_element_type=jnp.float32,
    )
    grad_scores = (
        softmax_again
        * (grad_softmax - jnp.sum(softmax_again * grad_softmax, axis=-1, keepdims=True))
    ).astype(jnp.bfloat16)
    grad_queries = unrotate(
        jnp.einsum("hqk,khd->qhd", grad_scores, key_rows, preferred_element_type=jnp.float32)
        * score_scale,
        cosine,
        sine_part,
    )
    grad_keys = unrotate(
        jnp.einsum("hqk,qhd->khd", grad_scores, queries, preferred_element_type=jnp.float32),
        cosine,
        sine_part,
    )
    grad_att_up = (
        jnp.stack([grad_queries, grad_keys, grad_values])
        .reshape(3, count_rows, local_width)
        .astype(jnp.bfloat16)
    )
    grad_att_in = jnp.einsum(
        "td,stc->sdc", normed_att, grad_att_up, preferred_element_type=jnp.float32
    )
    grad_normed = input_total(
        jnp.einsum("stc,sdc->td", grad_att_up, weight_mix[:3], preferred_element_type=jnp.float32)
    )
    grad_in, gain_one, shift_one = norm_backward(
        grad_normed, scaled_att, inverse_att, norm_vectors[1]
    )
    grad_residual = grad_residual + grad_in
    grad_residual, up_first, down_first, gain_zero, shift_zero = feed_backward(
        grad_residual, kept_first, 0, 0
    )
    feed_in_grad, feed_out_grad, mixer_in_grad, mixer_out_grad = (
        lax.psum_scatter(jnp.stack([up_first, up_second]), "dp", scatter_dimension=1, tiled=True),
        lax.psum_scatter(
            jnp.stack([down_first, down_second]), "dp", scatter_dimension=2, tiled=True
        ),
        lax.psum_scatter(
            jnp.concatenate([grad_att_in, grad_conv_in], axis=0),
            "dp",
            scatter_dimension=1,
            tiled=True,
        ),
        lax.psum_scatter(
            jnp.stack([grad_att_down, grad_conv_down]), "dp", scatter_dimension=2, tiled=True
        ),
    )
    norm_grads = jnp.stack(
        [
            gain_zero,
            gain_one,
            gain_two,
            gain_three,
            gain_last,
            shift_zero,
            shift_one,
            shift_two,
            shift_three,
            shift_last,
        ]
    )
    norm_total, kernel_total = lax.psum((norm_grads, kernel_grads), "dp")
    channel_grads = jnp.concatenate(
        [kernel_total, (inverse_batch * batch_sums[1])[None], batch_sums[0][None]], axis=0
    )
    rate_list = rate_table()
    feed_in_next, feed_in_mean_next, feed_in_square_next = adamw_step(
        feed_in, feed_in_mean, feed_in_square, feed_in_grad, rate_list[0]
    )
    feed_out_next, feed_out_mean_next, feed_out_square_next = adamw_step(
        feed_out, feed_out_mean, feed_out_square, feed_out_grad, rate_list[1]
    )
    mixer_in_next, mixer_in_mean_next, mixer_in_square_next = adamw_step(
        mixer_in, mixer_in_mean, mixer_in_square, mixer_in_grad, rate_list[2]
    )
    mixer_out_next, mixer_out_mean_next, mixer_out_square_next = adamw_step(
        mixer_out, mixer_out_mean, mixer_out_square, mixer_out_grad, rate_list[3]
    )
    norm_vectors_next, norm_vectors_mean_next, norm_vectors_square_next = adamw_step(
        norm_vectors, norm_vectors_mean, norm_vectors_square, norm_total, rate_list[4]
    )
    channel_vectors_next, channel_vectors_mean_next, channel_vectors_square_next = adamw_step(
        channel_vectors, channel_vectors_mean, channel_vectors_square, channel_grads, rate_list[5]
    )
    return (
        tokens_out,
        grad_residual,
        feed_in_next,
        feed_in_mean_next,
        feed_in_square_next,
        feed_out_next,
        feed_out_mean_next,
        feed_out_square_next,
        mixer_in_next,
        mixer_in_mean_next,
        mixer_in_square_next[:4],
        mixer_in_square_next[4],
        mixer_out_next,
        mixer_out_mean_next,
        mixer_out_square_next,
        norm_vectors_next,
        norm_vectors_mean_next,
        norm_vectors_square_next,
        channel_vectors_next,
        channel_vectors_mean_next,
        channel_vectors_square_next,
    )


MESH = pl.DeviceIdType.MESH
F32 = jnp.float32
BF16 = jnp.bfloat16
ROWS = 256
HALF = 128
QUAD = 64
OCT = 32
SHARD = 64
G_IN0, G_OUT0, G_ATT, G_CONV, G_IN1, G_OUT1 = range(6)


def dot_nn(a, b):
    return lax.dot_general(a, b, (((1,), (0,)), ((), ())), preferred_element_type=F32)


def dot_nt(a, b):
    return lax.dot_general(a, b, (((1,), (1,)), ((), ())), preferred_element_type=F32)


def dot_tn(a, b):
    return lax.dot_general(a, b, (((0,), (0,)), ((), ())), preferred_element_type=F32)


def sigm(v):
    return 1.0 / (1.0 + jnp.exp(-v))


def fused_kernel(
    tok, cot, lens, rot_hi, rot_lo, nv, cv, fi_h, fo_h, mi_h, mo_h,
    tout, tgrad, gfi, gfo, gmi, gmo, ngrad, cgrad,
    fi_f, fo_f, mi_f, mo_f, fi_b, fo_b, mi_b, mo_b,
    w0, w1, w2, w3, w4, w5, xg0, xg1, xg2, xg3, xb0, xb1,
    fh0, fh1, fs0, fs1, hb, qr, kr, vr, ctx, dqkv, pf,
    cu, sg, glu, zc, dd, cw, du, gid, live, rc_t, rs_t, lb,
    xh, inv, res, si, sd, hx, hy, sx, sy, rx, ry, part,
    gs0, gs1, gs2, gs3, gs4, gs5, gi0, gi1, gi2, gi3, gi4, gi5,
    ac0, ac1, ac2, ac3, ac4, ac5, stats, tapm, ngm, nsib, nx, ny, nz, cgm, tstage, cotb,
    ags, agr, rss, rsr, was, war, zs, zr, grs, grr, gas, gar, lss, lsr,
    bns, bnr, nss, nsr, cgs, cgr, outs, outr, cts, ctr, lds,
):
    w = (w0, w1, w2, w3, w4, w5)
    gst = (gs0, gs1, gs2, gs3, gs4, gs5)
    gin = (gi0, gi1, gi2, gi3, gi4, gi5)
    acc = (ac0, ac1, ac2, ac3, ac4, ac5)
    dp = lax.axis_index("dp")
    m = lax.axis_index("mp")
    x = dp % 2
    y = (dp // 2) % 2
    z = dp // 4
    p = dp % 4
    base = z * 4
    px = p + 1 - 2 * x
    py = p + 2 - 4 * y
    pd = 3 - p
    sib = (dp, 1 - m)
    xn = (base + px, m)
    yn = (base + py, m)
    dn = (base + pd, m)
    plane = ((px, xn), (py, yn), (pd, dn))
    inner = (z + 1) // 2 % 2
    others = tuple((z + k) % 4 for k in (1, 2, 3))

    def zdev(zz):
        return (zz * 4 + p, m)

    def remote(src, dst, ssem, rsem, dev):
        return pltpu.make_async_remote_copy(
            src_ref=src, dst_ref=dst, send_sem=ssem, recv_sem=rsem, device_id=dev, device_id_type=MESH
        )

    def rows(start, size):
        return pl.ds(pl.multiple_of(start, size), size)

    def block(b):
        return rows(b * ROWS, ROWS)

    pending = []

    def go_send(copy):
        copy.start()
        pending.append(copy)

    shards = {
        G_IN0: ((fi_h, fi_f, fi_b, slice(0, 1)),),
        G_OUT0: ((fo_h, fo_f, fo_b, slice(0, 1)),),
        G_ATT: ((mi_h, mi_f, mi_b, slice(0, 3)), (mo_h, mo_f, mo_b, slice(0, 1))),
        G_CONV: ((mi_h, mi_f, mi_b, slice(3, 5)), (mo_h, mo_f, mo_b, slice(1, 2))),
        G_IN1: ((fi_h, fi_f, fi_b, slice(1, 2)),),
        G_OUT1: ((fo_h, fo_f, fo_b, slice(1, 2)),),
    }

    def shard_copies(g):
        return [
            pltpu.make_async_copy(src.at[r], dst.at[r], lds.at[g, k])
            for k, (src, dst, _, r) in enumerate(shards[g])
        ]

    for g in range(6):
        for copy in shard_copies(g):
            copy.start()

    def round_shard(g):
        for copy in shard_copies(g):
            copy.wait()
        for _, src, dst, r in shards[g]:
            dst[r] = src[r].astype(BF16)

    barrier = pltpu.get_barrier_semaphore()
    greet = (sib, xn, yn, dn) + tuple(zdev(k) for k in others)
    greet += tuple((base + k, 1 - m) for k in (px, py, pd))
    for dev in greet:
        pl.semaphore_signal(barrier, inc=1, device_id=dev, device_id_type=MESH)
    pl.semaphore_wait(barrier, len(greet))

    def wview(g, start, size):
        r = pl.ds(pl.multiple_of(start, SHARD), size)
        return w[g].at[:, r] if g in (G_ATT, G_CONV) else w[g].at[r]

    def columns(i, wd):
        return pl.ds(pl.multiple_of(i * wd, 128), wd)

    def wpieces(g, peer, owner):
        r = pl.ds(pl.multiple_of(z * ROWS + owner * SHARD, SHARD), SHARD)
        if g == G_ATT:
            return (
                (mi_b.at[0:3, :, columns(peer, 128)], w[g].at[0:3, r]),
                (mo_b.at[0, :, columns(peer, 128)], w[g].at[3, r]),
            )
        if g == G_CONV:
            return (
                (mi_b.at[3:5, :, columns(peer, 128)], w[g].at[0:2, r]),
                (mo_b.at[1, :, columns(peer, 128)], w[g].at[2, r]),
            )
        src = fi_b if g in (G_IN0, G_IN1) else fo_b
        layer = 0 if g in (G_IN0, G_OUT0) else 1
        return ((src.at[layer, :, columns(peer, 512)], w[g].at[r]),)

    def plane_start(g):
        round_shard(g)
        for r, (peer, dev) in enumerate(plane):
            for k, (src, dst) in enumerate(wpieces(g, peer, p)):
                go_send(remote(src, dst, was.at[g, r, k], war.at[g, r, k], dev))
        for k, (src, dst) in enumerate(wpieces(g, p, p)):
            pltpu.make_async_copy(src, dst, was.at[g, 3, k]).start()

    def plane_wait(g):
        for r, (peer, dev) in enumerate(plane):
            for k, (_, dst) in enumerate(wpieces(g, peer, peer)):
                remote(dst, dst, was.at[g, r, k], war.at[g, r, k], dev).wait_recv()
        for k, (src, dst) in enumerate(wpieces(g, p, p)):
            pltpu.make_async_copy(src, dst, was.at[g, 3, k]).wait()

    targets = {0: (2, 1), 1: (3, 0, 2), 2: (0, 3, 1), 3: (1, 2)}
    far = {1: (3, 0), 2: (0, 3)}

    def zcopy(g, owner, k, to):
        part_w = wview(g, owner * ROWS, ROWS)
        return remote(part_w, part_w, zs.at[g, k], zr.at[g, owner], zdev(to))

    def zpiece(g, owner, k, to, peer):
        v = wview(g, owner * ROWS + peer * SHARD, SHARD)
        return remote(v, v, zs.at[g, k], zr.at[g, owner], zdev(to))

    def line_pieces(g, peer):
        for zz, tos in targets.items():

            @pl.when(z == zz)
            def _():
                for k, to in enumerate(tos):
                    zpiece(g, zz, k, to, peer).start()

    def line_start_own(g):
        for k, (src, dst) in enumerate(wpieces(g, p, p)):
            pltpu.make_async_copy(src, dst, was.at[g, 3, k]).wait()
        line_pieces(g, p)

    def line_start_rest(g):
        for r, (peer, dev) in enumerate(plane):
            for k, (_, dst) in enumerate(wpieces(g, peer, peer)):
                remote(dst, dst, was.at[g, r, k], war.at[g, r, k], dev).wait_recv()
            line_pieces(g, peer)

    def line_start(g):
        plane_wait(g)
        for zz, tos in targets.items():

            @pl.when(z == zz)
            def _():
                for k, to in enumerate(tos):
                    zcopy(g, zz, k, to).start()

    def line_pass(g):
        for zz, (owner, to) in far.items():

            @pl.when(z == zz)
            def _():
                zcopy(g, owner, 3, to).wait_recv()
                zcopy(g, owner, 3, to).start()

    def line_ready(g):
        for zz in range(4):

            @pl.when(z == zz)
            def _():
                for owner in range(4):
                    if owner != zz and (zz not in far or far[zz][0] != owner):
                        zcopy(g, owner, 0, zz).wait_recv()

    def line_done(g):
        for zz, tos in targets.items():

            @pl.when(z == zz)
            def _():
                for k, to in enumerate(tos):
                    zcopy(g, zz, k, to).wait_send()
                if zz in far:
                    zcopy(g, far[zz][0], 3, far[zz][1]).wait_send()

    def pieces(s):
        return lambda b, c, off, size: pl.ds(
            pl.multiple_of(s * 2 * ROWS + b * HALF + c * QUAD + off, OCT), size
        )

    def blocks_of_chips(b, c, off, size):
        return pl.ds(pl.multiple_of(place_of(b) * ROWS + c * HALF + off, QUAD), size)

    def place_of(b):
        return b % 2 * 2 + b // 2

    def mine(s):
        return pieces(s)(p, m, 0, QUAD)

    def settle(sends):
        for k in sends:
            k.wait_send()
        sends.clear()

    def gather(xg, where, half, sem, near, far_piece, name, sends):
        quad = half // 2

        def c(i, b, core, off, size, dev):
            r = xg.at[where(b, core, off, size)]
            return remote(r, r, ags.at[sem, i], agr.at[sem, i], dev)

        def start(*a):
            k = c(*a)
            k.start()
            sends.append(k)

        n = 1 - m
        settle(sends)
        start(1, p, m, 0, quad, xn)
        start(3, p, m, quad, quad, yn)
        start(2, p, m, quad, quad, xn)
        start(4, p, m, 0, quad, yn)
        start(0, p, m, 0, half, sib)
        yield name + ".0"
        c(1, px, m, 0, quad, xn).wait_recv()
        start(5, px, m, 0, quad, yn)
        c(3, py, m, quad, quad, yn).wait_recv()
        start(6, py, m, quad, quad, xn)
        yield name + ".1"
        c(2, px, m, quad, quad, xn).wait_recv()
        start(7, px, m, 0, half, sib)
        c(4, py, m, 0, quad, yn).wait_recv()
        start(8, py, m, 0, half, sib)
        yield name + ".1b"
        c(0, p, n, 0, half, sib).wait_recv()
        c(7, px, n, 0, half, sib).wait_recv()
        near()
        yield name + ".2"
        c(5, pd, m, 0, quad, yn).wait_recv()
        start(9, pd, m, 0, quad, sib)
        c(6, pd, m, quad, quad, xn).wait_recv()
        start(10, pd, m, quad, quad, sib)
        yield name + ".3"
        c(8, py, n, 0, half, sib).wait_recv()
        c(9, pd, n, 0, quad, sib).wait_recv()
        c(10, pd, n, quad, quad, sib).wait_recv()
        far_piece()

    def scatter(s, compute, name, sends):
        def csib(i):
            src = part.at[s, i % 2, held(i, 1 - m)]
            return remote(src, si.at[s, i], rss.at[s, i], rsr.at[s, i], sib)

        def start(k):
            k.start()
            sends.append(k)

        def held(i, core, off=0, size=QUAD):
            chip_x = x if i > 1 else 1 - x
            return pl.ds(pl.multiple_of(chip_x * HALF + core * QUAD + off, OCT), size)

        def mine_of(i, off=0, size=QUAD):
            return part[s, i % 2, held(i, m, off, size), :].astype(F32)

        a = slice(0, OCT)
        bb = slice(OCT, QUAD)
        chx = remote(sd.at[s, a], hx.at[s], rss.at[s, 4], rsr.at[s, 4], xn)
        chy = remote(sd.at[s, bb], hy.at[s], rss.at[s, 5], rsr.at[s, 5], yn)
        cxa = remote(sx.at[s, a], rx.at[s, a], rss.at[s, 6], rsr.at[s, 6], xn)
        cxb = remote(sx.at[s, bb], rx.at[s, bb], rss.at[s, 7], rsr.at[s, 7], xn)
        cyb = remote(sy.at[s, bb], ry.at[s, bb], rss.at[s, 8], rsr.at[s, 8], yn)
        cya = remote(sy.at[s, a], ry.at[s, a], rss.at[s, 9], rsr.at[s, 9], yn)
        settle(sends)
        part[s, 0] = compute(1 - y).astype(BF16)
        start(csib(0))
        start(csib(2))
        part[s, 1] = compute(y).astype(BF16)
        start(csib(1))
        start(csib(3))
        yield name + ".0"
        csib(0).wait_recv()
        sd[s] = (mine_of(0) + si[s, 0].astype(F32)).astype(BF16)
        start(chx)
        start(chy)
        csib(1).wait_recv()
        sx[s, a, :] = (mine_of(1, 0, OCT) + si[s, 1, a, :].astype(F32)).astype(BF16)
        start(cxa)
        csib(2).wait_recv()
        sy[s, bb, :] = (mine_of(2, OCT, OCT) + si[s, 2, bb, :].astype(F32)).astype(BF16)
        start(cyb)
        yield name + ".1"
        chy.wait_recv()
        sx[s, bb, :] = (
            mine_of(1, OCT, OCT) + si[s, 1, bb, :].astype(F32) + hy[s].astype(F32)
        ).astype(BF16)
        start(cxb)
        chx.wait_recv()
        sy[s, a, :] = (
            mine_of(2, 0, OCT) + si[s, 2, a, :].astype(F32) + hx[s].astype(F32)
        ).astype(BF16)
        start(cya)
        yield name + ".2"
        csib(3).wait_recv()
        cxa.wait_recv()
        cyb.wait_recv()
        cxb.wait_recv()
        cya.wait_recv()
        return mine_of(3) + si[s, 3].astype(F32) + rx[s].astype(F32) + ry[s].astype(F32)

    def hats(v):
        centre = v - jnp.mean(v, axis=-1, keepdims=True)
        scale = lax.rsqrt(jnp.mean(centre * centre, axis=-1, keepdims=True) + EPS_NORM)
        return centre * scale, scale

    def norm(v, i, s):
        hat, scale = hats(v)
        xh[i, s] = hat
        inv[i, s] = jnp.broadcast_to(scale, (QUAD, 128))
        return hat * nv[i : i + 1, :] + nv[5 + i : 6 + i, :]

    def norm_back(g, i, s):
        hat = xh[i, s]
        scale = inv[i, s, :, 0:1]
        gains = jnp.sum(g * hat, axis=0, keepdims=True)
        shifts = jnp.sum(g, axis=0, keepdims=True)
        if s == 0:
            ngm[i : i + 1, :] = gains
            ngm[5 + i : 6 + i, :] = shifts
        else:
            ngm[i : i + 1, :] = ngm[i : i + 1, :] + gains
            ngm[5 + i : 6 + i, :] = ngm[5 + i : 6 + i, :] + shifts
        e = g * nv[i : i + 1, :]
        return scale * (
            e
            - jnp.mean(e, axis=-1, keepdims=True)
            - hat * jnp.mean(e * hat, axis=-1, keepdims=True)
        )

    outer = 1 - inner
    c0 = 3 * (1 - z // 2)
    c1 = 2 - z // 2
    c2 = z + 1 - 2 * (z % 2)
    order = (c0, c1, c2, z)

    def grad_chunk(g, k):
        zz = order[k]
        cols = pl.ds(pl.multiple_of(zz * ROWS, ROWS), ROWS)
        if g == G_IN0:
            v = dot_tn(xg0[:, cols], hb[...])
        elif g == G_OUT0:
            v = dot_tn(xb1[:, cols], fs0[...])
        elif g == G_IN1:
            v = dot_tn(xg3[:, cols], hb[...])
        elif g == G_OUT1:
            v = dot_tn(xb0[:, cols], fs1[...])
        if g == G_ATT:
            v = dot_tn(xg1[:, cols], dqkv[...]).astype(BF16)
            for k in range(3):
                gst[g][zz, k] = v[:, k * 128 : (k + 1) * 128]
            gst[g][zz, 3] = dot_tn(xb0[:, cols], ctx[...]).astype(BF16)
        elif g == G_CONV:
            v = dot_tn(xg2[:, cols], du[...]).astype(BF16)
            for k in range(2):
                gst[g][zz, k] = v[:, k * 128 : (k + 1) * 128]
            gst[g][zz, 2] = dot_tn(xb1[:, cols], cw[...]).astype(BF16)
        else:
            gst[g][zz] = v.astype(BF16)

    neighbour = 1 + z // 2

    def acc_copy(g):
        return remote(gst[g].at[c0], acc[g], grs.at[g, 0], grr.at[g, 3], zdev(neighbour))

    def slot_copy(g, k):
        zz = order[k]
        if k == 0:
            slot = 1
        elif k == 1:
            slot = 1 + outer
        else:
            slot = 0
        return remote(gst[g].at[zz], gin[g].at[slot], grs.at[g, k], grr.at[g, slot], zdev(zz))

    def grad_send(g, k):
        if k == 0:

            @pl.when(outer == 1)
            def _():
                acc_copy(g).start()
        elif k < 3:
            slot_copy(g, k).start()

    def grad_acc(g):
        @pl.when(inner == 1)
        def _():
            acc_copy(g).wait_recv()
            gst[g][c0] = (gst[g][c0].astype(F32) + acc[g][...].astype(F32)).astype(BF16)
            slot_copy(g, 0).start()

    def gpieces(g, peer, owner):
        r = pl.ds(pl.multiple_of(peer * SHARD, SHARD), SHARD)
        if g == G_ATT:
            return (
                (gst[g].at[z, 0:3, r], gmi.at[0:3, :, columns(owner, 128)]),
                (gst[g].at[z, 3, r], gmo.at[0, :, columns(owner, 128)]),
            )
        if g == G_CONV:
            return (
                (gst[g].at[z, 0:2, r], gmi.at[3:5, :, columns(owner, 128)]),
                (gst[g].at[z, 2, r], gmo.at[1, :, columns(owner, 128)]),
            )
        dst = gfi if g in (G_IN0, G_IN1) else gfo
        layer = 0 if g in (G_IN0, G_OUT0) else 1
        return ((gst[g].at[z, r], dst.at[layer, :, columns(owner, 512)]),)

    def gplane(g):
        return [
            remote(src, dst, gas.at[g, r, k], gar.at[g, r, k], dev)
            for r, (peer, dev) in enumerate(plane)
            for k, (src, dst) in enumerate(gpieces(g, peer, p))
        ] + [
            pltpu.make_async_copy(src, dst, gas.at[g, 3, k])
            for k, (src, dst) in enumerate(gpieces(g, p, p))
        ]

    def slot_wait(g, slot):
        remote(gin[g].at[slot], gin[g].at[slot], grs.at[g, 1], grr.at[g, slot], sib).wait_recv()

    def grad_final(g):
        slot_wait(g, 0)
        slot_wait(g, 1)
        t = gst[g][z].astype(F32) + gin[g][0].astype(F32) + gin[g][1].astype(F32)
        keep_t = t

        @pl.when(outer == 1)
        def _():
            gst[g][z] = keep_t.astype(BF16)

        @pl.when(inner == 1)
        def _():
            slot_wait(g, 2)
            gst[g][z] = (keep_t + gin[g][2].astype(F32)).astype(BF16)

        for copy in gplane(g):
            copy.start()

    def grad_done(g):
        for r, (peer, dev) in enumerate(plane):
            for k, (_, dst) in enumerate(gpieces(g, peer, peer)):
                remote(dst, dst, gas.at[g, r, k], gar.at[g, r, k], dev).wait_recv()
        for i, copy in enumerate(gplane(g)):
            if i < 3 * len(gpieces(g, p, p)):
                copy.wait_send()
            else:
                copy.wait()

        @pl.when(outer == 1)
        def _():
            acc_copy(g).wait_send()

        @pl.when(inner == 1)
        def _():
            slot_copy(g, 0).wait_send()

        slot_copy(g, 1).wait_send()
        slot_copy(g, 2).wait_send()

    def line_share(buf, sem_s, sem_r, start):
        for k in range(3):
            to = others[k]
            if start:
                remote(buf.at[z], buf.at[z], sem_s.at[k], sem_r.at[2 - k], zdev(to)).start()
            else:
                frm = others[2 - k]
                remote(buf.at[z], buf.at[z], sem_s.at[k], sem_r.at[2 - k], zdev(to)).wait_send()
                remote(buf.at[frm], buf.at[frm], sem_s.at[k], sem_r.at[2 - k], zdev(frm)).wait_recv()

    stats[...] = jnp.zeros_like(stats)
    tapm[...] = jnp.zeros_like(tapm)
    ngm[10:16, :] = jnp.zeros((6, D), F32)
    lb[p, 0:1, :] = jnp.broadcast_to(lens[0:1, 0:1].astype(F32), (1, ROWS))
    lb[p, 1:2, :] = jnp.broadcast_to(lens[0:1, 1:2].astype(F32), (1, ROWS))
    lb[p, 2:8, :] = jnp.zeros((6, ROWS), F32)
    plane_start(G_IN0)
    for r in range(3):
        peer, dev = plane[r]
        remote(lb.at[p], lb.at[p], lss.at[r], lsr.at[r], dev).start()
    load = pltpu.make_async_copy(
        tok.at[pl.ds(pl.multiple_of(m * HALF, HALF), HALF)],
        xg0.at[blocks_of_chips(p, m, 0, HALF)],
        cts.at[1],
    )
    load.start()
    load.wait()

    def nothing():
        return None

    def either(here, a, b):
        @pl.when(here)
        def _():
            a()

        @pl.when(jnp.logical_not(here))
        def _():
            b()

    def cot_rows(owner_x):
        return cot.at[pl.ds(pl.multiple_of(owner_x * HALF + m * QUAD, QUAD), QUAD)]

    def cot_away():
        return remote(cot_rows(1 - x), cotb.at[x], cts.at[0], ctr.at[0], xn)

    def cot_local():
        return pltpu.make_async_copy(cot_rows(x), cotb.at[x], ctr.at[1])

    def cot_start():
        cot_away().start()
        cot_local().start()

    def cot_wait():
        cot_away().wait_send()
        remote(cotb.at[1 - x], cotb.at[1 - x], cts.at[0], ctr.at[0], xn).wait_recv()
        cot_local().wait()

    def tables():
        for r in range(3):
            peer, dev = plane[r]
            remote(lb.at[p], lb.at[p], lss.at[r], lsr.at[r], dev).wait_send()
            remote(lb.at[peer], lb.at[peer], lss.at[r], lsr.at[r], dev).wait_recv()
        place = lax.broadcasted_iota(jnp.int32, (ROWS, ROWS), 0).astype(F32)
        lane = lax.broadcasted_iota(jnp.int32, (ROWS, ROWS), 1).astype(F32)
        for b in range(4):
            l0 = lb[b % 2 * 2 + b // 2, 0:1, :]
            l1 = lb[b % 2 * 2 + b // 2, 1:2, :]
            first_in = jnp.where(place < l0, 1.0, 0.0)
            live_in = jnp.where(place < l0 + l1, 1.0, 0.0)
            at = place - l0 * (1.0 - first_in) - l1 * (1.0 - live_in)
            r = slice(b * ROWS, (b + 1) * ROWS)
            gid[r, :] = 3.0 * b + first_in[:, :128] + live_in[:, :128]
            live[r, :] = live_in[:, :128]
            hot = jnp.where(at == lane, 1.0, 0.0).astype(BF16)
            t = dot_nn(hot, rot_hi[...]) + dot_nn(hot, rot_lo[...])
            rc_t[r, :] = t[:, :128]
            rs_t[r, :] = t[:, 128:]

    first_sends = []
    opening = gather(xg0, blocks_of_chips, HALF, 2, nothing, nothing, "G0", first_sends)
    line_start_own(G_IN0)
    next(opening)
    line_start_rest(G_IN0)
    next(opening)
    plane_start(G_OUT0)
    next(opening)
    next(opening)
    tables()
    next(opening)
    line_pass(G_IN0)
    line_start(G_OUT0)
    for _ in opening:
        pass
    settle(first_sends)
    for g in (G_ATT, G_CONV, G_IN1, G_OUT1):
        plane_start(g)
    cot_start()
    for s in range(2):
        first = xg0[mine(s), :].astype(F32)
        res[s] = first
        norm(first, 0, s)

    @pl.loop(0, 8)
    def _(i):
        r = rows(i * HALF, HALF)
        hat, _ = hats(xg0[r, :].astype(F32))
        xg0[r, :] = (hat * nv[0:1, :] + nv[5:6, :]).astype(BF16)

    def block_rows(s, q):
        return pl.ds(pl.multiple_of((2 * s + q) * ROWS, ROWS), ROWS)

    def ff_hidden(s, xg, g, fh, fs):
        def f(q):
            r = block_rows(s, q)
            h = dot_nn(xg[r, :], w[g][...])
            fh[r, :] = h
            fs[r, :] = (h * sigm(h)).astype(BF16)

        return f

    def wide(g, first, last):
        return jnp.concatenate([w[g][k] for k in range(first, last)], axis=1)

    def part_nt(s, lhs, weight):
        def f(q):
            return dot_nt(lhs[block_rows(s, q), :], weight())

        return f

    def whole(g):
        return lambda: w[g][...]

    def turn(v, r):
        return v * rc_t[r, :] + pltpu.roll(v, 64, 1) * rs_t[r, :]

    def turn_back(v, r):
        return v * rc_t[r, :] - pltpu.roll(v, 64, 1) * rs_t[r, :]

    lane_row = lax.broadcasted_iota(jnp.int32, (1, ROWS), 1).astype(F32)

    def attend(s):
        def f(q):
            r = block_rows(s, q)
            b = 2 * q + s
            t = dot_nn(xg1[r, :], wide(G_ATT, 0, 3))
            qs = (turn(t[:, 0:128], r) * (HEAD_DIM**-0.5)).astype(BF16)
            k = turn(t[:, 128:256], r).astype(BF16)
            v = t[:, 256:384].astype(BF16)
            qr[r, :] = qs
            kr[r, :] = k
            vr[r, :] = v
            sc = dot_nt(qs, k)
            l0 = lb[b, 0:1, :]
            l1 = lb[b, 1:2, :]
            gk = (
                3.0 * (2 * s + q).astype(F32)
                + jnp.where(lane_row < l0, 1.0, 0.0)
                + jnp.where(lane_row < l0 + l1, 1.0, 0.0)
            )
            gq = gid[r, :]
            gq = jnp.concatenate([gq, gq], axis=1)
            sc = jnp.where(gq == gk, sc, BIG_NEG)
            e = jnp.exp(sc - jnp.max(sc, axis=-1, keepdims=True))
            pr = e / jnp.sum(e, axis=-1, keepdims=True)
            pf[r, :] = pr
            ctx[r, :] = dot_nn(pr.astype(BF16), v).astype(BF16)

        return f

    def attend_back(s):
        def f(q):
            r = block_rows(s, q)
            dc = dot_nn(xb0[r, :], w[G_ATT][3]).astype(BF16)
            pr = pf[r, :]
            k = kr[r, :]
            dp_ = dot_nt(dc, vr[r, :])
            dqkv[r, 256:384] = dot_tn(pr.astype(BF16), dc).astype(BF16)
            sb = (pr * (dp_ - jnp.sum(pr * dp_, axis=-1, keepdims=True))).astype(BF16)
            dqkv[r, 0:128] = turn_back(dot_nn(sb, k) * (HEAD_DIM**-0.5), r).astype(BF16)
            dqkv[r, 128:256] = turn_back(dot_tn(sb, qr[r, :]), r).astype(BF16)

        return f

    chan = pl.ds(pl.multiple_of(p * 128, 128), 128)
    taps = [cv[j : j + 1, chan] for j in range(KERNEL)]
    gain = cv[KERNEL : KERNEL + 1, chan]
    shift = cv[KERNEL + 1 : KERNEL + 2, chan]
    count = 2 * ROWS
    bn = {}

    def conv_in(s):
        def f(q):
            r = block_rows(s, q)
            t = dot_nn(xg2[r, :], wide(G_CONV, 0, 2))
            sig = sigm(t[:, 128:256])
            cu[r, :] = t[:, 0:128]
            sg[r, :] = sig
            glu[r, :] = t[:, 0:128] * sig

        return f

    def span(s):
        return slice(s * count, (s + 1) * count)

    def same(s, j):
        ids = gid[span(s), :]
        return jnp.where(pltpu.roll(ids, (2 - j) % count, 0) == ids, 1.0, 0.0)

    def add_row(ref, z_, row, value, s):
        at = slice(row, row + 1)
        ref[z_, at, :] = value if s == 0 else ref[z_, at, :] + value

    def mix(s):
        g_all = glu[span(s), :]
        mixed = taps[2] * g_all
        for j in (0, 1, 3, 4):
            mixed = mixed + taps[j] * pltpu.roll(g_all, (2 - j) % count, 0) * same(s, j)
        zc[span(s), :] = mixed
        lv = live[span(s), :]
        add_row(stats.at[0], z, 0, jnp.sum(lv * mixed, axis=0, keepdims=True), s)
        add_row(stats.at[0], z, 1, jnp.sum(lv * mixed * mixed, axis=0, keepdims=True), s)
        add_row(stats.at[0], z, 2, jnp.sum(lv, axis=0, keepdims=True), s)

    def bn_forward():
        line_share(stats.at[0], bns.at[0], bnr.at[0], True)
        line_pass(G_IN1)
        line_start(G_OUT1)
        line_share(stats.at[0], bns.at[0], bnr.at[0], False)
        tot = stats[0, 0] + stats[0, 1] + stats[0, 2] + stats[0, 3]
        bn["n"] = tot[2:3, :]
        bn["mean"] = tot[0:1, :] / bn["n"]
        bn["inv"] = lax.rsqrt(tot[1:2, :] / bn["n"] - bn["mean"] * bn["mean"] + EPS_NORM)

    def conv_out(s):
        def f(q):
            r = block_rows(s, q)
            v = (zc[r, :] - bn["mean"]) * bn["inv"] * gain + shift
            cw[r, :] = (v * sigm(v)).astype(BF16)
            return dot_nt(cw[r, :], w[G_CONV][2])

        return f

    def conv_back(s):
        def f(q):
            r = block_rows(s, q)
            v = (zc[r, :] - bn["mean"]) * bn["inv"] * gain + shift
            sig = sigm(v)
            dd[r, :] = dot_nn(xb1[r, :], w[G_CONV][2]) * sig * (1.0 + v * (1.0 - sig))

        return f

    def batch_sums(s):
        d_all = dd[span(s), :]
        add_row(stats.at[1], z, 0, jnp.sum(d_all, axis=0, keepdims=True), s)
        centred = zc[span(s), :] - bn["mean"]
        add_row(stats.at[1], z, 1, jnp.sum(d_all * centred, axis=0, keepdims=True), s)

    def bn_backward():
        line_share(stats.at[1], bns.at[1], bnr.at[1], True)
        for k in range(4):
            grad_chunk(G_IN1, k)
        line_share(stats.at[1], bns.at[1], bnr.at[1], False)
        tot = stats[1, 0] + stats[1, 1] + stats[1, 2] + stats[1, 3]
        i = bn["inv"]
        bn["s1"] = tot[0:1, :]
        bn["s2"] = tot[1:2, :]
        bn["dv"] = -0.5 * i * i * i * gain * bn["s2"]
        bn["dm"] = -i * gain * bn["s1"] - 2.0 * bn["mean"] * bn["dv"]

    def unmix(s):
        r = span(s)
        dz = dd[r, :] * (gain * bn["inv"]) + live[r, :] * (
            (bn["dm"] + 2.0 * zc[r, :] * bn["dv"]) / bn["n"]
        )
        g_all = glu[r, :]
        back = jnp.zeros_like(dz)
        for j in range(KERNEL):
            if j == 2:
                weighted = dz
                moved = g_all
            else:
                weighted = dz * same(s, j)
                moved = pltpu.roll(g_all, (2 - j) % count, 0)
            add_row(tapm, z, j, jnp.sum(weighted * moved, axis=0, keepdims=True), s)
            weighted = taps[j] * weighted
            if j != 2:
                weighted = pltpu.roll(weighted, (j - 2) % count, 0)
            back = back + weighted
        s_all = sg[r, :]
        du[r, 0:128] = (back * s_all).astype(BF16)
        du[r, 128:256] = (back * cu[r, :] * s_all * (1.0 - s_all)).astype(BF16)

    def ff_back(s, xb, g, fh):
        def f(q):
            r = block_rows(s, q)
            h = fh[r, :]
            sig = sigm(h)
            d = dot_nn(xb[r, :], w[g][...])
            hb[r, :] = (d * sig * (1.0 + h * (1.0 - sig))).astype(BF16)

        return f

    def out_rows(out, owner_x, core):
        return out.at[pl.ds(pl.multiple_of(owner_x * HALF + core * QUAD, QUAD), QUAD)]

    def give_out(i, s, out):
        there = out_rows(out, x, m)
        src = tstage.at[i, s]
        r_sem = outr.at[i, x, m]

        def a():
            pltpu.make_async_copy(src, there, r_sem).start()
            remote(src, there, outs.at[i, s, 0], r_sem, sib).start()

        def b():
            remote(src, there, outs.at[i, s, 0], r_sem, xn).start()
            remote(src, there, outs.at[i, s, 1], r_sem, (base + px, 1 - m)).start()

        either(x == s, a, b)

    def out_wait(i, out):
        there = out_rows(out, x, m)
        for s in range(2):
            src = tstage.at[i, s]
            remote(src, there, outs.at[i, s, 0], outr.at[i, x, m], xn).wait_send()

            @pl.when(x != s)
            def _():
                remote(src, there, outs.at[i, s, 1], outr.at[i, x, m], xn).wait_send()

        for cx in range(2):
            for cm in range(2):
                here = out.at[cx * HALF + cm * QUAD : cx * HALF + (cm + 1) * QUAD]
                remote(here, here, outs.at[i, 0, 0], outr.at[i, cx, cm], sib).wait_recv()

    def stream(s):
        g_sends = []
        r_sends = []
        at = mine(s)

        def take(xg, compute, name, ready=None):
            def near():
                if ready is not None and s == 0:
                    line_ready(ready)
                compute(y)

            return gather(xg, pieces(s), QUAD, s, near, lambda: compute(1 - y), name, g_sends)

        def give(compute, name):
            return scatter(s, compute, name, r_sends)

        hidden = ff_hidden(s, xg0, G_IN0, fh0, fs0)
        hidden(0)
        hidden(1)
        yield "W"
        t = yield from give(part_nt(s, fs0, whole(G_OUT0)), "R0")
        v = res[s] + 0.5 * t
        res[s] = v
        xg1[at, :] = norm(v, 1, s).astype(BF16)
        yield from take(xg1, attend(s), "G1", G_ATT)
        t = yield from give(part_nt(s, ctx, lambda: w[G_ATT][3]), "R1")
        v = res[s] + t
        res[s] = v
        xg2[at, :] = norm(v, 2, s).astype(BF16)
        yield from take(xg2, conv_in(s), "G2", G_CONV)
        mix(s)
        yield "BN1"
        t = yield from give(conv_out(s), "R2")
        v = res[s] + t
        res[s] = v
        xg3[at, :] = norm(v, 3, s).astype(BF16)
        yield from take(xg3, ff_hidden(s, xg3, G_IN1, fh1, fs1), "G3", G_IN1)
        if s == 0:
            line_ready(G_OUT1)
        t = yield from give(part_nt(s, fs1, whole(G_OUT1)), "R3")
        tstage[0, s] = norm(res[s] + 0.5 * t, 4, s).astype(BF16)
        if s == 0:
            cot_wait()
        v = norm_back(cotb[s].astype(F32), 4, s)
        res[s] = v
        xb0[at, :] = (0.5 * v).astype(BF16)
        yield from take(xb0, ff_back(s, xb0, G_OUT1, fh1), "H3")
        t = yield from give(part_nt(s, hb, whole(G_IN1)), "Q3")
        v = res[s] + norm_back(t, 3, s)
        res[s] = v
        xb1[at, :] = v.astype(BF16)
        yield from take(xb1, conv_back(s), "H2")
        batch_sums(s)
        yield "BN2"
        unmix(s)
        yield "TAPS"
        t = yield from give(part_nt(s, du, lambda: wide(G_CONV, 0, 2)), "Q2")
        v = res[s] + norm_back(t, 2, s)
        res[s] = v
        xb0[at, :] = v.astype(BF16)
        yield from take(xb0, attend_back(s), "H1")
        t = yield from give(part_nt(s, dqkv, lambda: wide(G_ATT, 0, 3)), "Q1")
        v = res[s] + norm_back(t, 1, s)
        res[s] = v
        xb1[at, :] = (0.5 * v).astype(BF16)
        yield from take(xb1, ff_back(s, xb1, G_OUT0, fh0), "H0")
        yield "TAIL"
        t = yield from give(part_nt(s, hb, whole(G_IN0)), "Q0")
        tstage[1, s] = (res[s] + norm_back(t, 0, s)).astype(BF16)
        give_out(1, s, tgrad)
        settle(g_sends)
        settle(r_sends)

    queue = []

    def chunks(g, send):
        def one(k):
            def f():
                grad_chunk(g, k)
                if send:
                    grad_send(g, k)

            return f

        return [one(k) for k in range(4)]

    def first_feed():
        line_pass(G_OUT0)
        line_start(G_ATT)
        line_ready(G_OUT0)

    def tap_share():
        line_share(tapm, bns.at[2], bnr.at[2], True)
        for k in range(3):
            grad_send(G_IN1, k)

    def tail():
        for f in chunks(G_OUT0, True) + chunks(G_IN0, True):
            f()
        for s in range(2):
            give_out(0, s, tout)

    def passing(g, following):
        def f():
            line_pass(g)
            if following is not None:
                line_start(following)

        return f

    meet = {
        "W": first_feed, "BN1": bn_forward, "BN2": bn_backward, "TAPS": tap_share, "TAIL": tail,
    }
    after = {
        "R0.2": [passing(G_ATT, G_CONV)],
        "R1.1": [passing(G_CONV, G_IN1)],
        "G3.0": [passing(G_OUT1, None)],
        "Q3.0": chunks(G_OUT1, True),
        "H2.0": [lambda: grad_acc(G_OUT1)],
        "Q2.0": chunks(G_CONV, True),
        "Q2.2": [lambda: grad_acc(G_IN1)],
        "H1.1": [lambda: grad_final(G_OUT1)],
        "H1.2": [lambda: grad_acc(G_CONV)],
        "Q1.0": chunks(G_ATT, True),
        "Q1.2": [lambda: grad_final(G_IN1)],
        "H0.1": [lambda: grad_acc(G_ATT)],
        "H0.2": [lambda: grad_final(G_CONV)],
        "Q0.1": [lambda: grad_acc(G_OUT0)],
    }
    line_ready(G_IN0)
    streams = [stream(0), stream(1)]
    state = ["", ""]
    while streams[1] is not None:
        for s in range(2):
            if streams[s] is None:
                continue
            try:
                state[s] = next(streams[s])
            except StopIteration:
                streams[s] = None
                continue
            if s == 1:
                queue.extend(after.get(state[s], []))
            if queue:
                queue.pop(0)()
            if s == 1 and state[s] in meet:
                while queue:
                    queue.pop(0)()
                meet[state[s]]()
    while queue:
        queue.pop(0)()
    grad_final(G_ATT)
    grad_acc(G_IN0)

    def swap(src, dst, k, dev):
        copy = remote(src, dst, nss.at[k], nsr.at[k], dev)
        copy.start()
        copy.wait()

    swap(ngm, nsib, 0, sib)
    ngm[...] = ngm[...] + nsib[...]
    swap(ngm, nx, 1, xn)
    ngm[...] = ngm[...] + nx[...]
    swap(ngm, ny, 2, yn)
    nz[z] = ngm[...] + ny[...]
    line_share(nz, nss.at[pl.ds(3, 3)], nsr.at[pl.ds(3, 3)], True)
    line_share(tapm, bns.at[2], bnr.at[2], False)
    cgm[...] = tapm[0] + tapm[1] + tapm[2] + tapm[3]
    cgm[5:6, :] = bn["inv"] * bn["s2"]
    cgm[6:7, :] = bn["s1"]
    cgrad[:, chan] = cgm[...]
    for r in range(3):
        remote(cgm, cgrad.at[:, chan], cgs.at[r], cgr.at[r], plane[r][1]).start()
    grad_final(G_OUT0)
    line_share(nz, nss.at[pl.ds(3, 3)], nsr.at[pl.ds(3, 3)], False)
    ngrad[...] = nz[0] + nz[1] + nz[2] + nz[3]
    for r in range(3):
        peer, dev = plane[r]
        there = cgrad.at[:, pl.ds(pl.multiple_of(peer * 128, 128), 128)]
        remote(there, there, cgs.at[r], cgr.at[r], dev).wait_recv()
        remote(cgm, cgrad.at[:, chan], cgs.at[r], cgr.at[r], dev).wait_send()
    grad_final(G_IN0)
    out_wait(0, tout)
    out_wait(1, tgrad)
    for copy in pending:
        copy.wait_send()
    for g in range(6):
        line_done(g)
        grad_done(g)


def group_shape(g, rows):
    if g == G_ATT:
        return (4, rows, 128)
    if g == G_CONV:
        return (3, rows, 128)
    return (rows, 512)


def rotation_tables():
    half = HEAD_DIM // 2
    frequency = np.exp(np.arange(half, dtype=np.float32) * np.float32(-2.0 * math.log(10000.0) / HEAD_DIM))
    angles = np.arange(ROWS, dtype=np.float32)[:, None] * frequency.astype(np.float32)[None, :]
    c = np.cos(angles.astype(np.float64))
    s = np.sin(angles.astype(np.float64))
    table = np.concatenate([c, c, -s, s], axis=1).astype(np.float32)
    high = table.astype(BF16)
    low_part = (table - high.astype(np.float32)).astype(BF16)
    return high, low_part


def fused_call(tok, cot, lens, norm_vectors, channel_vectors, fi, fo, mi, mo):
    high, low_part = rotation_tables()
    vm = pl.BlockSpec(memory_space=pltpu.VMEM)
    hbm = pl.BlockSpec(memory_space=pl.ANY)

    def v(shape, dtype):
        return pltpu.VMEM(shape, dtype)

    t16 = (4 * ROWS, D)
    h16 = (4 * ROWS, 512)
    c16 = (4 * ROWS, 128)
    shapes = ((2, SHARD, 2048), (2, SHARD, 2048), (5, SHARD, 512), (2, SHARD, 512))
    scratch = [v(k, F32) for k in shapes] + [v(k, BF16) for k in shapes]
    scratch += [v(group_shape(g, D), BF16) for g in range(6)]
    scratch += [v(t16, BF16)] * 6
    scratch += [v(h16, F32)] * 2 + [v(h16, BF16)] * 3
    scratch += [v(c16, BF16)] * 4 + [v((4 * ROWS, 384), BF16), v((4 * ROWS, ROWS), F32)]
    scratch += [v(c16, F32)] * 5 + [v(c16, BF16), v((4 * ROWS, 256), BF16)]
    scratch += [v(c16, F32)] * 4 + [v((4, 8, ROWS), F32)]
    scratch += [v((5, 2, QUAD, D), F32), v((5, 2, QUAD, 128), F32), v((2, QUAD, D), F32)]
    scratch += [v((2, 4, QUAD, D), BF16)] + [v((2, QUAD, D), BF16)] + [v((2, OCT, D), BF16)] * 2
    scratch += [v((2, QUAD, D), BF16)] * 4 + [v((2, 2, ROWS, D), BF16)]
    scratch += [v((4,) + group_shape(g, ROWS), BF16) for g in range(6)]
    scratch += [v((3,) + group_shape(g, ROWS), BF16) for g in range(6)]
    scratch += [v(group_shape(g, ROWS), BF16) for g in range(6)]
    scratch += [v((2, 4, 8, 128), F32), v((4, 8, 128), F32)]
    scratch += [v((16, D), F32)] * 4 + [v((4, 16, D), F32), v((8, 128), F32), v((2, 2, QUAD, D), BF16)]
    scratch += [v((2, QUAD, D), BF16)]
    dma = pltpu.SemaphoreType.DMA
    sems = [(3, 11), (3, 11), (2, 10), (2, 10), (6, 4, 2), (6, 4, 2), (6, 4), (6, 4), (6, 4), (6, 4)]
    sems += [(6, 4, 2), (6, 4, 2), (3,), (3,), (3, 3), (3, 3), (6,), (6,), (3,), (3,), (2, 2, 2), (2, 2, 2), (2,), (2,), (6, 2)]
    scratch += [dma(k) for k in sems]
    out_shape = (
        jax.ShapeDtypeStruct((ROWS, D), BF16),
        jax.ShapeDtypeStruct((ROWS, D), BF16),
        jax.ShapeDtypeStruct((2, SHARD, 2048), BF16),
        jax.ShapeDtypeStruct((2, SHARD, 2048), BF16),
        jax.ShapeDtypeStruct((5, SHARD, 512), BF16),
        jax.ShapeDtypeStruct((2, SHARD, 512), BF16),
        jax.ShapeDtypeStruct((16, D), F32),
        jax.ShapeDtypeStruct((8, 512), F32),
    )
    return pl.pallas_call(
        fused_kernel,
        out_shape=out_shape,
        in_specs=[hbm, hbm] + [vm] * 5 + [hbm] * 4,
        out_specs=(hbm,) * 6 + (vm, vm),
        scratch_shapes=scratch,
        compiler_params=pltpu.CompilerParams(
            collective_id=0, has_side_effects=True, vmem_limit_bytes=63 * 2**20
        ),
    )(tok, cot, lens, jnp.asarray(high), jnp.asarray(low_part), norm_vectors, channel_vectors, fi, fo, mi, mo)


def update_kernel(*refs):
    to, tg, gfi, gfo, gmi, gmo, ng, cg = refs[:8]
    state = [refs[8 + 3 * k : 11 + 3 * k] for k in range(6)]
    out = refs[26:]
    out[0][...] = to[...].astype(F32)
    out[1][...] = tg[...].astype(F32)
    rates = (D**-0.5, FF**-0.5, D**-0.5, None, 0.3, 0.3)

    def step(k, at, gradient, rate):
        weight, mean, square = (r[at] for r in state[k])
        return adamw_step(weight, mean, square, gradient.astype(F32), rate)

    for k, g in ((0, gfi), (1, gfo)):
        for layer in range(2):
            new = step(k, layer, g[layer], rates[k])
            for i in range(3):
                out[2 + 3 * k + i][layer] = new[i]
    for layer in range(5):
        a, b, c = step(2, layer, gmi[layer], rates[2])
        out[8][layer] = a
        out[9][layer] = b
        if layer < 4:
            out[10][layer] = c
        else:
            out[11][...] = c
    for layer in range(2):
        rate = (max(2 * D // TOK_DEV, 1) ** -0.5, D**-0.5)[layer]
        new = step(3, layer, gmo[layer], rate)
        for i in range(3):
            out[12 + i][layer] = new[i]
    for k, g, n in ((4, ng, 10), (5, cg, 7)):
        new = step(k, slice(0, n), g[0:n, :], rates[k])
        for i in range(3):
            out[3 + 3 * k + i][...] = new[i]


def update_call(grads, *states):
    steps = 4
    r = SHARD // steps

    def stacked(layers, width):
        return pl.BlockSpec((layers, r, width), lambda i: (0, i, 0))

    def fixed(a, b):
        return pl.BlockSpec((a, b), lambda i: (0, 0))

    frames = pl.BlockSpec((ROWS // steps, D), lambda i: (i, 0))
    big = [stacked(2, 2048), stacked(2, 2048), stacked(5, 512), stacked(2, 512)]
    small = [fixed(10, D), fixed(7, 512)]
    in_specs = [frames, frames] + big + [fixed(16, D), fixed(8, 512)]
    out_specs = [frames, frames]
    out_shape = [jax.ShapeDtypeStruct((ROWS, D), F32)] * 2
    flat = list(grads)
    for k, three in enumerate(states):
        spec = (big + small)[k]
        for i, a in enumerate(three):
            flat.append(a)
            in_specs.append(spec)
            if k == 2 and i == 2:
                out_specs += [stacked(4, 512), pl.BlockSpec((r, 512), lambda i: (i, 0))]
                out_shape += [
                    jax.ShapeDtypeStruct((4, SHARD, 512), F32),
                    jax.ShapeDtypeStruct((SHARD, 512), F32),
                ]
            else:
                out_specs.append(spec)
                out_shape.append(jax.ShapeDtypeStruct(a.shape, F32))
    return pl.pallas_call(
        update_kernel,
        grid=(steps,),
        in_specs=in_specs,
        out_specs=out_specs,
        out_shape=out_shape,
        compiler_params=pltpu.CompilerParams(vmem_limit_bytes=63 * 2**20),
    )(*flat)


def fast_body(
    tokens_in, out_cotangent, utt_lengths,
    feed_in, feed_in_mean, feed_in_square,
    feed_out, feed_out_mean, feed_out_square,
    mixer_in, mixer_in_mean, mixer_in_square,
    mixer_out, mixer_out_mean, mixer_out_square,
    norm_vectors, norm_vectors_mean, norm_vectors_square,
    channel_vectors, channel_vectors_mean, channel_vectors_square,
):
    fo_t = jnp.swapaxes(feed_out, 1, 2)
    mo_t = jnp.swapaxes(mixer_out, 1, 2)
    tokens_out, tokens_grad, gfi, gfo, gmi, gmo, ngrad, cgrad = fused_call(
        tokens_in, out_cotangent, utt_lengths, norm_vectors, channel_vectors,
        feed_in, fo_t, mixer_in, mo_t,
    )

    def turned(v):
        return jnp.swapaxes(v, 1, 2)

    new = update_call(
        (tokens_out, tokens_grad, gfi, gfo, gmi, gmo, ngrad, cgrad),
        (feed_in, feed_in_mean, feed_in_square),
        (fo_t, turned(feed_out_mean), turned(feed_out_square)),
        (mixer_in, mixer_in_mean, mixer_in_square),
        (mo_t, turned(mixer_out_mean), turned(mixer_out_square)),
        (norm_vectors, norm_vectors_mean, norm_vectors_square),
        (channel_vectors, channel_vectors_mean, channel_vectors_square),
    )
    new = list(new)
    for k in (5, 6, 7, 12, 13, 14):
        new[k] = turned(new[k])
    return tuple(new)


def solution(mesh):
    fits = mesh.shape["dp"] == 16 and mesh.shape["mp"] == 2
    placed = (
        P("dp", None),
        P("dp", None),
        P("dp", None),
        P(None, "dp", "mp"),
        P(None, "dp", "mp"),
        P(None, "dp", "mp"),
        P(None, "mp", "dp"),
        P(None, "mp", "dp"),
        P(None, "mp", "dp"),
        P(None, "dp", "mp"),
        P(None, "dp", "mp"),
        P(None, "dp", "mp"),
        P(None, "mp", "dp"),
        P(None, "mp", "dp"),
        P(None, "mp", "dp"),
        P(),
        P(),
        P(),
        P(None, "mp"),
        P(None, "mp"),
        P(None, "mp"),
    )
    return jax.shard_map(
        fast_body if fits else body,
        mesh=mesh,
        in_specs=placed,
        out_specs=(
            P("dp", None),
            P("dp", None),
            P(None, "dp", "mp"),
            P(None, "dp", "mp"),
            P(None, "dp", "mp"),
            P(None, "mp", "dp"),
            P(None, "mp", "dp"),
            P(None, "mp", "dp"),
            P(None, "dp", "mp"),
            P(None, "dp", "mp"),
            P(None, "dp", "mp"),
            P("dp", "mp"),
            P(None, "mp", "dp"),
            P(None, "mp", "dp"),
            P(None, "mp", "dp"),
            P(),
            P(),
            P(),
            P(None, "mp"),
            P(None, "mp"),
            P(None, "mp"),
        ),
        check_vma=False,
    )
```
